256 devices in a mesh: gx: 64 (over y, x_hi, z), gz: 4 (over x_lo, core).
Axes of the slice: x: 4 (x_hi: 2, x_lo: 2; x = x_hi * 2 + x_lo), y: 4, z: 8, core: 2. Of those that a mesh axis runs over, the one named last changes fastest.
Arguments:
- solid_state: float32 [9, 20, 65536], P(None, None, ('gx', 'gz')), may hold values from -6 to 6
- jacobians: float32 [3, 9, 9, 65536], P(None, None, None, ('gx', 'gz')), may hold values from -2 to 2
- flux_solvers: float32 [4, 9, 9, 65536], P(None, None, None, ('gx', 'gz')), may hold values from -2 to 2
- stiffness: float32 [3, 20, 20], replicated, may hold values from -1.25 to 1.25
- trace_matrix: float32 [4, 10, 20], replicated, may hold values from -1.25 to 1.25
- lift_matrix: float32 [4, 20, 10], replicated, may hold values from -2 to 2
- neighbours: int32 [4, 65536], P(None, ('gx', 'gz')), may hold values from 0 to 1575, as said below
- send_faces: int32 [4, 32768], P(None, ('gx', 'gz')), may hold values from 0 to 1023, as said below
- surface_map: int32 [3, 5, 2048], P(None, None, ('gx', 'gz')), may hold values from 0 to 16383, as said below
- surface_normals: float32 [3, 5, 2048], P(None, None, ('gx', 'gz')), may hold values from -1 to 1
- air_state: float32 [4, 512, 64, 128], P(None, 'gx', 'gz'), may hold values from -6 to 6
- wind_field: float32 [3, 512, 64, 128], P(None, 'gx', 'gz'), may hold values from -0.3 to 0.3
- air_medium: float32 [2, 512, 64, 128], P(None, 'gx', 'gz'), may hold values from 0.05 to 0.25
Outputs:
- solid_next: float32 [9, 20, 65536], P(None, None, ('gx', 'gz'))
- air_next: float32 [4, 512, 64, 128], P(None, 'gx', 'gz')
The draws below stay inside these ranges and needn't reach their ends.
Inputs may be any that keep to these rules, and one draw needn't show every extreme that they name: `neighbours`: entry [f, e] of a partition names what lies across face f of its tetrahedron e: below 1024 a face slot of the same partition (such slots name each other in pairs), from 1024 the slot 1024 + d * 128 + k of the k-th face shared in direction d, from 1536 the surface slot r * 8 + k. `send_faces`: the entries of a partition are distinct face slots; the face slot in [d, k] has neighbour entry 1024 + d * 128 + k. `surface_map`: row 0 holds distinct face slots, none of them in send_faces, whose neighbour entry is their surface slot; row 1 a cell index below 16384; row 2 is 1 for coupled slots and 0 otherwise. The coupled slots of one r are the lowest k; slots whose target strip lies outside 0 to 63 are uncoupled; the slots with r = 2 are all coupled.
All inputs are finite; a program needn't handle non-finite values.
Results may differ from the reference program's by a relative error of at most 0.0003.
Values sent between devices are 32-bit elements; how exact they have to be, the bound alone decides.
A program may use at most 128 MiB of HBM per device.

```python
import jax
import jax.numpy as jnp
from jax import lax

QUANT = 9
BASIS = 20
FACE_BASIS = 10
ORDERS = 4
RADIUS = 4
SUBSTEPS = 3
REACH = 5
TET_DEV = 256
BF = 128
CAP = 8
CX = 8
CZ = 16
CY = 128
STRIPS = 64
BANDS = 4
TETS = 65536
NX = 512
NZ = 64
DEVICES = 256


def layout(key):
    slots = 4 * TET_DEV

    def single(partition):
        device_key = jax.random.fold_in(key, partition)
        shuffle_key, count_key, cell_key = jax.random.split(device_key, 3)
        shuffled = jax.random.permutation(shuffle_key, slots).astype(jnp.int32)
        top_where = jnp.argmax((shuffled == slots - 1).astype(jnp.int32)).astype(jnp.int32)
        shuffled = shuffled.at[top_where].set(shuffled[0])
        shuffled = shuffled.at[0].set(slots - 1)
        low_where = jnp.argmax((shuffled == 0).astype(jnp.int32)).astype(jnp.int32)
        shuffled = shuffled.at[low_where].set(shuffled[1])
        shuffled = shuffled.at[1].set(0)
        shared_slots = shuffled[:4 * BF]
        surface_slots = shuffled[4 * BF:4 * BF + REACH * CAP]
        remaining = shuffled[4 * BF + REACH * CAP:]
        first_half = remaining[0::2]
        second_half = remaining[1::2]
        partner_slots = jnp.zeros((slots,), jnp.int32)
        partner_slots = partner_slots.at[shared_slots].set(slots + jnp.arange(4 * BF, dtype=jnp.int32))
        partner_slots = partner_slots.at[surface_slots].set(slots + 4 * BF + jnp.arange(REACH * CAP, dtype=jnp.int32))
        partner_slots = partner_slots.at[first_half].set(second_half)
        partner_slots = partner_slots.at[second_half].set(first_half)
        strip_id = partition // BANDS
        limits = jnp.array([CAP // 2 + 1, CAP + 1, CAP + 1, CAP + 1, CAP // 2 + 1], jnp.int32)
        counts = jax.random.randint(count_key, (REACH,), 0, limits).astype(jnp.int32)
        counts = counts.at[REACH // 2].set(CAP)
        targets = strip_id + jnp.arange(REACH, dtype=jnp.int32) - REACH // 2
        inside = (targets >= 0) & (targets < STRIPS)
        coupled = ((jnp.arange(CAP, dtype=jnp.int32)[None, :] < counts[:, None]) & inside[:, None]).astype(jnp.int32)
        target_cells = jax.random.randint(cell_key, (REACH, CAP), 0, CX * CZ * CY).astype(jnp.int32)
        target_cells = target_cells.at[REACH // 2, 0].set(CX * CZ * CY - 1)
        surface_rows = jnp.stack([surface_slots.reshape(REACH, CAP), target_cells, coupled])
        return (partner_slots.reshape(4, TET_DEV), shared_slots.reshape(4, BF), surface_rows)
    partner_all, shared_all, surface_all = jax.vmap(single)(jnp.arange(STRIPS * BANDS, dtype=jnp.int32))
    neighbour_whole = jnp.moveaxis(partner_all, 0, 1).reshape(4, STRIPS * BANDS * TET_DEV)
    shared_whole = jnp.moveaxis(shared_all, 0, 1).reshape(4, STRIPS * BANDS * BF)
    surface_whole = jnp.moveaxis(surface_all, 0, 2).reshape(3, REACH, STRIPS * BANDS * CAP)
    return (neighbour_whole, shared_whole, surface_whole)


def draw_neighbours(key, part):
    pieces = layout(key)
    return pieces[0]


def draw_send_faces(key, part):
    pieces = layout(key)
    return pieces[1]


def draw_surface_map(key, part):
    pieces = layout(key)
    return pieces[2]


def levels(own_key, dims, cuts, low, high):
    def one(dim, parts):
        steps = jax.random.uniform(jax.random.fold_in(jax.random.fold_in(own_key, 6), dim), (parts,), jnp.float32, low / len(cuts), high / len(cuts))
        return jnp.repeat(jnp.exp(steps), dims[dim] // parts).reshape((-1,) + (1,) * (len(dims) - dim - 1))

    loudness = one(*cuts[0])
    for cut in cuts[1:]:
        loudness = loudness * one(*cut)
    return loudness


def normal_values(key, dims, width, most, cuts=(), held_as=jnp.bfloat16):
    result = jax.random.normal(key, dims, jnp.float32) * width
    if len(cuts) > 0:
        result = levels(key, dims, cuts, -0.22, 0.18) * result
    return jnp.clip(result, min=-most, max=most).astype(held_as)


def setup_inputs(seed: int = 0) -> dict:
    arg_keys = jax.random.split(jax.random.key(seed), 14)
    solid_state = normal_values(arg_keys[0], (QUANT, BASIS, TETS), 1.0, 6.0, ((2, 256),), jnp.float32)
    jacobians = normal_values(arg_keys[1], (3, QUANT, QUANT, TETS), QUANT ** -0.5, 2.0, ((3, 256),), jnp.float32)
    flux_solvers = normal_values(arg_keys[2], (4, QUANT, QUANT, TETS), QUANT ** -0.5, 2.0, ((3, 256),), jnp.float32)
    stiffness = normal_values(arg_keys[3], (3, BASIS, BASIS), BASIS ** -0.5, 1.25, (), jnp.float32)
    trace_matrix = normal_values(arg_keys[4], (4, FACE_BASIS, BASIS), BASIS ** -0.5, 1.25, (), jnp.float32)
    lift_matrix = normal_values(arg_keys[5], (4, BASIS, FACE_BASIS), FACE_BASIS ** -0.5, 2.0, (), jnp.float32)
    neighbours = draw_neighbours(jax.random.fold_in(arg_keys[13], 71), 0)
    send_faces = draw_send_faces(jax.random.fold_in(arg_keys[13], 71), 0)
    surface_map = draw_surface_map(jax.random.fold_in(arg_keys[13], 71), 0)
    surface_normals = jnp.clip(jax.random.uniform(arg_keys[9], (3, REACH, CAP * DEVICES), jnp.float32, -1.0, 1.0) * levels(arg_keys[9], (3, REACH, CAP * DEVICES), ((2, 256),), -0.4, 0.0), -1.0, 1.0)
    air_state = normal_values(arg_keys[10], (4, NX, NZ, CY), 1.0, 6.0, ((1, 64), (2, 4)), jnp.float32)
    wind_field = jnp.clip(jax.random.uniform(arg_keys[11], (3, NX, NZ, CY), jnp.float32, -0.3, 0.3) * levels(arg_keys[11], (3, NX, NZ, CY), ((1, 64), (2, 4)), -0.4, 0.0), -0.3, 0.3)
    air_medium = jnp.clip(0.05 + 0.2 * jax.random.uniform(arg_keys[12], (2, NX, NZ, CY), jnp.float32) ** levels(arg_keys[12], (2, NX, NZ, CY), ((1, 64), (2, 4)), -0.2, 0.2), 0.05, 0.25)
    return {"solid_state": solid_state, "jacobians": jacobians, "flux_solvers": flux_solvers, "stiffness": stiffness, "trace_matrix": trace_matrix, "lift_matrix": lift_matrix, "neighbours": neighbours, "send_faces": send_faces, "surface_map": surface_map, "surface_normals": surface_normals, "air_state": air_state, "wind_field": wind_field, "air_medium": air_medium}


PRECISE = lax.Precision.HIGHEST
TIME_STEP = 0.5
COUPLING_GAIN = 1.0
STENCIL_WEIGHTS = (0.8, -0.2, 4.0 / 105.0, -1.0 / 280.0)


def centered(values, dimension, begin_at, length_out):
    accumulated = jnp.zeros_like(lax.slice_in_dim(values, begin_at, begin_at + length_out, axis=dimension))
    for offset, weight in enumerate(STENCIL_WEIGHTS, 1):
        ahead = lax.slice_in_dim(values, begin_at + offset, begin_at + offset + length_out, axis=dimension)
        behind = lax.slice_in_dim(values, begin_at - offset, begin_at - offset + length_out, axis=dimension)
        accumulated = accumulated + weight * (ahead - behind)
    return accumulated


def derivative(values, margin, rim_out, dimension):
    shift_in = margin - rim_out
    first_len = values.shape[0] - 2 * shift_in
    second_len = values.shape[1] - 2 * shift_in
    if dimension == 0:
        return centered(values[:, shift_in:shift_in + second_len], 0, shift_in, first_len)
    if dimension == 1:
        return centered(values[shift_in:shift_in + first_len], 1, shift_in, second_len)
    cropped = values[shift_in:shift_in + first_len, shift_in:shift_in + second_len]
    padded = jnp.pad(cropped, ((0, 0), (0, 0), (RADIUS, RADIUS)))
    return centered(padded, 2, RADIUS, values.shape[2])


def pressure_update(widened, margin, rim_out, wind_part, bulk_part):
    pressure = widened[0]
    shift_in = margin - rim_out
    first_len = pressure.shape[0] - 2 * shift_in
    second_len = pressure.shape[1] - 2 * shift_in
    divergence = derivative(widened[1], margin, rim_out, 0) + derivative(widened[2], margin, rim_out, 1) + derivative(widened[3], margin, rim_out, 2)
    advection = wind_part[0] * derivative(pressure, margin, rim_out, 0) + wind_part[1] * derivative(pressure, margin, rim_out, 1) + wind_part[2] * derivative(pressure, margin, rim_out, 2)
    return pressure[shift_in:shift_in + first_len, shift_in:shift_in + second_len] - bulk_part * divergence - advection


def velocity_update(widened, margin, new_pressure, pressure_margin, wind_part, buoyancy):
    results = []
    for component in range(3):
        velocity = widened[1 + component]
        interior = velocity[margin:velocity.shape[0] - margin, margin:velocity.shape[1] - margin]
        advection = wind_part[0] * derivative(velocity, margin, 0, 0) + wind_part[1] * derivative(velocity, margin, 0, 1) + wind_part[2] * derivative(velocity, margin, 0, 2)
        results.append(interior - buoyancy * derivative(new_pressure, pressure_margin, 0, component) - advection)
    return jnp.stack(results)


def predict(state, jacobians, stiffness):
    current = state
    integral = TIME_STEP * state
    weight_now = TIME_STEP
    for degree in range(1, ORDERS):
        rotated = jnp.einsum("dbc,qce->dqbe", stiffness, current, precision=PRECISE)
        current = -jnp.einsum("dpqe,dqbe->pbe", jacobians, rotated, precision=PRECISE)
        weight_now = weight_now * TIME_STEP / (degree + 1)
        integral = integral + weight_now * current
    return integral


def correct(state, integral, jacobians, flux_solvers, stiffness, lift_matrix, own_traces, outer_traces):
    rotated = jnp.einsum("dcb,qce->dqbe", stiffness, integral, precision=PRECISE)
    volume_term = jnp.einsum("dpqe,dqbe->pbe", jacobians, rotated, precision=PRECISE)
    fluxed = jnp.einsum("fpqe,qjfe->pjfe", flux_solvers, outer_traces - own_traces, precision=PRECISE)
    surface_term = jnp.einsum("fbj,pjfe->pbe", lift_matrix, fluxed, precision=PRECISE)
    return state + volume_term + surface_term


def from_lower(values, dimension):
    empty_rim = jnp.zeros_like(lax.slice_in_dim(values, 0, 1, axis=dimension))
    return jnp.concatenate([empty_rim, lax.slice_in_dim(values, 0, values.shape[dimension] - 1, axis=dimension)], axis=dimension)


def from_upper(values, dimension):
    empty_rim = jnp.zeros_like(lax.slice_in_dim(values, 0, 1, axis=dimension))
    return jnp.concatenate([lax.slice_in_dim(values, 1, values.shape[dimension], axis=dimension), empty_rim], axis=dimension)


def reference(solid_state, jacobians, flux_solvers, stiffness, trace_matrix, lift_matrix, neighbours, send_faces, surface_map, surface_normals, air_state, wind_field, air_medium):
    partitions = STRIPS * BANDS

    def by_partition(values):
        values = values.reshape(values.shape[:-1] + (partitions, values.shape[-1] // partitions))
        return jnp.moveaxis(values, -2, 0)

    state_parts = by_partition(solid_state)
    jacobian_parts = by_partition(jacobians)
    solver_parts = by_partition(flux_solvers)
    neighbour_parts = by_partition(neighbours)
    send_parts = by_partition(send_faces)
    surface_parts = by_partition(surface_map)
    normal_parts = by_partition(surface_normals)

    def predict_part(packed):
        state_one, jacobian_one = packed
        integral = predict(state_one, jacobian_one, stiffness)
        own_traces = jnp.einsum("fjb,qbe->qjfe", trace_matrix, integral, precision=PRECISE)
        return integral, own_traces.reshape(QUANT, FACE_BASIS, 4 * TET_DEV)

    integral_parts, trace_parts = lax.map(predict_part, (state_parts, jacobian_parts))

    def pick_outgoing(traces_one, sends_one):
        return jnp.take(traces_one, sends_one.reshape(-1), axis=2).reshape(QUANT, FACE_BASIS, 4, BF)

    outgoing = jax.vmap(pick_outgoing)(trace_parts, send_parts)
    partition_grid = outgoing.reshape(STRIPS, BANDS, QUANT, FACE_BASIS, 4, BF)
    received = jnp.stack([
        from_lower(partition_grid[:, :, :, :, 1], 0),
        from_upper(partition_grid[:, :, :, :, 0], 0),
        from_lower(partition_grid[:, :, :, :, 3], 1),
        from_upper(partition_grid[:, :, :, :, 2], 1)], axis=4).reshape(partitions, QUANT, FACE_BASIS, 4 * BF)

    face_slots = surface_parts[:, 0]
    target_cells = surface_parts[:, 1]
    coupled = surface_parts[:, 2].astype(jnp.float32)
    mean_speed = jnp.mean(trace_parts[:, 6:9], axis=2)

    def pick_speed(speed_one, slots_one):
        return jnp.take(speed_one, slots_one.reshape(-1), axis=1).reshape(3, REACH, CAP)

    at_faces = jax.vmap(pick_speed)(mean_speed, face_slots)
    normal_speed = coupled * jnp.sum(normal_parts * at_faces, axis=1)

    part_ids = jnp.arange(partitions, dtype=jnp.int32)
    strip_ids = part_ids // BANDS
    band_ids = part_ids % BANDS
    targets = jnp.clip(strip_ids[:, None] + jnp.arange(REACH, dtype=jnp.int32)[None, :] - 2, 0, STRIPS - 1)
    first_idx = targets[:, :, None] * CX + target_cells // (CZ * CY)
    vertical_idx = band_ids[:, None, None] * CZ + (target_cells // CY) % CZ
    third_idx = target_cells % CY
    flat_index = ((first_idx * NZ + vertical_idx) * CY + third_idx).astype(jnp.int32)
    pressure_flat = air_state[0].reshape(-1)
    replies = coupled * pressure_flat[flat_index]
    injected = pressure_flat.at[flat_index.reshape(-1)].add(COUPLING_GAIN * normal_speed.reshape(-1))

    air_now = jnp.concatenate([injected.reshape((1,) + air_state.shape[1:]), air_state[1:]], axis=0)
    for substep in range(SUBSTEPS):
        padded = jnp.pad(air_now, ((0, 0), (RADIUS, RADIUS), (RADIUS, RADIUS), (0, 0)))
        new_pressure = pressure_update(padded, RADIUS, 0, wind_field, air_medium[0])
        padded_pressure = jnp.pad(new_pressure, ((RADIUS, RADIUS), (RADIUS, RADIUS), (0, 0)))
        velocities = velocity_update(padded, RADIUS, padded_pressure, RADIUS, wind_field, air_medium[1])
        air_now = jnp.concatenate([new_pressure[None], velocities], axis=0)

    def correct_part(packed):
        state_one, integral_one, jacobian_one, solver_one, traces_one, received_one, slots_one, replies_one, neighbour_one = packed
        own_at = jnp.take(traces_one, slots_one.reshape(-1), axis=2)
        mirrored = jnp.concatenate([-2.0 * replies_one.reshape(-1) - own_at[0:3], own_at[3:]], axis=0)
        extended = jnp.concatenate([traces_one, received_one, mirrored], axis=2)
        outer_traces = jnp.take(extended, neighbour_one.reshape(-1), axis=2).reshape(QUANT, FACE_BASIS, 4, TET_DEV)
        return correct(state_one, integral_one, jacobian_one, solver_one, stiffness, lift_matrix, traces_one.reshape(QUANT, FACE_BASIS, 4, TET_DEV), outer_traces)

    next_parts = lax.map(correct_part, (state_parts, integral_parts, jacobian_parts, solver_parts, trace_parts, received, face_slots, replies, neighbour_parts))
    solid_next = jnp.moveaxis(next_parts, 0, 2).reshape(QUANT, BASIS, TETS)
    return solid_next, air_now
```

```python
import jax
import jax.numpy as jnp
from jax import lax
from jax.experimental import pallas as pl
from jax.experimental.pallas import tpu as pltpu
from jax.sharding import PartitionSpec as P

F32, BF16 = jnp.float32, jnp.bfloat16
MESH = pl.DeviceIdType.MESH

ORDERS = 4
TIME_STEP = 0.5
SUBSTEPS = 3
TAPS = (672.0, -168.0, 32.0, -3.0)
TAP_UNIT = 1.0 / 840.0

NQ, NB, NBP = 9, 20, 24
NJ, NJP = 10, 16
NT = 256
SLOTS = 4 * NT
RIM = 128
CAP, REACH = 8, 5
LEFT, RIGHT, BELOW, ABOVE = range(4)


def halves(x):
    high = x.astype(BF16)
    return high, (x - high.astype(F32)).astype(BF16)


def thirds(x):
    high = x.astype(BF16)
    rest = x - high.astype(F32)
    mid = rest.astype(BF16)
    return high, mid, (rest - mid.astype(F32)).astype(BF16)


def dot(a, b):
    return jnp.dot(a, b, preferred_element_type=F32)


def dot_nt(a, b):
    return lax.dot_general(a, b, (((1,), (1,)), ((), ())), preferred_element_type=F32)


def iota(shape, dim):
    return lax.broadcasted_iota(jnp.int32, shape, dim)


def stacked_left(padded, gap):
    high = padded.astype(BF16).astype(F32)
    low = padded - high
    return high + pltpu.roll(high, gap, 1) + pltpu.roll(low, 2 * gap, 1)


def lane_row(tile):
    total = tile[0:1]
    for r in range(1, REACH):
        total = total + pltpu.roll(tile, CAP * r, 1)[r : r + 1]
    return total


def kernel(strips, bands, *refs):
    (
        sol_h, jac_h, flx_h, stiff_ref, trace_ref, lift_ref, nbr_ref, surf_ref, normal_ref,
        air_h, wind_h, med_h,
        sol_out, air_out,
        sol, jac, flx, e0, e1, e2, e3, wind, med,
        ds, rot, integ, own, ohl, nmat, diff, vol, sout, uout,
        ksc, lsc, tsc, kp, kv, ts, ls, wy, smt, nmt,
        base, adv, a1, bt,
        ctile, stile, ptile, crecv, srecv, precv, tout, trecv, rl,
        local_sem, send_sem, recv_sem,
    ) = refs
    ext = (e0, e1, e2, e3)
    a = lax.axis_index("gx")
    b = lax.axis_index("gz")

    own_x, own_z = pl.ds(4, 8), pl.ds(8, 16)
    local = {}

    def fetch(name, src, dst):
        local[name] = pltpu.make_async_copy(src, dst, local_sem.at[len(local)])
        local[name].start()

    fetch("sol", sol_h, sol)
    fetch("jac", jac_h, jac)
    fetch("air", air_h, e0.at[:, own_x, own_z, :])
    fetch("wind", wind_h, wind)
    fetch("med", med_h, med)
    fetch("flx", flx_h, flx)

    can = {LEFT: a > 0, RIGHT: a < strips - 1, BELOW: b > 0, ABOVE: b < bands - 1}
    peer = {
        LEFT: (jnp.maximum(a - 1, 0), b),
        RIGHT: (jnp.minimum(a + 1, strips - 1), b),
        BELOW: (a, jnp.maximum(b - 1, 0)),
        ABOVE: (a, jnp.minimum(b + 1, bands - 1)),
    }
    mirror_of = {LEFT: RIGHT, RIGHT: LEFT, BELOW: ABOVE, ABOVE: BELOW}
    sem_count = [0]
    pending = []

    def next_sem():
        sem_count[0] += 1
        return sem_count[0] - 1

    def remote(src, dst, device, sem):
        return pltpu.make_async_remote_copy(
            src_ref=src, dst_ref=dst, send_sem=send_sem.at[sem], recv_sem=recv_sem.at[sem],
            device_id=device, device_id_type=MESH,
        )

    def exchange(make):
        sems = {d: next_sem() for d in range(4)}
        copies = {d: remote(*make(d), peer[d], sems[d]) for d in range(4)}
        for d in range(4):
            pl.when(can[d])(copies[d].start)
            pending.append((can[d], copies[d]))

        def arrive():
            for d in range(4):
                pl.when(can[d])(copies[mirror_of[d]].wait_recv)

        return arrive

    def surface(src, buffer, sign):
        waits = []
        for r in range(REACH):
            if r == 2:
                continue
            to = a + sign * (r - 2)
            source = a - sign * (r - 2)
            to_ok = (to >= 0) & (to < strips)
            from_ok = (source >= 0) & (source < strips)
            copy = remote(src, buffer.at[r], (jnp.clip(to, 0, strips - 1), b), next_sem())
            pl.when(to_ok)(copy.start)
            pending.append((to_ok, copy))
            waits.append((from_ok, copy))

        def arrive():
            for from_ok, copy in waits:
                pl.when(from_ok)(copy.wait_recv)

        return arrive

    x_send = {LEFT: pl.ds(4, 4), RIGHT: pl.ds(8, 4)}
    x_land = {LEFT: pl.ds(12, 4), RIGHT: pl.ds(0, 4)}
    z_send = {BELOW: pl.ds(8, 8), ABOVE: pl.ds(16, 8)}
    z_land = {BELOW: pl.ds(24, 8), ABOVE: pl.ds(0, 8)}

    def halo(buffer, fields):
        def make(d):
            if d in (LEFT, RIGHT):
                return buffer.at[fields, x_send[d], own_z, :], buffer.at[fields, x_land[d], own_z, :]
            return buffer.at[fields, own_x, z_send[d], :], buffer.at[fields, own_x, z_land[d], :]

        return make

    speeds_of, pressure_of = pl.ds(1, 3), pl.ds(0, 1)

    def halo_first(d):
        x_from = {LEFT: pl.ds(0, 4), RIGHT: pl.ds(4, 4)}
        z_from = {BELOW: pl.ds(0, 8), ABOVE: pl.ds(8, 8)}
        if d in (LEFT, RIGHT):
            return air_h.at[speeds_of, x_from[d]], e0.at[speeds_of, x_land[d], own_z, :]
        return air_h.at[speeds_of, :, z_from[d], :], e0.at[speeds_of, own_x, z_land[d], :]

    for d, where in ((LEFT, pl.ds(0, 4)), (RIGHT, pl.ds(12, 4))):
        @pl.when(jnp.logical_not(can[d]))
        def _(where=where):
            for buffer in (e0, e1, e2):
                buffer[:, where, own_z, :] = jnp.zeros((4, 4, 16, 128), F32)
            e3[pressure_of, where, own_z, :] = jnp.zeros((1, 4, 16, 128), F32)
    for d, where in ((BELOW, pl.ds(0, 8)), (ABOVE, pl.ds(24, 8))):
        @pl.when(jnp.logical_not(can[d]))
        def _(where=where):
            for buffer in (e0, e1, e2):
                buffer[:, own_x, where, :] = jnp.zeros((4, 8, 8, 128), F32)
            e3[pressure_of, own_x, where, :] = jnp.zeros((1, 8, 8, 128), F32)
    crecv[...] = jnp.zeros_like(crecv)
    srecv[...] = jnp.zeros_like(srecv)
    precv[...] = jnp.zeros_like(precv)
    trecv[...] = jnp.zeros_like(trecv)

    barrier = pltpu.get_barrier_semaphore()
    for off in (-2, -1, 1, 2):
        pl.semaphore_signal(
            barrier, inc=1, device_id=(lax.rem(a + off + strips, strips), b), device_id_type=MESH
        )
    for off in (-1, 1):
        pl.semaphore_signal(
            barrier, inc=1, device_id=(a, lax.rem(b + off + bands, bands)), device_id_type=MESH
        )

    smt[...] = jnp.zeros_like(smt)
    nmt[...] = jnp.zeros_like(nmt)
    for i in range(3):
        smt[i, 0:REACH, 0:CAP] = surf_ref[i].astype(F32)
        nmt[i, 0:REACH, 0:CAP] = normal_ref[i]
    own_cells = lane_row(smt[1])
    coupled = lane_row(smt[2])
    normals = [lane_row(nmt[c]) for c in range(3)]
    ctile[...] = jnp.broadcast_to(own_cells, (8, 128))

    ksc[...] = jnp.zeros_like(ksc)
    tsc[...] = jnp.zeros_like(tsc)
    lsc[...] = jnp.zeros_like(lsc)
    for d in range(3):
        ksc[d * NBP : d * NBP + NB, 0:NB] = stiff_ref[d]
    for f in range(4):
        rows = trace_ref[f]
        tsc[f * NJP : f * NJP + NJ, 0:NB] = rows
        tsc[f * NJP + NJ : f * NJP + NJ + 1, 0:NB] = jnp.sum(rows, axis=0, keepdims=True) * (1.0 / NJ)
        lsc[f, 0:NB, 0:NJ] = lift_ref[f]
    stiff = ksc[...]
    kp[...] = (-stacked_left(stiff[0:80], 32)).astype(BF16)
    flipped = jnp.transpose(stiff)[0:NBP]
    lanes = iota((NBP, 128), 1)
    turned = [jnp.where(lanes < NBP, flipped if d == 0 else pltpu.roll(flipped, 128 - d * NBP, 1), 0.0) for d in range(3)]
    turned.append(jnp.zeros((8, 128), F32))
    kv[...] = stacked_left(jnp.concatenate(turned, axis=0), 32).astype(BF16)
    ts[...] = stacked_left(tsc[...], 32).astype(BF16)
    lift = lsc[0]
    for f in range(1, 4):
        lift = lift + pltpu.roll(lsc[f], f * NJP, 1)
    lift_high = lift.astype(BF16).astype(F32)
    ls[:, 0:128] = (lift_high + pltpu.roll(lift_high, 64, 1)).astype(BF16)
    ls[:, 128:256] = (lift - lift_high).astype(BF16)
    shift = lax.rem(iota((256, 128), 0), 128) - iota((256, 128), 1)
    taps = jnp.zeros((256, 128), F32)
    for m, tap in enumerate(TAPS, 1):
        taps = jnp.where(shift == m, tap, jnp.where(shift == -m, -tap, taps))
    wy[...] = taps.astype(BF16)
    ds[:, 96:128, :] = jnp.zeros((NQ, 32, NT), BF16)

    def onehot_rows(start, count):
        names = iota((count, NT), 0) + start
        return [jnp.where(names == nbr_ref[f : f + 1, :], 1.0, 0.0).astype(BF16) for f in range(4)]

    for f, block in enumerate(onehot_rows(1536, 128)):
        nmat[1536:1664, f * NT : (f + 1) * NT] = block

    pl.semaphore_wait(barrier, 6)
    cells_arrive = surface(ctile, crecv, 1)
    first_arrive = exchange(halo_first)

    def put_stack(q, x):
        high, low = halves(jnp.concatenate([x, jnp.zeros((8, NT), F32)], axis=0))
        ds[q, 0:32, :] = high
        ds[q, 32:64, :] = low
        ds[q, 64:96, :] = high

    def rotate(left):
        for q in range(NQ):
            rot[q] = dot(left[...], ds[q])

    def contract(p0):
        total = None
        for q in range(NQ):
            for d in range(3):
                term = jac[d, pl.ds(p0, 3), pl.ds(q, 1), :] * rot[q, d * NBP : (d + 1) * NBP, :][None]
                total = term if total is None else total + term
        return total

    local["sol"].wait()
    integ[...] = jnp.zeros_like(integ)
    for q in range(NQ):
        integ[q, 0:NB, :] = TIME_STEP * sol[q]
    for q in range(NQ):
        put_stack(q, integ[q] * (1.0 / TIME_STEP))
    local["jac"].wait()
    weight = TIME_STEP
    for degree in range(1, ORDERS):
        weight = weight * TIME_STEP / (degree + 1)
        rotate(kp)

        def step(i, carry, weight=weight, last=degree == ORDERS - 1):
            now = contract(3 * i)
            for k in range(3):
                total = integ[3 * i + k] + weight * now[k]
                integ[3 * i + k] = total
                put_stack(3 * i + k, total if last else now[k])
            return carry

        lax.fori_loop(0, 3, step, 0)

    for q in reversed(range(NQ)):
        traces = dot(ts[...], ds[q])
        own[q] = traces
        high, low = halves(traces)
        for f in range(4):
            rows, cols = slice(f * NJP, (f + 1) * NJP), slice(f * NT, (f + 1) * NT)
            ohl[q * NJP : (q + 1) * NJP, cols] = high[rows]
            ohl[(NQ + q) * NJP : (NQ + q + 1) * NJP, cols] = low[rows]
    surf_names = nmat[1536:1664, :]
    at_faces = dot_nt(ohl[96:144, :], surf_names) + dot_nt(ohl[240:288, :], surf_names)
    speed = jnp.zeros((1, 128), F32)
    for c in range(3):
        speed = speed + normals[c] * at_faces[c * NJP + NJ : c * NJP + NJ + 1, :]
    own_speed = coupled * speed
    stile[...] = jnp.broadcast_to(own_speed, (8, 128))
    speeds_arrive = surface(stile, srecv, 1)

    slot_row = iota((1, 128), 1) // CAP

    def combine(mine, buffer, sign):
        total = jnp.where(slot_row == 2, mine, 0.0)
        for r in range(REACH):
            if r != 2:
                source = a - sign * (r - 2)
                ok = (source >= 0) & (source < strips)
                total = jnp.where(slot_row == jnp.where(ok, r, -1), buffer[r, 0:1, :], total)
        return total

    cells_arrive()
    cells = combine(own_cells, crecv, 1).astype(jnp.int32)
    cell_rows = lax.shift_right_logical(cells, 7)
    cell_lanes = lax.bitwise_and(cells, 127)
    a1[...] = jnp.where(iota((128, 128), 0) == cell_rows, 1.0, 0.0)
    bt[...] = jnp.where(iota((128, 128), 0) == cell_lanes, 1.0, 0.0)
    local["air"].wait()
    pressure = e0[0, own_x, own_z, :].reshape(128, 128)
    at_lane = bt[...].astype(BF16)
    picked = dot(jnp.concatenate(thirds(pressure), axis=0), at_lane)
    picked = picked[0:128] + picked[128:256] + picked[256:384]
    looked = jnp.sum(picked * a1[...], axis=0, keepdims=True)
    ptile[...] = jnp.broadcast_to(looked, (8, 128))
    replies_arrive = surface(ptile, precv, -1)

    def along_x(ref, f):
        total = None
        for m, tap in enumerate(TAPS, 1):
            term = tap * (ref[f, 4 + m : 12 + m, 8:24, :] - ref[f, 4 - m : 12 - m, 8:24, :])
            total = term if total is None else total + term
        return total

    def along_z(ref, f):
        total = None
        for m, tap in enumerate(TAPS, 1):
            term = tap * (ref[f, 4:12, 8 + m : 24 + m, :] - ref[f, 4:12, 8 - m : 24 - m, :])
            total = term if total is None else total + term
        return total

    def along_y(ref, f):
        x = ref[f, 4:12, 8:24, :].reshape(128, 128)
        return dot(jnp.concatenate(halves(x), axis=1), wy[...]).reshape(8, 16, 128)

    def store_divergence(ref, into):
        into[...] = ref[0, 4:12, 8:24, :] - med[0] * (along_x(ref, 1) + along_z(ref, 2) + along_y(ref, 3))

    def advected(ref, f):
        return wind[0] * along_x(ref, f) + wind[1] * along_z(ref, f) + wind[2] * along_y(ref, f)

    local["wind"].wait()
    local["med"].wait()
    wind[...] = wind[...] * TAP_UNIT
    med[...] = med[...] * TAP_UNIT

    def names_block(i, carry):
        start = pl.multiple_of(64 * i, 64)
        for f, block in enumerate(onehot_rows(start, 64)):
            nmat[pl.ds(start, 64), f * NT : (f + 1) * NT] = block
        return carry

    first_arrive()
    store_divergence(e0, base)

    speeds_arrive()
    arrived = combine(own_speed, srecv, 1)
    at_row = jnp.concatenate(thirds(a1[...] * arrived), axis=1)
    injected = dot_nt(at_row, jnp.concatenate([at_lane] * 3, axis=1)).reshape(8, 16, 128)
    e0[0, own_x, own_z, :] = e0[0, own_x, own_z, :] + injected
    base[...] = base[...] + injected
    pressure_arrive = exchange(halo(e0, pressure_of))

    lax.fori_loop(0, 24, names_block, 0)
    given = dot_nt(ohl[...], nmat[1024:1664, :])
    given = given[0:144] + given[144:288]
    for d in range(4):
        for q in range(NQ):
            tout[d, q * NJ : (q + 1) * NJ, :] = given[q * NJP : q * NJP + NJ, d * RIM : (d + 1) * RIM]
    traces_arrive = exchange(lambda d: (tout.at[d], trecv.at[mirror_of[d]]))
    own_at = given[:, 512:640]

    def shadow_first():
        for f in range(4):
            cols = slice(f * NT, (f + 1) * NT)
            gathered = dot(ohl[...], nmat[0:SLOTS, cols])
            gathered = gathered[0:144] + gathered[144:288]
            for q in range(NQ):
                rows = slice(f * NJP, (f + 1) * NJP)
                diff[q, rows, :] = gathered[q * NJP : (q + 1) * NJP] - own[q, rows, :]

    def shadow_second():
        rotate(kv)

        def step(i, carry):
            vol[pl.ds(3 * i, 3)] = contract(3 * i)
            return carry

        lax.fori_loop(0, 3, step, 0)

    def shadow_third():
        replies_arrive()
        traces_arrive()
        replies = coupled * combine(looked, precv, -1)
        row_q = iota((NQ * NJP, 128), 0) // NJP
        mirrored = jnp.where(row_q < 3, -2.0 * replies - own_at, own_at)
        for half, values in enumerate(halves(mirrored)):
            rl[half * 144 : half * 144 + 144, 512:640] = values
        for d in range(4):
            for q in range(NQ):
                x = jnp.concatenate([trecv[d, q * NJ : (q + 1) * NJ, :], jnp.zeros((NJP - NJ, RIM), F32)], axis=0)
                for half, values in enumerate(halves(x)):
                    start = half * 144 + q * NJP
                    rl[start : start + NJP, d * RIM : (d + 1) * RIM] = values
        for f in range(4):
            cols = slice(f * NT, (f + 1) * NT)
            gathered = dot(rl[...], nmat[SLOTS:1664, cols])
            gathered = gathered[0:144] + gathered[144:288]
            for q in range(NQ):
                rows = slice(f * NJP, (f + 1) * NJP)
                diff[q, rows, :] = diff[q, rows, :] + gathered[q * NJP : (q + 1) * NJP]

    def shadow_fourth():
        local["flx"].wait()

        def step(i, carry):
            faces = []
            for f in range(4):
                total = None
                for q in range(NQ):
                    term = flx[f, pl.ds(3 * i, 3), pl.ds(q, 1), :] * diff[q, f * NJP : (f + 1) * NJP, :][None]
                    total = term if total is None else total + term
                faces.append(total)
            fluxed = jnp.concatenate(faces, axis=1)
            for k in range(3):
                high, low = halves(fluxed[k])
                lifted = dot(ls[:, 0:192], jnp.concatenate([high, low, high], axis=0))
                p = 3 * i + k
                sout[p] = sol[p] + (vol[p] + lifted[0:NBP])[0:NB]
            return carry

        lax.fori_loop(0, 3, step, 0)

    shadows = {1: shadow_first, 2: shadow_second, 3: shadow_third, 4: shadow_fourth}
    turn = 0
    for substep in range(SUBSTEPS):
        here, there = ext[substep], ext[substep + 1]
        final = substep == SUBSTEPS - 1
        if substep == 0:
            pressure_arrive()
            base[...] = base[...] - advected(here, 0)
        else:
            velocity_arrive()
            base[...] = base[...] - med[0] * (along_x(here, 1) + along_z(here, 2) + along_y(here, 3))
        there[0, own_x, own_z, :] = base[...]
        pressure_arrive = exchange(halo(there, pressure_of))
        for f in range(3):
            adv[f] = here[1 + f, own_x, own_z, :] - advected(here, 1 + f)
        turn += 1
        if turn in shadows:
            shadows[turn]()
        pressure_arrive()
        slopes = (along_x(there, 0), along_z(there, 0), along_y(there, 0))
        if final:
            for f in range(3):
                uout[1 + f] = adv[f] - med[1] * slopes[f]
            uout[0] = there[0, own_x, own_z, :]
        else:
            for f in range(3):
                there[1 + f, own_x, own_z, :] = adv[f] - med[1] * slopes[f]
            velocity_arrive = exchange(halo(there, speeds_of))
            base[...] = there[0, own_x, own_z, :] - (
                wind[0] * slopes[0] + wind[1] * slopes[1] + wind[2] * slopes[2]
            )
            turn += 1
            if turn in shadows:
                shadows[turn]()

    fetch("sol_out", sout, sol_out)
    fetch("air_out", uout, air_out)
    local["sol_out"].wait()
    local["air_out"].wait()
    for ok, copy in pending:
        pl.when(ok)(copy.wait_send)


def vmem(*shape, dtype=F32):
    return pltpu.VMEM(shape, dtype)


def solution(mesh):
    strips, bands = mesh.shape["gx"], mesh.shape["gz"]

    def shards(
        solid_state, jacobians, flux_solvers, stiffness, trace_matrix, lift_matrix,
        neighbours, send_faces, surface_map, surface_normals, air_state, wind_field, air_medium,
    ):
        def body(*refs):
            kernel(strips, bands, *refs)

        hbm = pl.BlockSpec(memory_space=pl.ANY)
        near = pl.BlockSpec(memory_space=pltpu.VMEM)
        return pl.pallas_call(
            body,
            out_shape=(
                jax.ShapeDtypeStruct(solid_state.shape, F32),
                jax.ShapeDtypeStruct(air_state.shape, F32),
            ),
            in_specs=[hbm, hbm, hbm, near, near, near, near, near, near, hbm, hbm, hbm],
            out_specs=(hbm, hbm),
            scratch_shapes=[
                vmem(NQ, NB, NT), vmem(3, NQ, NQ, NT), vmem(4, NQ, NQ, NT),
                vmem(4, 16, 32, 128), vmem(4, 16, 32, 128), vmem(4, 16, 32, 128), vmem(4, 16, 32, 128),
                vmem(3, 8, 16, 128), vmem(2, 8, 16, 128),
                vmem(NQ, 128, NT, dtype=BF16), vmem(NQ, 80, NT), vmem(NQ, NBP, NT), vmem(NQ, 64, NT),
                vmem(288, SLOTS, dtype=BF16), vmem(1664, SLOTS, dtype=BF16), vmem(NQ, 64, NT),
                vmem(NQ, NBP, NT), vmem(NQ, NB, NT), vmem(4, 8, 16, 128),
                vmem(128, 128), vmem(4, 32, 128), vmem(64, 128),
                vmem(80, 128, dtype=BF16), vmem(80, 128, dtype=BF16), vmem(64, 128, dtype=BF16),
                vmem(32, 256, dtype=BF16), vmem(256, 128, dtype=BF16),
                vmem(3, 8, 128), vmem(3, 8, 128),
                vmem(8, 16, 128), vmem(3, 8, 16, 128), vmem(128, 128), vmem(128, 128),
                vmem(8, 128), vmem(8, 128), vmem(8, 128),
                vmem(REACH, 8, 128), vmem(REACH, 8, 128), vmem(REACH, 8, 128),
                vmem(4, 96, RIM), vmem(4, 96, RIM), vmem(288, 640, dtype=BF16),
                pltpu.SemaphoreType.DMA((8,)),
                pltpu.SemaphoreType.DMA((48,)),
                pltpu.SemaphoreType.DMA((48,)),
            ],
            compiler_params=pltpu.CompilerParams(
                collective_id=0, has_side_effects=True, vmem_limit_bytes=56 * 1024 * 1024
            ),
            name="coupled_step",
        )(
            solid_state, jacobians, flux_solvers, stiffness, trace_matrix, lift_matrix,
            neighbours, surface_map, surface_normals, air_state, wind_field, air_medium,
        )

    in_specs = (
        P(None, None, ("gx", "gz")),
        P(None, None, None, ("gx", "gz")),
        P(None, None, None, ("gx", "gz")),
        P(),
        P(),
        P(),
        P(None, ("gx", "gz")),
        P(None, ("gx", "gz")),
        P(None, None, ("gx", "gz")),
        P(None, None, ("gx", "gz")),
        P(None, "gx", "gz", None),
        P(None, "gx", "gz", None),
        P(None, "gx", "gz", None),
    )
    out_specs = (P(None, None, ("gx", "gz")), P(None, "gx", "gz", None))
    return jax.shard_map(shards, mesh=mesh, in_specs=in_specs, out_specs=out_specs, check_vma=False)
```

```python
import jax
import jax.numpy as jnp
from jax import lax
from jax.experimental import pallas as pl
from jax.experimental.pallas import tpu as pltpu
from jax.sharding import PartitionSpec as P

F32, BF16 = jnp.float32, jnp.bfloat16
MESH = pl.DeviceIdType.MESH

ORDERS = 4
TIME_STEP = 0.5
SUBSTEPS = 3
TAPS = (672.0, -168.0, 32.0, -3.0)
TAP_UNIT = 1.0 / 840.0

NQ, NB, NBP = 9, 20, 24
NJ, NJP = 10, 16
NT = 256
SLOTS = 4 * NT
RIM = 128
CAP, REACH = 8, 5
LEFT, RIGHT, BELOW, ABOVE = range(4)


def halves(x):
    high = x.astype(BF16)
    return high, (x - high.astype(F32)).astype(BF16)


def thirds(x):
    high = x.astype(BF16)
    rest = x - high.astype(F32)
    mid = rest.astype(BF16)
    return high, mid, (rest - mid.astype(F32)).astype(BF16)


def dot(a, b):
    return jnp.dot(a, b, preferred_element_type=F32)


def dot_nt(a, b):
    return lax.dot_general(a, b, (((1,), (1,)), ((), ())), preferred_element_type=F32)


def iota(shape, dim):
    return lax.broadcasted_iota(jnp.int32, shape, dim)


def stacked_left(padded, gap):
    high = padded.astype(BF16).astype(F32)
    low = padded - high
    return high + pltpu.roll(high, gap, 1) + pltpu.roll(low, 2 * gap, 1)


def lane_row(tile):
    total = tile[0:1]
    for r in range(1, REACH):
        total = total + pltpu.roll(tile, CAP * r, 1)[r : r + 1]
    return total


def kernel(strips, bands, *refs):
    (
        sol_h, jac_h, flx_h, stiff_h, trace_h, lift_h, nbr_h, surf_h, normal_h,
        air_h, wind_h, med_h,
        sol_out, air_out,
        stiff_ref, trace_ref, lift_ref, nbr_ref, surf_ref, normal_ref,
        sol, jac, flx, e0, e1, e2, coef, pe, lift_of,
        ds, rot, integ, own, ohl, nmat, diff, vol, sout, uout,
        ksc, lsc, tsc, kp, kv, ts, ls, wy, smt, nmt,
        base, adv, start_pressure, gained, bt,
        stile, ptile, srecv, precv, tout, trecv, rl,
        local_sem, send_sem, recv_sem,
    ) = refs
    ext = (e0, e1, e2)
    a = lax.axis_index("gx")
    b = lax.axis_index("gz")

    own_x, own_z = pl.ds(8, 8), pl.ds(16, 16)
    coef_x_own, coef_z_own = pl.ds(4, 8), pl.ds(8, 16)
    local = {}

    def fetch(name, src, dst):
        local[name] = pltpu.make_async_copy(src, dst, local_sem.at[len(local)])
        local[name].start()

    fetch("stiff", stiff_h, stiff_ref)
    fetch("sol", sol_h, sol)
    fetch("jac", jac_h, jac)
    fetch("trace", trace_h, trace_ref)
    fetch("nbr", nbr_h, nbr_ref)
    fetch("surf", surf_h, surf_ref)
    fetch("normal", normal_h, normal_ref)
    fetch("air", air_h, e0.at[:, own_x, own_z, :])
    fetch("wind", wind_h, coef.at[pl.ds(0, 3), coef_x_own, coef_z_own])
    fetch("bulk", med_h.at[0], coef.at[3, coef_x_own, coef_z_own])
    fetch("lift", med_h.at[1], lift_of)
    fetch("flx", flx_h, flx)
    fetch("lifting", lift_h, lift_ref)

    can = {LEFT: a > 0, RIGHT: a < strips - 1, BELOW: b > 0, ABOVE: b < bands - 1}
    peer = {
        LEFT: (jnp.maximum(a - 1, 0), b),
        RIGHT: (jnp.minimum(a + 1, strips - 1), b),
        BELOW: (a, jnp.maximum(b - 1, 0)),
        ABOVE: (a, jnp.minimum(b + 1, bands - 1)),
    }
    mirror_of = {LEFT: RIGHT, RIGHT: LEFT, BELOW: ABOVE, ABOVE: BELOW}
    sem_count = [0]
    pending = []

    def remote(src, dst, device, sem):
        return pltpu.make_async_remote_copy(
            src_ref=src, dst_ref=dst, send_sem=send_sem.at[sem], recv_sem=recv_sem.at[sem],
            device_id=device, device_id_type=MESH,
        )

    def exchange(parts):
        copies = []
        for d, src, dst in parts:
            ok, device = side(d)
            copy = remote(src, dst, device, sem_count[0])
            sem_count[0] += 1
            pl.when(ok)(copy.start)
            pending.append((ok, copy))
            copies.append((d, copy))

        def arrive():
            for d, copy in copies:
                pl.when(side(opposite(d))[0])(copy.wait_recv)

        return arrive

    def opposite(d):
        return tuple(mirror_of[k] for k in d) if isinstance(d, tuple) else mirror_of[d]

    def side(d):
        if isinstance(d, tuple):
            return can[d[0]] & can[d[1]], (peer[d[0]][0], peer[d[1]][1])
        return can[d], peer[d]

    def surface(src, place, sign, reach):
        waits = []
        for off in (3, -3, 2, -2, 1, -1):
            if abs(off) > reach:
                continue
            to = a + sign * off
            source = a - sign * off
            to_ok = (to >= 0) & (to < strips)
            from_ok = (source >= 0) & (source < strips)
            copy = remote(src, place(off), (jnp.clip(to, 0, strips - 1), b), sem_count[0])
            sem_count[0] += 1
            pl.when(to_ok)(copy.start)
            pending.append((to_ok, copy))
            waits.append((from_ok, copy))

        def arrive():
            for from_ok, copy in waits:
                pl.when(from_ok)(copy.wait_recv)

        return arrive

    diagonals = ((LEFT, BELOW), (LEFT, ABOVE), (RIGHT, BELOW), (RIGHT, ABOVE))
    x_near = {LEFT: pl.ds(8, 4), RIGHT: pl.ds(12, 4)}
    x_far = {LEFT: pl.ds(12, 4), RIGHT: pl.ds(8, 4)}
    near_land = {LEFT: pl.ds(16, 4), RIGHT: pl.ds(4, 4)}
    far_land = {LEFT: pl.ds(20, 4), RIGHT: pl.ds(0, 4)}
    all_land = {LEFT: pl.ds(16, 8), RIGHT: pl.ds(0, 8)}
    z_near = {BELOW: pl.ds(16, 8), ABOVE: pl.ds(24, 8)}
    z_land = {BELOW: pl.ds(32, 8), ABOVE: pl.ds(8, 8)}
    raw_x = {LEFT: pl.ds(0, 4), RIGHT: pl.ds(4, 4)}
    raw_z = {BELOW: pl.ds(0, 8), ABOVE: pl.ds(8, 8)}
    coef_x = {LEFT: pl.ds(12, 4), RIGHT: pl.ds(0, 4)}
    coef_z = {BELOW: pl.ds(24, 8), ABOVE: pl.ds(0, 8)}
    with_arms = pl.ds(4, 16)

    def send_speeds(buffer, raw=None):
        parts = []
        for d in (LEFT, RIGHT):
            if raw is None:
                parts.append((d, buffer.at[1, own_x, own_z], buffer.at[1, all_land[d], own_z]))
                parts.append((d, buffer.at[pl.ds(2, 2), x_near[d], own_z], buffer.at[pl.ds(2, 2), near_land[d], own_z]))
            else:
                parts.append((d, raw.at[1], buffer.at[1, all_land[d], own_z]))
                parts.append((d, raw.at[pl.ds(2, 2), raw_x[d]], buffer.at[pl.ds(2, 2), near_land[d], own_z]))
        for d in diagonals:
            src = buffer.at[pl.ds(1, 2), x_near[d[0]], z_near[d[1]]]
            if raw is not None:
                src = raw.at[pl.ds(1, 2), raw_x[d[0]], raw_z[d[1]]]
            parts.append((d, src, buffer.at[pl.ds(1, 2), near_land[d[0]], z_land[d[1]]]))
        for d in (BELOW, ABOVE):
            src = buffer.at[pl.ds(1, 3), own_x, z_near[d]]
            if raw is not None:
                src = raw.at[pl.ds(1, 3), :, raw_z[d]]
            parts.append((d, src, buffer.at[pl.ds(1, 3), own_x, z_land[d]]))
        return exchange(parts)

    def send_pressure_z(buffer):
        return [(d, buffer.at[0, with_arms, z_near[d]], buffer.at[0, with_arms, z_land[d]]) for d in (BELOW, ABOVE)]

    def send_pressure(buffer):
        parts = [(d, buffer.at[0, x_far[d], own_z], buffer.at[0, far_land[d], own_z]) for d in (LEFT, RIGHT)]
        return exchange(parts + send_pressure_z(buffer))

    def send_first():
        first = exchange([(d, air_h.at[0], e0.at[0, all_land[d], own_z]) for d in (LEFT, RIGHT)])
        second = send_speeds(e0, air_h)
        parts = []
        for d in (LEFT, RIGHT):
            parts.append((d, wind_h.at[:, raw_x[d]], coef.at[pl.ds(0, 3), coef_x[d], coef_z_own]))
            parts.append((d, med_h.at[0, raw_x[d]], coef.at[3, coef_x[d], coef_z_own]))
        for d in (BELOW, ABOVE):
            parts.append((d, wind_h.at[:, :, raw_z[d]], coef.at[pl.ds(0, 3), coef_x_own, coef_z[d]]))
            parts.append((d, med_h.at[0, :, raw_z[d]], coef.at[3, coef_x_own, coef_z[d]]))
        third = exchange(parts)

        def arrive():
            second()
            third()

        return first, arrive

    for d, where, narrow in ((LEFT, pl.ds(0, 8), pl.ds(0, 4)), (RIGHT, pl.ds(16, 8), pl.ds(12, 4))):
        @pl.when(jnp.logical_not(can[d]))
        def _(where=where, narrow=narrow):
            for buffer in ext:
                buffer[:, where, 8:40, :] = jnp.zeros((4, 8, 32, 128), F32)
            coef[:, narrow, 8:24, :] = jnp.zeros((4, 4, 16, 128), F32)
    for d, where, narrow in ((BELOW, pl.ds(8, 8), pl.ds(0, 8)), (ABOVE, pl.ds(32, 8), pl.ds(24, 8))):
        @pl.when(jnp.logical_not(can[d]))
        def _(where=where, narrow=narrow):
            for buffer in ext:
                buffer[:, 4:20, where, :] = jnp.zeros((4, 16, 8, 128), F32)
            coef[:, 4:12, narrow, :] = jnp.zeros((4, 8, 8, 128), F32)
    srecv[...] = jnp.zeros_like(srecv)
    precv[...] = jnp.zeros_like(precv)
    trecv[...] = jnp.zeros_like(trecv)

    barrier = pltpu.get_barrier_semaphore()
    greet = [(off, 0) for off in (-3, -2, -1, 1, 2, 3)] + [(x, z) for x in (-1, 0, 1) for z in (-1, 1)]
    for x, z in greet:
        pl.semaphore_signal(
            barrier, inc=1, device_id=(lax.rem(a + x + strips, strips), lax.rem(b + z + bands, bands)),
            device_id_type=MESH,
        )

    def put_stack(q, x):
        high, low = halves(jnp.concatenate([x, jnp.zeros((8, NT), F32)], axis=0))
        ds[q, 0:32, :] = high
        ds[q, 32:64, :] = low
        ds[q, 64:96, :] = high

    def rotate(left):
        for q in range(NQ):
            rot[q] = dot(left[...], ds[q])

    def contract(p0):
        total = None
        for q in range(NQ):
            for d in range(3):
                term = jac[pl.ds(p0, 3), q, d : d + 1, :] * rot[q, d * NBP : (d + 1) * NBP, :][None]
                total = term if total is None else total + term
        return total

    ksc[...] = jnp.zeros_like(ksc)
    tsc[...] = jnp.zeros_like(tsc)
    lsc[...] = jnp.zeros_like(lsc)
    smt[...] = jnp.zeros_like(smt)
    nmt[...] = jnp.zeros_like(nmt)
    integ[...] = jnp.zeros_like(integ)
    ds[:, 96:128, :] = jnp.zeros((NQ, 32, NT), BF16)
    local["stiff"].wait()
    for d in range(3):
        ksc[d * NBP : d * NBP + NB, 0:NB] = stiff_ref[d]
    kp[...] = (-stacked_left(ksc[0:80], 32)).astype(BF16)
    local["sol"].wait()
    for q in range(NQ):
        integ[q, 0:NB, :] = TIME_STEP * sol[q]
    for q in range(NQ):
        put_stack(q, integ[q] * (1.0 / TIME_STEP))
    local["jac"].wait()
    weight = TIME_STEP
    for degree in range(1, ORDERS):
        weight = weight * TIME_STEP / (degree + 1)
        rotate(kp)

        def step(i, carry, weight=weight, last=degree == ORDERS - 1):
            now = contract(3 * i)
            for k in range(3):
                total = integ[3 * i + k] + weight * now[k]
                integ[3 * i + k] = total
                put_stack(3 * i + k, total if last else now[k])
            return carry

        lax.fori_loop(0, 3, step, 0)

    local["trace"].wait()
    for f in range(4):
        rows = trace_ref[:, f, :]
        tsc[f * NJP : f * NJP + NJ, 0:NB] = rows
        tsc[f * NJP + NJ : f * NJP + NJ + 1, 0:NB] = jnp.sum(rows, axis=0, keepdims=True) * (1.0 / NJ)
    ts[...] = stacked_left(tsc[...], 32).astype(BF16)

    def names(start, count):
        these = iota((count, NT), 0) + start
        return [jnp.where(these == nbr_ref[f : f + 1, :], 1.0, 0.0).astype(BF16) for f in range(4)]

    local["nbr"].wait()
    for f, block in enumerate(names(1536, 128)):
        nmat[1536:1664, f * NT : (f + 1) * NT] = block
    local["surf"].wait()
    local["normal"].wait()
    for i in range(3):
        smt[i, 0:REACH, 0:CAP] = surf_ref[:, i, :].astype(F32)
        nmt[i, 0:REACH, 0:CAP] = normal_ref[:, i, :]
    own_cells = lane_row(smt[1])
    coupled = lane_row(smt[2])
    normals = [lane_row(nmt[c]) for c in range(3)]

    for q in reversed(range(NQ)):
        traces = dot(ts[...], ds[q])
        own[q] = traces
        high, low = halves(traces)
        for f in range(4):
            rows, cols = slice(f * NJP, (f + 1) * NJP), slice(f * NT, (f + 1) * NT)
            ohl[q * NJP : (q + 1) * NJP, cols] = high[rows]
            ohl[(NQ + q) * NJP : (NQ + q + 1) * NJP, cols] = low[rows]
    surf_names = nmat[1536:1664, :]
    at_faces = dot_nt(ohl[96:144, :], surf_names) + dot_nt(ohl[240:288, :], surf_names)
    speed = jnp.zeros((1, 128), F32)
    for c in range(3):
        speed = speed + normals[c] * at_faces[c * NJP + NJ : c * NJP + NJ + 1, :]
    own_speed = coupled * speed
    stile[...] = jnp.where(iota((8, 128), 0) == 0, own_speed, own_cells)

    pl.semaphore_wait(barrier, len(greet))
    speeds_arrive = surface(stile, lambda off: srecv.at[3 - off], 1, 3)
    pressure_first, first_arrive = send_first()

    local["lifting"].wait()
    for f in range(4):
        lsc[f * NJP : f * NJP + NJ, 0:NB] = lift_ref[:, f, :]
    flipped = jnp.transpose(ksc[...])[0:NBP]
    lanes = iota((NBP, 128), 1)
    turned = [jnp.where(lanes < NBP, flipped if d == 0 else pltpu.roll(flipped, 128 - d * NBP, 1), 0.0) for d in range(3)]
    turned.append(jnp.zeros((8, 128), F32))
    kv[...] = stacked_left(jnp.concatenate(turned, axis=0), 32).astype(BF16)
    lift = jnp.transpose(lsc[...])[0:32]
    lift_high = lift.astype(BF16).astype(F32)
    ls[:, 0:128] = (lift_high + pltpu.roll(lift_high, 64, 1)).astype(BF16)
    ls[:, 128:256] = (lift - lift_high).astype(BF16)
    shift = lax.rem(iota((256, 128), 0), 128) - iota((256, 128), 1)
    taps = jnp.zeros((256, 128), F32)
    for m, tap in enumerate(TAPS, 1):
        taps = jnp.where(shift == m, tap, jnp.where(shift == -m, -tap, taps))
    wy[...] = taps.astype(BF16)

    slot_row = iota((1, 128), 1) // CAP

    def combine(block, mine, buffer, row):
        total = jnp.zeros((1, 128), F32)
        for r in range(REACH):
            gap = block - (r - 2)
            if gap == 0:
                total = jnp.where(slot_row == r, mine, total)
            else:
                ok = (a + gap >= 0) & (a + gap < strips)
                total = jnp.where(slot_row == jnp.where(ok, r, -1), buffer[gap + 3, row : row + 1, :], total)
        return total

    pieces = (((8, 8), (8, 32), (4, 8), (0, 32)), ((4, 4), (16, 16), (0, 4), (8, 16)), ((16, 4), (16, 16), (12, 4), (8, 16)))
    middle = ((8, 8), (16, 16), (4, 8), (8, 16))

    def view(ref, f, box, dx=0, dz=0):
        (x, nx), (z, nz) = box[:2]
        return ref[f, x + dx : x + dx + nx, z + dz : z + dz + nz, :]

    def tap_sum(pick):
        total = None
        for m, tap in enumerate(TAPS, 1):
            term = tap * (pick(m) - pick(-m))
            total = term if total is None else total + term
        return total

    def along_x(ref, f, box):
        return tap_sum(lambda m: view(ref, f, box, dx=m))

    def along_z(ref, f, box):
        return tap_sum(lambda m: view(ref, f, box, dz=m))

    def along_y(ref, f, box):
        x = view(ref, f, box)
        shape = x.shape
        x = x.reshape(shape[0] * shape[1], 128)
        return dot(jnp.concatenate(halves(x), axis=1), wy[...]).reshape(shape)

    def coefs(f, box):
        (x, nx), (z, nz) = box[2:]
        return coef[f, x : x + nx, z : z + nz, :]

    def gradient(ref, f, box):
        return along_x(ref, f, box), along_z(ref, f, box), along_y(ref, f, box)

    def blown(slopes, box):
        return coefs(0, box) * slopes[0] + coefs(1, box) * slopes[1] + coefs(2, box) * slopes[2]

    def put(ref, box, value):
        (x, nx), (z, nz) = box[2:]
        ref[x : x + nx, z : z + nz, :] = value

    def get(ref, box):
        (x, nx), (z, nz) = box[2:]
        return ref[x : x + nx, z : z + nz, :]

    def squeeze(ref, box):
        return coefs(3, box) * (along_x(ref, 1, box) + along_z(ref, 2, box) + along_y(ref, 3, box))

    def names_block(i, carry):
        start = pl.multiple_of(64 * i, 64)
        for f, block in enumerate(names(start, 64)):
            nmat[pl.ds(start, 64), f * NT : (f + 1) * NT] = block
        return carry

    lax.fori_loop(0, 24, names_block, 0)
    given = dot_nt(ohl[...], nmat[1024:1664, :])
    given = given[0:144] + given[144:288]
    for d in range(4):
        for q in range(NQ):
            tout[d, q * NJ : (q + 1) * NJ, :] = given[q * NJP : q * NJP + NJ, d * RIM : (d + 1) * RIM]
    traces_arrive = exchange([(d, tout.at[d], trecv.at[mirror_of[d]]) for d in range(4)])
    own_at = given[:, 512:640]

    local["air"].wait()
    speeds_arrive()
    start_pressure[...] = e0[0, own_x, own_z, :].reshape(128, 128)
    for block in (-1, 0, 1):
        arrived = combine(block, own_speed, srecv, 0)
        cells = combine(block, own_cells, srecv, 1).astype(jnp.int32)
        cell_rows = lax.shift_right_logical(cells, 7)
        cell_lanes = lax.bitwise_and(cells, 127)
        at_row = jnp.where(iota((128, 128), 0) == cell_rows, arrived, 0.0)
        at_lane = jnp.where(iota((128, 128), 0) == cell_lanes, 1.0, 0.0).astype(BF16)
        if block == 0:
            own_rows = cell_rows
            bt[...] = at_lane
        gained[block + 1] = dot_nt(
            jnp.concatenate(halves(at_row), axis=1), jnp.concatenate([at_lane, at_lane], axis=1)
        ).reshape(8, 16, 128)
    e0[0, own_x, own_z, :] = e0[0, own_x, own_z, :] + gained[1]
    pressure_first()
    for block in (-1, 1):
        where = pl.ds(8 + 8 * block, 8)
        e0[0, where, own_z, :] = e0[0, where, own_z, :] + gained[block + 1]
    pressure_arrive = exchange(send_pressure_z(e0))

    picked = dot(jnp.concatenate(thirds(start_pressure[...]), axis=0), bt[...])
    picked = picked[0:128] + picked[128:256] + picked[256:384]
    looked = jnp.sum(jnp.where(iota((128, 128), 0) == own_rows, picked, 0.0), axis=0, keepdims=True)
    ptile[...] = jnp.broadcast_to(looked, (8, 128))
    replies_arrive = surface(ptile, lambda off: precv.at[off + 2], -1, 2)

    first_arrive()
    local["wind"].wait()
    local["bulk"].wait()
    local["lift"].wait()
    for box in pieces:
        (x, nx), (z, nz) = box[2:]
        coef[:, x : x + nx, z : z + nz, :] = coef[:, x : x + nx, z : z + nz, :] * TAP_UNIT
    lift_of[...] = lift_of[...] * TAP_UNIT
    for box in pieces:
        put(base, box, squeeze(e0, box))

    def shadow_first():
        for f in range(4):
            cols = slice(f * NT, (f + 1) * NT)
            gathered = dot(ohl[...], nmat[0:SLOTS, cols])
            gathered = gathered[0:144] + gathered[144:288]
            for q in range(NQ):
                rows = slice(f * NJP, (f + 1) * NJP)
                diff[q, rows, :] = gathered[q * NJP : (q + 1) * NJP] - own[q, rows, :]

    def shadow_second():
        rotate(kv)

        def step(i, carry):
            vol[pl.ds(3 * i, 3)] = contract(3 * i)
            return carry

        lax.fori_loop(0, 3, step, 0)

    def shadow_third():
        replies_arrive()
        traces_arrive()
        replies = jnp.where(slot_row == 2, looked, 0.0)
        for r in (0, 1, 3, 4):
            ok = (a + r - 2 >= 0) & (a + r - 2 < strips)
            replies = jnp.where(slot_row == jnp.where(ok, r, -1), precv[r, 0:1, :], replies)
        replies = coupled * replies
        row_q = iota((NQ * NJP, 128), 0) // NJP
        mirrored = jnp.where(row_q < 3, -2.0 * replies - own_at, own_at)
        for half, values in enumerate(halves(mirrored)):
            rl[half * 144 : half * 144 + 144, 512:640] = values
        for d in range(4):
            for q in range(NQ):
                x = jnp.concatenate([trecv[d, q * NJ : (q + 1) * NJ, :], jnp.zeros((NJP - NJ, RIM), F32)], axis=0)
                for half, values in enumerate(halves(x)):
                    start = half * 144 + q * NJP
                    rl[start : start + NJP, d * RIM : (d + 1) * RIM] = values
        for f in range(4):
            cols = slice(f * NT, (f + 1) * NT)
            gathered = dot(rl[...], nmat[SLOTS:1664, cols])
            gathered = gathered[0:144] + gathered[144:288]
            for q in range(NQ):
                rows = slice(f * NJP, (f + 1) * NJP)
                diff[q, rows, :] = diff[q, rows, :] + gathered[q * NJP : (q + 1) * NJP]

    def shadow_fourth():
        local["flx"].wait()

        def step(i, carry):
            faces = []
            for f in range(4):
                total = None
                for q in range(NQ):
                    term = flx[pl.ds(3 * i, 3), q, f : f + 1, :] * diff[q, f * NJP : (f + 1) * NJP, :][None]
                    total = term if total is None else total + term
                faces.append(total)
            fluxed = jnp.concatenate(faces, axis=1)
            for k in range(3):
                high, low = halves(fluxed[k])
                lifted = dot(ls[:, 0:192], jnp.concatenate([high, low, high], axis=0))
                p = 3 * i + k
                sout[p] = sol[p] + (vol[p] + lifted[0:NBP])[0:NB]
            return carry

        lax.fori_loop(0, 3, step, 0)

    for f in range(3):
        adv[f] = view(e0, 1 + f, middle) - blown(gradient(e0, 1 + f, middle), middle)
    shadow_first()
    for substep in range(SUBSTEPS):
        here = ext[substep]
        final = substep == SUBSTEPS - 1
        pressure_arrive()
        if substep == 0:
            for box in pieces:
                put(pe, box, view(here, 0, box) - get(base, box) - blown(gradient(here, 0, box), box))
        else:
            for box in pieces:
                put(base, box, view(here, 0, box) - blown(gradient(here, 0, box), box))
            velocity_arrive()
            for box in pieces:
                put(pe, box, get(base, box) - squeeze(here, box))
            for f in range(3):
                adv[f] = view(here, 1 + f, middle) - blown(gradient(here, 1 + f, middle), middle)
        if not final:
            there = ext[substep + 1]
            there[0, 4:20, own_z, :] = pe[:, 8:24, :]
            pressure_arrive = send_pressure(there)
        slopes = [tap_sum(lambda m: pe[4 + m : 12 + m, 8:24, :]), tap_sum(lambda m: pe[4:12, 8 + m : 24 + m, :])]
        x = pe[4:12, 8:24, :].reshape(128, 128)
        slopes.append(dot(jnp.concatenate(halves(x), axis=1), wy[...]).reshape(8, 16, 128))
        for f in range(3):
            value = adv[f] - lift_of[...] * slopes[f]
            if final:
                uout[1 + f] = value
            else:
                there[1 + f, own_x, own_z, :] = value
        if final:
            uout[0] = pe[4:12, 8:24, :]
        else:
            velocity_arrive = send_speeds(there)
            if substep == 0:
                shadow_second()
            else:
                shadow_third()
                shadow_fourth()

    fetch("sol_out", sout, sol_out)
    fetch("air_out", uout, air_out)
    local["sol_out"].wait()
    local["air_out"].wait()
    for ok, copy in pending:
        pl.when(ok)(copy.wait_send)


def vmem(*shape, dtype=F32):
    return pltpu.VMEM(shape, dtype)


def solution(mesh):
    strips, bands = mesh.shape["gx"], mesh.shape["gz"]

    def shards(
        solid_state, jacobians, flux_solvers, stiffness, trace_matrix, lift_matrix,
        neighbours, send_faces, surface_map, surface_normals, air_state, wind_field, air_medium,
    ):
        def body(*refs):
            kernel(strips, bands, *refs)

        hbm = pl.BlockSpec(memory_space=pl.ANY)
        return pl.pallas_call(
            body,
            out_shape=(
                jax.ShapeDtypeStruct(solid_state.shape, F32),
                jax.ShapeDtypeStruct(air_state.shape, F32),
            ),
            in_specs=[hbm] * 12,
            out_specs=(hbm, hbm),
            scratch_shapes=[
                vmem(3, NB, NB), vmem(NJ, 4, NB), vmem(NJ, 4, NB), vmem(4, NT, dtype=jnp.int32),
                vmem(REACH, 3, CAP, dtype=jnp.int32), vmem(REACH, 3, CAP),
                vmem(NQ, NB, NT), vmem(NQ, NQ, 3, NT), vmem(NQ, NQ, 4, NT),
                vmem(4, 24, 48, 128), vmem(4, 24, 48, 128), vmem(4, 24, 48, 128),
                vmem(4, 16, 32, 128), vmem(16, 32, 128), vmem(8, 16, 128),
                vmem(NQ, 128, NT, dtype=BF16), vmem(NQ, 80, NT), vmem(NQ, NBP, NT), vmem(NQ, 64, NT),
                vmem(288, SLOTS, dtype=BF16), vmem(1664, SLOTS, dtype=BF16), vmem(NQ, 64, NT),
                vmem(NQ, NBP, NT), vmem(NQ, NB, NT), vmem(4, 8, 16, 128),
                vmem(128, 128), vmem(128, 128), vmem(64, 128),
                vmem(80, 128, dtype=BF16), vmem(80, 128, dtype=BF16), vmem(64, 128, dtype=BF16),
                vmem(32, 256, dtype=BF16), vmem(256, 128, dtype=BF16),
                vmem(3, 8, 128), vmem(3, 8, 128),
                vmem(16, 32, 128), vmem(3, 8, 16, 128), vmem(128, 128), vmem(3, 8, 16, 128), vmem(128, 128, dtype=BF16),
                vmem(8, 128), vmem(8, 128),
                vmem(7, 8, 128), vmem(REACH, 8, 128),
                vmem(4, 96, RIM), vmem(4, 96, RIM), vmem(288, 640, dtype=BF16),
                pltpu.SemaphoreType.DMA((16,)),
                pltpu.SemaphoreType.DMA((96,)),
                pltpu.SemaphoreType.DMA((96,)),
            ],
            compiler_params=pltpu.CompilerParams(
                collective_id=0, has_side_effects=True, vmem_limit_bytes=56 * 1024 * 1024
            ),
            name="coupled_step",
        )(
            solid_state,
            jnp.transpose(jacobians, (1, 2, 0, 3)),
            jnp.transpose(flux_solvers, (1, 2, 0, 3)),
            stiffness,
            jnp.transpose(trace_matrix, (1, 0, 2)),
            jnp.transpose(lift_matrix, (2, 0, 1)),
            neighbours,
            jnp.transpose(surface_map, (1, 0, 2)),
            jnp.transpose(surface_normals, (1, 0, 2)),
            air_state, wind_field, air_medium,
        )

    in_specs = (
        P(None, None, ("gx", "gz")),
        P(None, None, None, ("gx", "gz")),
        P(None, None, None, ("gx", "gz")),
        P(),
        P(),
        P(),
        P(None, ("gx", "gz")),
        P(None, ("gx", "gz")),
        P(None, None, ("gx", "gz")),
        P(None, None, ("gx", "gz")),
        P(None, "gx", "gz", None),
        P(None, "gx", "gz", None),
        P(None, "gx", "gz", None),
    )
    out_specs = (P(None, None, ("gx", "gz")), P(None, "gx", "gz", None))
    return jax.shard_map(shards, mesh=mesh, in_specs=in_specs, out_specs=out_specs, check_vma=False)
```

```python
import jax
import jax.numpy as jnp
from jax import lax
from jax.experimental import pallas as pl
from jax.experimental.pallas import tpu as pltpu
from jax.sharding import PartitionSpec as P

F32, BF16 = jnp.float32, jnp.bfloat16
MESH = pl.DeviceIdType.MESH

ORDERS = 4
TIME_STEP = 0.5
SUBSTEPS = 3
TAPS = (672.0, -168.0, 32.0, -3.0)
TAP_UNIT = 1.0 / 840.0

NQ, NB, NBP = 9, 20, 24
NJ, NJP = 10, 16
NT = 256
SLOTS = 4 * NT
RIM = 128
CAP, REACH = 8, 5
LEFT, RIGHT, BELOW, ABOVE = range(4)


def halves(x):
    high = x.astype(BF16)
    return high, (x - high.astype(F32)).astype(BF16)


def thirds(x):
    high = x.astype(BF16)
    rest = x - high.astype(F32)
    mid = rest.astype(BF16)
    return high, mid, (rest - mid.astype(F32)).astype(BF16)


def dot(a, b):
    return jnp.dot(a, b, preferred_element_type=F32)


def dot_nt(a, b):
    return lax.dot_general(a, b, (((1,), (1,)), ((), ())), preferred_element_type=F32)


def iota(shape, dim):
    return lax.broadcasted_iota(jnp.int32, shape, dim)


def stacked_left(padded, gap):
    high = padded.astype(BF16).astype(F32)
    low = padded - high
    return high + pltpu.roll(high, gap, 1) + pltpu.roll(low, 2 * gap, 1)


def lane_row(tile):
    total = tile[0:1]
    for r in range(1, REACH):
        total = total + pltpu.roll(tile, CAP * r, 1)[r : r + 1]
    return total


def kernel(strips, bands, *refs):
    (
        sol_h, jac_h, flx_h, stiff_h, trace_h, lift_h, nbr_h, surf_h, normal_h,
        air_h, wind_h, med_h,
        sol_out, air_out,
        stiff_ref, trace_ref, lift_ref, nbr_ref, surf_ref, normal_ref,
        sol, jac, flx, e0, e1, e2, coef, pe, lift_of,
        ds, rot, integ, own, ohl, nmat, diff, vol, sout, uout,
        ksc, lsc, tsc, kp, kv, ts, ls, wy, smt, nmt,
        base, adv, start_pressure, gained, bt, packed, corners,
        stile, ptile, srecv, precv, tout, trecv, rl,
        local_sem, send_sem, recv_sem,
    ) = refs
    ext = (e0, e1, e2)
    a = lax.axis_index("gx")
    b = lax.axis_index("gz")

    own_x, own_z = pl.ds(8, 8), pl.ds(16, 16)
    coef_x_own, coef_z_own = pl.ds(4, 8), pl.ds(8, 16)
    local = {}

    def fetch(name, src, dst):
        local[name] = pltpu.make_async_copy(src, dst, local_sem.at[len(local)])
        local[name].start()

    fetch("stiff", stiff_h, stiff_ref)
    fetch("sol", sol_h, sol)
    fetch("jac", jac_h, jac)
    fetch("trace", trace_h, trace_ref)
    fetch("nbr", nbr_h, nbr_ref)
    fetch("surf", surf_h, surf_ref)
    fetch("normal", normal_h, normal_ref)
    fetch("air", air_h, e0.at[:, own_x, own_z, :])
    fetch("wind", wind_h, coef.at[pl.ds(0, 3), coef_x_own, coef_z_own])
    fetch("bulk", med_h.at[0], coef.at[3, coef_x_own, coef_z_own])
    fetch("lift", med_h.at[1], lift_of)
    fetch("flx", flx_h, flx)
    fetch("lifting", lift_h, lift_ref)

    can = {LEFT: a > 0, RIGHT: a < strips - 1, BELOW: b > 0, ABOVE: b < bands - 1}
    peer = {
        LEFT: (jnp.maximum(a - 1, 0), b),
        RIGHT: (jnp.minimum(a + 1, strips - 1), b),
        BELOW: (a, jnp.maximum(b - 1, 0)),
        ABOVE: (a, jnp.minimum(b + 1, bands - 1)),
    }
    mirror_of = {LEFT: RIGHT, RIGHT: LEFT, BELOW: ABOVE, ABOVE: BELOW}
    sem_count = [0]
    pending = []

    def remote(src, dst, device, sem):
        return pltpu.make_async_remote_copy(
            src_ref=src, dst_ref=dst, send_sem=send_sem.at[sem], recv_sem=recv_sem.at[sem],
            device_id=device, device_id_type=MESH,
        )

    def exchange(parts):
        copies = []
        for d, src, dst in parts:
            ok, device = side(d)
            copy = remote(src, dst, device, sem_count[0])
            sem_count[0] += 1
            pl.when(ok)(copy.start)
            pending.append((ok, copy))
            copies.append((d, copy))

        def arrive():
            for d, copy in copies:
                pl.when(side(opposite(d))[0])(copy.wait_recv)

        return arrive

    def opposite(d):
        return tuple(mirror_of[k] for k in d) if isinstance(d, tuple) else mirror_of[d]

    def side(d):
        if isinstance(d, tuple):
            return can[d[0]] & can[d[1]], (peer[d[0]][0], peer[d[1]][1])
        return can[d], peer[d]

    def surface(src, place, sign, reach):
        waits = []
        for off in (3, -3, 2, -2, 1, -1):
            if abs(off) > reach:
                continue
            to = a + sign * off
            source = a - sign * off
            to_ok = (to >= 0) & (to < strips)
            from_ok = (source >= 0) & (source < strips)
            copy = remote(src, place(off), (jnp.clip(to, 0, strips - 1), b), sem_count[0])
            sem_count[0] += 1
            pl.when(to_ok)(copy.start)
            pending.append((to_ok, copy))
            waits.append((from_ok, copy))

        def arrive():
            for from_ok, copy in waits:
                pl.when(from_ok)(copy.wait_recv)

        return arrive

    diagonals = ((LEFT, BELOW), (LEFT, ABOVE), (RIGHT, BELOW), (RIGHT, ABOVE))
    x_near = {LEFT: pl.ds(8, 4), RIGHT: pl.ds(12, 4)}
    x_far = {LEFT: pl.ds(12, 4), RIGHT: pl.ds(8, 4)}
    near_land = {LEFT: pl.ds(16, 4), RIGHT: pl.ds(4, 4)}
    far_land = {LEFT: pl.ds(20, 4), RIGHT: pl.ds(0, 4)}
    all_land = {LEFT: pl.ds(16, 8), RIGHT: pl.ds(0, 8)}
    z_near = {BELOW: pl.ds(16, 8), ABOVE: pl.ds(24, 8)}
    z_land = {BELOW: pl.ds(32, 8), ABOVE: pl.ds(8, 8)}
    raw_x = {LEFT: pl.ds(0, 4), RIGHT: pl.ds(4, 4)}
    raw_z = {BELOW: pl.ds(0, 8), ABOVE: pl.ds(8, 8)}
    coef_x = {LEFT: pl.ds(12, 4), RIGHT: pl.ds(0, 4)}
    coef_z = {BELOW: pl.ds(24, 8), ABOVE: pl.ds(0, 8)}
    with_arms = pl.ds(4, 16)

    corner_x = {LEFT: (8, 16), RIGHT: (12, 4)}
    corner_z = {BELOW: (16, 32), ABOVE: (28, 12)}

    def send_corners(buffer, turn):
        parts = []
        for i, d in enumerate(diagonals):
            x, z = corner_x[d[0]][0], corner_z[d[1]][0]
            for plane in range(4):
                half = 4 * (plane % 2)
                packed[turn, i, :, plane // 2, half : half + 4, :] = buffer[1:3, x + plane, z : z + 4, :]
            parts.append((d, packed.at[turn, i], corners.at[turn, i]))
        arrive = exchange(parts)

        def unpack():
            arrive()
            for i, d in enumerate(diagonals):
                x, z = corner_x[d[0]][1], corner_z[d[1]][1]
                for plane in range(4):
                    half = 4 * (plane % 2)
                    buffer[1:3, x + plane, z : z + 4, :] = corners[turn, i, :, plane // 2, half : half + 4, :]

        return unpack

    def send_speeds(buffer, turn, raw=None):
        parts = []
        for d in (LEFT, RIGHT):
            if raw is None:
                parts.append((d, buffer.at[1, own_x, own_z], buffer.at[1, all_land[d], own_z]))
                parts.append((d, buffer.at[pl.ds(2, 2), x_near[d], own_z], buffer.at[pl.ds(2, 2), near_land[d], own_z]))
            else:
                parts.append((d, raw.at[1], buffer.at[1, all_land[d], own_z]))
                parts.append((d, raw.at[pl.ds(2, 2), raw_x[d]], buffer.at[pl.ds(2, 2), near_land[d], own_z]))
        for d in (BELOW, ABOVE):
            src = buffer.at[pl.ds(1, 3), own_x, z_near[d]]
            if raw is not None:
                src = raw.at[pl.ds(1, 3), :, raw_z[d]]
            parts.append((d, src, buffer.at[pl.ds(1, 3), own_x, z_land[d]]))
        sides = exchange(parts)
        unpack = send_corners(buffer, turn)

        def arrive():
            sides()
            unpack()

        return arrive

    def send_pressure_z(buffer):
        return [(d, buffer.at[0, with_arms, z_near[d]], buffer.at[0, with_arms, z_land[d]]) for d in (BELOW, ABOVE)]

    def send_pressure(buffer):
        parts = [(d, buffer.at[0, x_far[d], own_z], buffer.at[0, far_land[d], own_z]) for d in (LEFT, RIGHT)]
        return exchange(parts + send_pressure_z(buffer))

    def send_first():
        first = exchange([(d, air_h.at[0], e0.at[0, all_land[d], own_z]) for d in (LEFT, RIGHT)])
        local["air"].wait()
        second = send_speeds(e0, 0, air_h)
        parts = []
        for d in (LEFT, RIGHT):
            parts.append((d, wind_h.at[:, raw_x[d]], coef.at[pl.ds(0, 3), coef_x[d], coef_z_own]))
            parts.append((d, med_h.at[0, raw_x[d]], coef.at[3, coef_x[d], coef_z_own]))
        for d in (BELOW, ABOVE):
            parts.append((d, wind_h.at[:, :, raw_z[d]], coef.at[pl.ds(0, 3), coef_x_own, coef_z[d]]))
            parts.append((d, med_h.at[0, :, raw_z[d]], coef.at[3, coef_x_own, coef_z[d]]))
        third_parts = parts

        def arrive():
            second()
            third[0]()

        third = []
        return first, arrive, lambda: third.append(exchange(third_parts))

    for d, where, narrow in ((LEFT, pl.ds(0, 8), pl.ds(0, 4)), (RIGHT, pl.ds(16, 8), pl.ds(12, 4))):
        @pl.when(jnp.logical_not(can[d]))
        def _(where=where, narrow=narrow):
            for buffer in ext:
                buffer[:, where, 8:40, :] = jnp.zeros((4, 8, 32, 128), F32)
            coef[:, narrow, 8:24, :] = jnp.zeros((4, 4, 16, 128), F32)
    for d, where, narrow in ((BELOW, pl.ds(8, 8), pl.ds(0, 8)), (ABOVE, pl.ds(32, 8), pl.ds(24, 8))):
        @pl.when(jnp.logical_not(can[d]))
        def _(where=where, narrow=narrow):
            for buffer in ext:
                buffer[:, 4:20, where, :] = jnp.zeros((4, 16, 8, 128), F32)
            coef[:, 4:12, narrow, :] = jnp.zeros((4, 8, 8, 128), F32)
    srecv[...] = jnp.zeros_like(srecv)
    precv[...] = jnp.zeros_like(precv)
    trecv[...] = jnp.zeros_like(trecv)
    corners[...] = jnp.zeros_like(corners)

    barrier = pltpu.get_barrier_semaphore()
    greet = [(off, 0) for off in (-3, -2, -1, 1, 2, 3)] + [(x, z) for x in (-1, 0, 1) for z in (-1, 1)]
    for x, z in greet:
        pl.semaphore_signal(
            barrier, inc=1, device_id=(lax.rem(a + x + strips, strips), lax.rem(b + z + bands, bands)),
            device_id_type=MESH,
        )

    lane_halves = (slice(0, 128), slice(128, 256))

    def put_stack(cols, x):
        high, low = halves(jnp.concatenate([x, jnp.zeros((NQ, 8, 128), F32)], axis=1))
        ds[:, 0:32, cols] = high
        ds[:, 32:64, cols] = low
        ds[:, 64:96, cols] = high

    def rotate(left):
        for q in range(NQ):
            rot[q] = dot(left[...], ds[q])

    def contract(cols):
        total = None
        for q in range(NQ):
            for d in range(3):
                term = jac[:, q, d : d + 1, cols] * rot[q, d * NBP : (d + 1) * NBP, cols][None]
                total = term if total is None else total + term
        return total

    ksc[...] = jnp.zeros_like(ksc)
    tsc[...] = jnp.zeros_like(tsc)
    lsc[...] = jnp.zeros_like(lsc)
    smt[...] = jnp.zeros_like(smt)
    nmt[...] = jnp.zeros_like(nmt)
    integ[...] = jnp.zeros_like(integ)
    ds[:, 96:128, :] = jnp.zeros((NQ, 32, NT), BF16)
    local["stiff"].wait()
    for d in range(3):
        ksc[d * NBP : d * NBP + NB, 0:NB] = stiff_ref[d]
    kp[...] = (-stacked_left(ksc[0:80], 32)).astype(BF16)
    local["sol"].wait()
    for q in range(NQ):
        integ[q, 0:NB, :] = TIME_STEP * sol[q]
    for cols in lane_halves:
        put_stack(cols, integ[:, :, cols] * (1.0 / TIME_STEP))
    local["jac"].wait()
    weight = TIME_STEP
    for degree in range(1, ORDERS):
        weight = weight * TIME_STEP / (degree + 1)
        rotate(kp)
        if degree==2:
            pl.semaphore_wait(barrier, len(greet))
            pressure_first, first_arrive, send_coefs = send_first()

        for cols in lane_halves:
            now = contract(cols)
            total = integ[:, :, cols] + weight * now
            integ[:, :, cols] = total
            put_stack(cols, total if degree == ORDERS - 1 else now)

    local["trace"].wait()
    for f in range(4):
        rows = trace_ref[:, f, :]
        tsc[f * NJP : f * NJP + NJ, 0:NB] = rows
        tsc[f * NJP + NJ : f * NJP + NJ + 1, 0:NB] = jnp.sum(rows, axis=0, keepdims=True) * (1.0 / NJ)
    ts[...] = stacked_left(tsc[...], 32).astype(BF16)

    def names(start, count):
        these = iota((count, NT), 0) + start
        return [jnp.where(these == nbr_ref[f : f + 1, :], 1.0, 0.0).astype(BF16) for f in range(4)]

    local["nbr"].wait()
    for f, block in enumerate(names(1536, 128)):
        nmat[1536:1664, f * NT : (f + 1) * NT] = block
    local["surf"].wait()
    local["normal"].wait()
    for i in range(3):
        smt[i, 0:REACH, 0:CAP] = surf_ref[:, i, :].astype(F32)
        nmt[i, 0:REACH, 0:CAP] = normal_ref[:, i, :]
    own_cells = lane_row(smt[1])
    coupled = lane_row(smt[2])
    normals = [lane_row(nmt[c]) for c in range(3)]

    for q in reversed(range(NQ)):
        traces = dot(ts[...], ds[q])
        own[q] = traces
        high, low = halves(traces)
        for f in range(4):
            rows, cols = slice(f * NJP, (f + 1) * NJP), slice(f * NT, (f + 1) * NT)
            ohl[q * NJP : (q + 1) * NJP, cols] = high[rows]
            ohl[(NQ + q) * NJP : (NQ + q + 1) * NJP, cols] = low[rows]
    surf_names = nmat[1536:1664, :]
    at_faces = dot_nt(ohl[96:144, :], surf_names) + dot_nt(ohl[240:288, :], surf_names)
    speed = jnp.zeros((1, 128), F32)
    for c in range(3):
        speed = speed + normals[c] * at_faces[c * NJP + NJ : c * NJP + NJ + 1, :]
    own_speed = coupled * speed
    stile[...] = jnp.where(iota((8, 128), 0) == 0, own_speed, own_cells)

    speeds_arrive = surface(stile, lambda off: srecv.at[3 - off], 1, 3)

    send_coefs()
    local["lifting"].wait()
    for f in range(4):
        lsc[f * NJP : f * NJP + NJ, 0:NB] = lift_ref[:, f, :]
    flipped = jnp.transpose(ksc[...])[0:NBP]
    lanes = iota((NBP, 128), 1)
    turned = [jnp.where(lanes < NBP, flipped if d == 0 else pltpu.roll(flipped, 128 - d * NBP, 1), 0.0) for d in range(3)]
    turned.append(jnp.zeros((8, 128), F32))
    kv[...] = stacked_left(jnp.concatenate(turned, axis=0), 32).astype(BF16)
    lift = jnp.transpose(lsc[...])[0:32]
    lift_high = lift.astype(BF16).astype(F32)
    ls[:, 0:128] = (lift_high + pltpu.roll(lift_high, 64, 1)).astype(BF16)
    ls[:, 128:256] = (lift - lift_high).astype(BF16)
    shift = lax.rem(iota((256, 128), 0), 128) - iota((256, 128), 1)
    taps = jnp.zeros((256, 128), F32)
    for m, tap in enumerate(TAPS, 1):
        taps = jnp.where(shift == m, tap, jnp.where(shift == -m, -tap, taps))
    wy[...] = taps.astype(BF16)

    slot_row = iota((1, 128), 1) // CAP

    def combine(block, mine, buffer, row):
        total = jnp.zeros((1, 128), F32)
        for r in range(REACH):
            gap = block - (r - 2)
            if gap == 0:
                total = jnp.where(slot_row == r, mine, total)
            else:
                ok = (a + gap >= 0) & (a + gap < strips)
                total = jnp.where(slot_row == jnp.where(ok, r, -1), buffer[gap + 3, row : row + 1, :], total)
        return total

    pieces = (((8, 8), (8, 32), (4, 8), (0, 32)), ((4, 4), (16, 16), (0, 4), (8, 16)), ((16, 4), (16, 16), (12, 4), (8, 16)))
    middle = ((8, 8), (16, 16), (4, 8), (8, 16))

    def view(ref, f, box, dx=0, dz=0):
        (x, nx), (z, nz) = box[:2]
        return ref[f, x + dx : x + dx + nx, z + dz : z + dz + nz, :]

    def tap_sum(pick):
        total = None
        for m, tap in enumerate(TAPS, 1):
            term = tap * (pick(m) - pick(-m))
            total = term if total is None else total + term
        return total

    def along_x(ref, f, box):
        return tap_sum(lambda m: view(ref, f, box, dx=m))

    def along_z(ref, f, box):
        return tap_sum(lambda m: view(ref, f, box, dz=m))

    def along_y(ref, f, box):
        x = view(ref, f, box)
        shape = x.shape
        x = x.reshape(shape[0] * shape[1], 128)
        return dot(jnp.concatenate(halves(x), axis=1), wy[...]).reshape(shape)

    def coefs(f, box):
        (x, nx), (z, nz) = box[2:]
        return coef[f, x : x + nx, z : z + nz, :]

    def gradient(ref, f, box):
        return along_x(ref, f, box), along_z(ref, f, box), along_y(ref, f, box)

    def blown(slopes, box):
        return coefs(0, box) * slopes[0] + coefs(1, box) * slopes[1] + coefs(2, box) * slopes[2]

    def put(ref, box, value):
        (x, nx), (z, nz) = box[2:]
        ref[x : x + nx, z : z + nz, :] = value

    def get(ref, box):
        (x, nx), (z, nz) = box[2:]
        return ref[x : x + nx, z : z + nz, :]

    def squeeze(ref, box):
        return coefs(3, box) * (along_x(ref, 1, box) + along_z(ref, 2, box) + along_y(ref, 3, box))

    def names_block(i, carry):
        start = pl.multiple_of(64 * i, 64)
        for f, block in enumerate(names(start, 64)):
            nmat[pl.ds(start, 64), f * NT : (f + 1) * NT] = block
        return carry

    lax.fori_loop(0, 24, names_block, 0)
    given = dot_nt(ohl[...], nmat[1024:1664, :])
    given = given[0:144] + given[144:288]
    for d in range(4):
        for q in range(NQ):
            tout[d, q * NJ : (q + 1) * NJ, :] = given[q * NJP : q * NJP + NJ, d * RIM : (d + 1) * RIM]
    traces_arrive = exchange([(d, tout.at[d], trecv.at[mirror_of[d]]) for d in range(4)])
    own_at = given[:, 512:640]

    speeds_arrive()
    start_pressure[...] = e0[0, own_x, own_z, :].reshape(128, 128)
    for block in (-1, 0, 1):
        arrived = combine(block, own_speed, srecv, 0)
        cells = combine(block, own_cells, srecv, 1).astype(jnp.int32)
        cell_rows = lax.shift_right_logical(cells, 7)
        cell_lanes = lax.bitwise_and(cells, 127)
        at_row = jnp.where(iota((128, 128), 0) == cell_rows, arrived, 0.0)
        at_lane = jnp.where(iota((128, 128), 0) == cell_lanes, 1.0, 0.0).astype(BF16)
        if block == 0:
            own_rows = cell_rows
            bt[...] = at_lane
        gained[block + 1] = dot_nt(
            jnp.concatenate(halves(at_row), axis=1), jnp.concatenate([at_lane, at_lane], axis=1)
        ).reshape(8, 16, 128)
    e0[0, own_x, own_z, :] = e0[0, own_x, own_z, :] + gained[1]
    pressure_first()
    for block in (-1, 1):
        where = pl.ds(8 + 8 * block, 8)
        e0[0, where, own_z, :] = e0[0, where, own_z, :] + gained[block + 1]
    pressure_arrive = exchange(send_pressure_z(e0))

    picked = dot(jnp.concatenate(thirds(start_pressure[...]), axis=0), bt[...])
    picked = picked[0:128] + picked[128:256] + picked[256:384]
    looked = jnp.sum(jnp.where(iota((128, 128), 0) == own_rows, picked, 0.0), axis=0, keepdims=True)
    ptile[...] = jnp.broadcast_to(looked, (8, 128))
    replies_arrive = surface(ptile, lambda off: precv.at[off + 2], -1, 2)

    first_arrive()
    local["wind"].wait()
    local["bulk"].wait()
    local["lift"].wait()
    for box in pieces:
        (x, nx), (z, nz) = box[2:]
        coef[:, x : x + nx, z : z + nz, :] = coef[:, x : x + nx, z : z + nz, :] * TAP_UNIT
    lift_of[...] = lift_of[...] * TAP_UNIT
    for box in pieces:
        put(base, box, squeeze(e0, box))

    def shadow_first():
        for f in range(4):
            cols = slice(f * NT, (f + 1) * NT)
            gathered = dot(ohl[...], nmat[0:SLOTS, cols])
            gathered = gathered[0:144] + gathered[144:288]
            for q in range(NQ):
                rows = slice(f * NJP, (f + 1) * NJP)
                diff[q, rows, :] = gathered[q * NJP : (q + 1) * NJP] - own[q, rows, :]

    def shadow_second():
        rotate(kv)

        for cols in lane_halves:
            vol[:, :, cols] = contract(cols)

    def shadow_third():
        replies_arrive()
        traces_arrive()
        replies = jnp.where(slot_row == 2, looked, 0.0)
        for r in (0, 1, 3, 4):
            ok = (a + r - 2 >= 0) & (a + r - 2 < strips)
            replies = jnp.where(slot_row == jnp.where(ok, r, -1), precv[r, 0:1, :], replies)
        replies = coupled * replies
        row_q = iota((NQ * NJP, 128), 0) // NJP
        mirrored = jnp.where(row_q < 3, -2.0 * replies - own_at, own_at)
        for half, values in enumerate(halves(mirrored)):
            rl[half * 144 : half * 144 + 144, 512:640] = values
        for d in range(4):
            for q in range(NQ):
                x = jnp.concatenate([trecv[d, q * NJ : (q + 1) * NJ, :], jnp.zeros((NJP - NJ, RIM), F32)], axis=0)
                for half, values in enumerate(halves(x)):
                    start = half * 144 + q * NJP
                    rl[start : start + NJP, d * RIM : (d + 1) * RIM] = values
        for f in range(4):
            cols = slice(f * NT, (f + 1) * NT)
            gathered = dot(rl[...], nmat[SLOTS:1664, cols])
            gathered = gathered[0:144] + gathered[144:288]
            for q in range(NQ):
                rows = slice(f * NJP, (f + 1) * NJP)
                diff[q, rows, :] = diff[q, rows, :] + gathered[q * NJP : (q + 1) * NJP]

    def shadow_fourth():
        local["flx"].wait()

        def step(i, carry):
            faces = []
            for f in range(4):
                total = None
                for q in range(NQ):
                    term = flx[pl.ds(3 * i, 3), q, f : f + 1, :] * diff[q, f * NJP : (f + 1) * NJP, :][None]
                    total = term if total is None else total + term
                faces.append(total)
            fluxed = jnp.concatenate(faces, axis=1)
            for k in range(3):
                high, low = halves(fluxed[k])
                lifted = dot(ls[:, 0:192], jnp.concatenate([high, low, high], axis=0))
                p = 3 * i + k
                sout[p] = sol[p] + (vol[p] + lifted[0:NBP])[0:NB]
            return carry

        lax.fori_loop(0, 3, step, 0)

    for f in range(3):
        adv[f] = view(e0, 1 + f, middle) - blown(gradient(e0, 1 + f, middle), middle)
    shadow_first()
    for substep in range(SUBSTEPS):
        here = ext[substep]
        final = substep == SUBSTEPS - 1
        pressure_arrive()
        if substep == 0:
            for box in pieces:
                put(pe, box, view(here, 0, box) - get(base, box) - blown(gradient(here, 0, box), box))
        else:
            for box in pieces:
                put(base, box, view(here, 0, box) - blown(gradient(here, 0, box), box))
            velocity_arrive()
            for box in pieces:
                put(pe, box, get(base, box) - squeeze(here, box))
            for f in range(3):
                adv[f] = view(here, 1 + f, middle) - blown(gradient(here, 1 + f, middle), middle)
        if not final:
            there = ext[substep + 1]
            there[0, 4:20, own_z, :] = pe[:, 8:24, :]
            pressure_arrive = send_pressure(there)
        slopes = [tap_sum(lambda m: pe[4 + m : 12 + m, 8:24, :]), tap_sum(lambda m: pe[4:12, 8 + m : 24 + m, :])]
        x = pe[4:12, 8:24, :].reshape(128, 128)
        slopes.append(dot(jnp.concatenate(halves(x), axis=1), wy[...]).reshape(8, 16, 128))
        for f in range(3):
            value = adv[f] - lift_of[...] * slopes[f]
            if final:
                uout[1 + f] = value
            else:
                there[1 + f, own_x, own_z, :] = value
        if final:
            uout[0] = pe[4:12, 8:24, :]
        else:
            velocity_arrive = send_speeds(there, substep + 1)
            if substep == 0:
                shadow_second()
            else:
                shadow_third()
                shadow_fourth()

    fetch("sol_out", sout, sol_out)
    fetch("air_out", uout, air_out)
    local["sol_out"].wait()
    local["air_out"].wait()
    for ok, copy in pending:
        pl.when(ok)(copy.wait_send)


def vmem(*shape, dtype=F32):
    return pltpu.VMEM(shape, dtype)


def solution(mesh):
    strips, bands = mesh.shape["gx"], mesh.shape["gz"]

    def shards(
        solid_state, jacobians, flux_solvers, stiffness, trace_matrix, lift_matrix,
        neighbours, send_faces, surface_map, surface_normals, air_state, wind_field, air_medium,
    ):
        def body(*refs):
            kernel(strips, bands, *refs)

        hbm = pl.BlockSpec(memory_space=pl.ANY)
        out = pl.pallas_call(
            body,
            out_shape=(
                jax.ShapeDtypeStruct(solid_state.shape, F32),
                jax.ShapeDtypeStruct(air_state.shape, F32),
            ),
            in_specs=[hbm] * 12,
            out_specs=(hbm, hbm),
            scratch_shapes=[
                vmem(3, NB, NB), vmem(NJ, 4, NB), vmem(NJ, 4, NB), vmem(4, NT, dtype=jnp.int32),
                vmem(REACH, 3, CAP, dtype=jnp.int32), vmem(REACH, 3, CAP),
                vmem(NQ, NB, NT), vmem(NQ, NQ, 3, NT), vmem(NQ, NQ, 4, NT),
                vmem(4, 24, 48, 128), vmem(4, 24, 48, 128), vmem(4, 24, 48, 128),
                vmem(4, 16, 32, 128), vmem(16, 32, 128), vmem(8, 16, 128),
                vmem(NQ, 128, NT, dtype=BF16), vmem(NQ, 80, NT), vmem(NQ, NBP, NT), vmem(NQ, 64, NT),
                vmem(288, SLOTS, dtype=BF16), vmem(1664, SLOTS, dtype=BF16), vmem(NQ, 64, NT),
                vmem(NQ, NBP, NT), vmem(NQ, NB, NT), vmem(4, 8, 16, 128),
                vmem(128, 128), vmem(128, 128), vmem(64, 128),
                vmem(80, 128, dtype=BF16), vmem(80, 128, dtype=BF16), vmem(64, 128, dtype=BF16),
                vmem(32, 256, dtype=BF16), vmem(256, 128, dtype=BF16),
                vmem(3, 8, 128), vmem(3, 8, 128),
                vmem(16, 32, 128), vmem(3, 8, 16, 128), vmem(128, 128), vmem(3, 8, 16, 128), vmem(128, 128, dtype=BF16),
                vmem(3, 4, 2, 2, 8, 128), vmem(3, 4, 2, 2, 8, 128),
                vmem(8, 128), vmem(8, 128),
                vmem(7, 8, 128), vmem(REACH, 8, 128),
                vmem(4, 96, RIM), vmem(4, 96, RIM), vmem(288, 640, dtype=BF16),
                pltpu.SemaphoreType.DMA((16,)),
                pltpu.SemaphoreType.DMA((96,)),
                pltpu.SemaphoreType.DMA((96,)),
            ],
            compiler_params=pltpu.CompilerParams(
                collective_id=0, has_side_effects=True, vmem_limit_bytes=56 * 1024 * 1024
            ),
            name="coupled_step",
        )(
            solid_state,
            jnp.transpose(jacobians, (1, 2, 0, 3)),
            jnp.transpose(flux_solvers, (1, 2, 0, 3)),
            stiffness,
            jnp.transpose(trace_matrix, (1, 0, 2)),
            jnp.transpose(lift_matrix, (2, 0, 1)),
            neighbours,
            jnp.transpose(surface_map, (1, 0, 2)),
            jnp.transpose(surface_normals, (1, 0, 2)),
            air_state, wind_field, air_medium,
        )
        def hand(x, y, xo, yo, xv, yv, sem):
            pairs = [(x, xv, xo)] + [(y.at[k], yv.at[k], yo.at[k]) for k in range(4)]
            reads = [pltpu.make_async_copy(p[0], p[1], sem.at[0, i]) for i, p in enumerate(pairs)]
            writes = [pltpu.make_async_copy(p[1], p[2], sem.at[1, i]) for i, p in enumerate(pairs)]
            for r in reads:
                r.start()
            for r, w in zip(reads, writes):
                r.wait()
                w.start()
            for w in writes:
                w.wait()

        return pl.pallas_call(
            hand,
            out_shape=(jax.ShapeDtypeStruct(solid_state.shape, F32), jax.ShapeDtypeStruct(air_state.shape, F32)),
            in_specs=[hbm, hbm],
            out_specs=(hbm, hbm),
            scratch_shapes=[vmem(*solid_state.shape), vmem(*air_state.shape), pltpu.SemaphoreType.DMA((2, 5))],
            compiler_params=pltpu.CompilerParams(vmem_limit_bytes=60 * 1024 * 1024),
            name="hand_over",
        )(*out)

    in_specs = (
        P(None, None, ("gx", "gz")),
        P(None, None, None, ("gx", "gz")),
        P(None, None, None, ("gx", "gz")),
        P(),
        P(),
        P(),
        P(None, ("gx", "gz")),
        P(None, ("gx", "gz")),
        P(None, None, ("gx", "gz")),
        P(None, None, ("gx", "gz")),
        P(None, "gx", "gz", None),
        P(None, "gx", "gz", None),
        P(None, "gx", "gz", None),
    )
    out_specs = (P(None, None, ("gx", "gz")), P(None, "gx", "gz", None))
    return jax.shard_map(shards, mesh=mesh, in_specs=in_specs, out_specs=out_specs, check_vma=False)
```

```python
import jax
import jax.numpy as jnp
from jax import lax
from jax.experimental import pallas as pl
from jax.experimental.pallas import tpu as pltpu
from jax.sharding import PartitionSpec as P

F32, BF16 = jnp.float32, jnp.bfloat16
MESH = pl.DeviceIdType.MESH

ORDERS = 4
TIME_STEP = 0.5
SUBSTEPS = 3
TAPS = (672.0, -168.0, 32.0, -3.0)
TAP_UNIT = 1.0 / 840.0

NQ, NB, NBP = 9, 20, 24
NJ, NJP = 10, 16
NT = 256
SLOTS = 4 * NT
RIM = 128
CAP, REACH = 8, 5
LEFT, RIGHT, BELOW, ABOVE = range(4)


def halves(x):
    high = x.astype(BF16)
    return high, (x - high.astype(F32)).astype(BF16)


def thirds(x):
    high = x.astype(BF16)
    rest = x - high.astype(F32)
    mid = rest.astype(BF16)
    return high, mid, (rest - mid.astype(F32)).astype(BF16)


def dot(a, b):
    return jnp.dot(a, b, preferred_element_type=F32)


def dot_nt(a, b):
    return lax.dot_general(a, b, (((1,), (1,)), ((), ())), preferred_element_type=F32)


def iota(shape, dim):
    return lax.broadcasted_iota(jnp.int32, shape, dim)


def stacked_left(padded, gap):
    high = padded.astype(BF16).astype(F32)
    low = padded - high
    return high + pltpu.roll(high, gap, 1) + pltpu.roll(low, 2 * gap, 1)


def lane_row(tile):
    total = tile[0:1]
    for r in range(1, REACH):
        total = total + pltpu.roll(tile, CAP * r, 1)[r : r + 1]
    return total


def kernel(strips, bands, *refs):
    (
        sol_h, jac_h, flx_h, stiff_h, trace_h, lift_h, nbr_h, surf_h, normal_h,
        air_h, wind_h, med_h,
        sol_out, air_out,
        stiff_ref, trace_ref, lift_ref, nbr_ref, surf_ref, normal_ref,
        sol, jac, flx, e0, e1, e2, coef, pe, lift_of,
        ds, rot, integ, own, ohl, nmat, diff, vol, sout, uout,
        ksc, lsc, tsc, kp, kv, ts, ls, wy, smt, nmt,
        base, adv, start_pressure, gained, bt, packed, corners, beyond, added,
        stile, ptile, srecv, precv, tout, trecv, rl,
        local_sem, send_sem, recv_sem,
    ) = refs
    ext = (e0, e1, e2)
    a = lax.axis_index("gx")
    b = lax.axis_index("gz")

    own_x, own_z = pl.ds(8, 8), pl.ds(16, 16)
    coef_x_own, coef_z_own = pl.ds(4, 8), pl.ds(8, 16)
    local = {}

    def fetch(name, src, dst):
        local[name] = pltpu.make_async_copy(src, dst, local_sem.at[len(local)])
        local[name].start()

    fetch("stiff", stiff_h, stiff_ref)
    fetch("sol", sol_h, sol)
    fetch("jac", jac_h, jac)
    fetch("trace", trace_h, trace_ref)
    fetch("nbr", nbr_h, nbr_ref)
    fetch("surf", surf_h, surf_ref)
    fetch("normal", normal_h, normal_ref)
    fetch("air", air_h, e0.at[:, own_x, own_z, :])
    fetch("wind", wind_h, coef.at[pl.ds(0, 3), coef_x_own, coef_z_own])
    fetch("bulk", med_h.at[0], coef.at[3, coef_x_own, coef_z_own])
    fetch("lift", med_h.at[1], lift_of)
    fetch("flx", flx_h, flx)
    fetch("lifting", lift_h, lift_ref)

    can = {LEFT: a > 0, RIGHT: a < strips - 1, BELOW: b > 0, ABOVE: b < bands - 1}
    peer = {
        LEFT: (jnp.maximum(a - 1, 0), b),
        RIGHT: (jnp.minimum(a + 1, strips - 1), b),
        BELOW: (a, jnp.maximum(b - 1, 0)),
        ABOVE: (a, jnp.minimum(b + 1, bands - 1)),
    }
    mirror_of = {LEFT: RIGHT, RIGHT: LEFT, BELOW: ABOVE, ABOVE: BELOW}
    sem_count = [0]
    pending = []

    def remote(src, dst, device, sem):
        return pltpu.make_async_remote_copy(
            src_ref=src, dst_ref=dst, send_sem=send_sem.at[sem], recv_sem=recv_sem.at[sem],
            device_id=device, device_id_type=MESH,
        )

    def exchange(parts):
        groups = {}
        for d, src, dst in parts:
            groups.setdefault(d, []).append(remote(src, dst, side(d)[1], sem_count[0]))
            sem_count[0] += 1
        for d, copies in groups.items():
            pl.when(side(d)[0])(every(copies, "start"))
            pending.append((side(d)[0], copies))

        def arrive():
            for d, copies in groups.items():
                pl.when(side(opposite(d))[0])(every(copies, "wait_recv"))

        return arrive

    def every(copies, name):
        def act():
            for copy in copies:
                getattr(copy, name)()

        return act

    def settle():
        for ok, copies in pending:
            pl.when(ok)(every(copies, "wait_send"))
        pending.clear()

    def opposite(d):
        return tuple(mirror_of[k] for k in d) if isinstance(d, tuple) else mirror_of[d]

    def side(d):
        if isinstance(d, tuple):
            return can[d[0]] & can[d[1]], (peer[d[0]][0], peer[d[1]][1])
        return can[d], peer[d]

    def surface(src, place, sign, reach):
        waits = []
        for off in (3, -3, 2, -2, 1, -1):
            if abs(off) > reach:
                continue
            to = a + sign * off
            source = a - sign * off
            to_ok = (to >= 0) & (to < strips)
            from_ok = (source >= 0) & (source < strips)
            copy = remote(src, place(off), (jnp.clip(to, 0, strips - 1), b), sem_count[0])
            sem_count[0] += 1
            pl.when(to_ok)(copy.start)
            pending.append((to_ok, [copy]))
            waits.append((from_ok, copy))

        def arrive():
            for from_ok, copy in waits:
                pl.when(from_ok)(copy.wait_recv)

        return arrive

    diagonals = ((LEFT, BELOW), (LEFT, ABOVE), (RIGHT, BELOW), (RIGHT, ABOVE))
    x_near = {LEFT: pl.ds(8, 4), RIGHT: pl.ds(12, 4)}
    near_land = {LEFT: pl.ds(16, 4), RIGHT: pl.ds(4, 4)}
    z_near = {BELOW: pl.ds(16, 8), ABOVE: pl.ds(24, 8)}
    z_land = {BELOW: pl.ds(32, 8), ABOVE: pl.ds(8, 8)}
    raw_x = {LEFT: pl.ds(0, 4), RIGHT: pl.ds(4, 4)}
    raw_z = {BELOW: pl.ds(0, 8), ABOVE: pl.ds(8, 8)}
    coef_x = {LEFT: pl.ds(12, 4), RIGHT: pl.ds(0, 4)}
    coef_z = {BELOW: pl.ds(24, 8), ABOVE: pl.ds(0, 8)}
    with_arms = pl.ds(4, 16)

    corner_x = {LEFT: (8, 16), RIGHT: (12, 4)}
    corner_z = {BELOW: (16, 32), ABOVE: (28, 12)}

    def send_corners(buffer, turn):
        parts = []
        for i, d in enumerate(diagonals):
            x, z = corner_x[d[0]][0], corner_z[d[1]][0]
            for plane in range(4):
                half = 4 * (plane % 2)
                packed[turn, i, :, plane // 2, half : half + 4, :] = buffer[1:3, x + plane, z : z + 4, :]
            parts.append((d, packed.at[turn, i], corners.at[turn, i]))
        arrive = exchange(parts)

        def unpack():
            arrive()
            for i, d in enumerate(diagonals):
                x, z = corner_x[d[0]][1], corner_z[d[1]][1]
                for plane in range(4):
                    half = 4 * (plane % 2)
                    buffer[1:3, x + plane, z : z + 4, :] = corners[turn, i, :, plane // 2, half : half + 4, :]

        return unpack

    def send_speeds(buffer, turn):
        some = pl.ds(1, 3)
        parts = [(d, buffer.at[some, x_near[d], own_z], buffer.at[some, near_land[d], own_z]) for d in (LEFT, RIGHT)]
        for d in (BELOW, ABOVE):
            parts.append((d, buffer.at[pl.ds(1, 3), own_x, z_near[d]], buffer.at[pl.ds(1, 3), own_x, z_land[d]]))
        sides = exchange(parts)
        unpack = send_corners(buffer, turn)

        def arrive():
            sides()
            unpack()

        return arrive

    def send_beyond(buffer, turn, unit=1.0):
        for d in (LEFT, RIGHT):
            for plane in range(4):
                x = 8 + plane if d == LEFT else 12 + plane
                parts = []
                for f in (0, 1):
                    total = None
                    for m, tap in enumerate(TAPS, 1):
                        other = x + m if d == LEFT else x - m
                        if (d == LEFT) == (other >= 12):
                            term = tap * buffer[f, other, 16:32, :]
                            total = term if total is None else total + term
                    parts.append(total)
                value = unit * (coef[0, x - 4, 8:24, :] * parts[0] + coef[3, x - 4, 8:24, :] * parts[1])
                beyond[turn, d, plane] = -value if d == LEFT else value
        return exchange([(d, beyond.at[turn, d], added.at[turn, mirror_of[d]]) for d in (LEFT, RIGHT)])

    def send_pressure_z(buffer):
        return [(d, buffer.at[0, with_arms, z_near[d]], buffer.at[0, with_arms, z_land[d]]) for d in (BELOW, ABOVE)]

    def send_pressure(buffer):
        return exchange(send_pressure_z(buffer))

    def send_first():
        local["air"].wait()
        local["wind"].wait()
        local["bulk"].wait()
        first = exchange([(d, air_h.at[0, raw_x[d]], e0.at[0, near_land[d], own_z]) for d in (LEFT, RIGHT)])
        second = send_beyond(e0, 0, TAP_UNIT)
        fourth = send_speeds(e0, 0)
        parts = []
        for d in (LEFT, RIGHT):
            parts.append((d, wind_h.at[:, raw_x[d]], coef.at[pl.ds(0, 3), coef_x[d], coef_z_own]))
            parts.append((d, med_h.at[0, raw_x[d]], coef.at[3, coef_x[d], coef_z_own]))
        for d in (BELOW, ABOVE):
            parts.append((d, wind_h.at[:, :, raw_z[d]], coef.at[pl.ds(0, 3), coef_x_own, coef_z[d]]))
            parts.append((d, med_h.at[0, :, raw_z[d]], coef.at[3, coef_x_own, coef_z[d]]))
        third_parts = parts

        def arrive():
            second()
            fourth()
            third[0]()

        third = []
        return first, arrive, lambda: third.append(exchange(third_parts))

    for d, where, narrow in ((LEFT, pl.ds(0, 8), pl.ds(0, 4)), (RIGHT, pl.ds(16, 8), pl.ds(12, 4))):
        @pl.when(jnp.logical_not(can[d]))
        def _(where=where, narrow=narrow):
            for buffer in ext:
                buffer[:, where, 8:40, :] = jnp.zeros((4, 8, 32, 128), F32)
            coef[:, narrow, 8:24, :] = jnp.zeros((4, 4, 16, 128), F32)
    for d, where, narrow in ((BELOW, pl.ds(8, 8), pl.ds(0, 8)), (ABOVE, pl.ds(32, 8), pl.ds(24, 8))):
        @pl.when(jnp.logical_not(can[d]))
        def _(where=where, narrow=narrow):
            for buffer in ext:
                buffer[:, 4:20, where, :] = jnp.zeros((4, 16, 8, 128), F32)
            coef[:, 4:12, narrow, :] = jnp.zeros((4, 8, 8, 128), F32)
    srecv[...] = jnp.zeros_like(srecv)
    precv[...] = jnp.zeros_like(precv)
    trecv[...] = jnp.zeros_like(trecv)
    corners[...] = jnp.zeros_like(corners)
    added[...] = jnp.zeros_like(added)
    for buffer in ext:
        for x in (0, 20):
            buffer[0:2, x : x + 4, 16:32, :] = jnp.zeros((2, 4, 16, 128), F32)

    barrier = pltpu.get_barrier_semaphore()
    greet = [(off, 0) for off in (-3, -2, -1, 1, 2, 3)] + [(x, z) for x in (-1, 0, 1) for z in (-1, 1)]
    for x, z in greet:
        pl.semaphore_signal(
            barrier, inc=1, device_id=(lax.rem(a + x + strips, strips), lax.rem(b + z + bands, bands)),
            device_id_type=MESH,
        )

    lane_halves = (slice(0, 128), slice(128, 256))

    def put_stack(cols, x):
        high, low = halves(jnp.concatenate([x, jnp.zeros((NQ, 8, 128), F32)], axis=1))
        ds[:, 0:32, cols] = high
        ds[:, 32:64, cols] = low
        ds[:, 64:96, cols] = high

    def rotate(left):
        for q in range(NQ):
            rot[q] = dot(left[...], ds[q])

    def contract(cols):
        total = None
        for q in range(NQ):
            for d in range(3):
                term = jac[:, q, d : d + 1, cols] * rot[q, d * NBP : (d + 1) * NBP, cols][None]
                total = term if total is None else total + term
        return total

    ksc[...] = jnp.zeros_like(ksc)
    tsc[...] = jnp.zeros_like(tsc)
    lsc[...] = jnp.zeros_like(lsc)
    smt[...] = jnp.zeros_like(smt)
    nmt[...] = jnp.zeros_like(nmt)
    integ[...] = jnp.zeros_like(integ)
    ds[:, 96:128, :] = jnp.zeros((NQ, 32, NT), BF16)
    local["stiff"].wait()
    for d in range(3):
        ksc[d * NBP : d * NBP + NB, 0:NB] = stiff_ref[d]
    kp[...] = (-stacked_left(ksc[0:80], 32)).astype(BF16)
    local["trace"].wait()
    for f in range(4):
        rows = trace_ref[:, f, :]
        tsc[f * NJP : f * NJP + NJ, 0:NB] = rows
        tsc[f * NJP + NJ : f * NJP + NJ + 1, 0:NB] = jnp.sum(rows, axis=0, keepdims=True) * (1.0 / NJ)
    ts[...] = stacked_left(tsc[...], 32).astype(BF16)

    def names(start, count):
        these = iota((count, NT), 0) + start
        return [jnp.where(these == nbr_ref[f : f + 1, :], 1.0, 0.0).astype(BF16) for f in range(4)]

    local["nbr"].wait()
    for f, block in enumerate(names(1536, 128)):
        nmat[1536:1664, f * NT : (f + 1) * NT] = block
    local["surf"].wait()
    local["normal"].wait()
    for i in range(3):
        smt[i, 0:REACH, 0:CAP] = surf_ref[:, i, :].astype(F32)
        nmt[i, 0:REACH, 0:CAP] = normal_ref[:, i, :]
    own_cells = lane_row(smt[1])
    coupled = lane_row(smt[2])
    normals = [lane_row(nmt[c]) for c in range(3)]

    local["sol"].wait()
    for q in range(NQ):
        integ[q, 0:NB, :] = TIME_STEP * sol[q]
    for cols in lane_halves:
        put_stack(cols, integ[:, :, cols] * (1.0 / TIME_STEP))
    local["jac"].wait()
    weight = TIME_STEP
    for degree in range(1, ORDERS):
        weight = weight * TIME_STEP / (degree + 1)
        rotate(kp)
        if degree==2:
            pl.semaphore_wait(barrier, len(greet))
            pressure_first, first_arrive, send_coefs = send_first()

        for cols in lane_halves:
            now = contract(cols)
            total = integ[:, :, cols] + weight * now
            integ[:, :, cols] = total
            put_stack(cols, total if degree == ORDERS - 1 else now)

    def put_traces(q):
        traces = dot(ts[...], ds[q])
        own[q] = traces
        high, low = halves(traces)
        for f in range(4):
            rows, cols = slice(f * NJP, (f + 1) * NJP), slice(f * NT, (f + 1) * NT)
            ohl[q * NJP : (q + 1) * NJP, cols] = high[rows]
            ohl[(NQ + q) * NJP : (NQ + q + 1) * NJP, cols] = low[rows]

    for q in (6, 7, 8):
        put_traces(q)
    surf_names = nmat[1536:1664, :]
    at_faces = dot_nt(ohl[96:144, :], surf_names) + dot_nt(ohl[240:288, :], surf_names)
    speed = jnp.zeros((1, 128), F32)
    for c in range(3):
        speed = speed + normals[c] * at_faces[c * NJP + NJ : c * NJP + NJ + 1, :]
    own_speed = coupled * speed
    stile[...] = jnp.where(iota((8, 128), 0) == 0, own_speed, own_cells)

    speeds_arrive = surface(stile, lambda off: srecv.at[3 - off], 1, 3)

    send_coefs()
    for q in range(6):
        put_traces(q)

    local["lifting"].wait()
    for f in range(4):
        lsc[f * NJP : f * NJP + NJ, 0:NB] = lift_ref[:, f, :]
    flipped = jnp.transpose(ksc[...])[0:NBP]
    lanes = iota((NBP, 128), 1)
    turned = [jnp.where(lanes < NBP, flipped if d == 0 else pltpu.roll(flipped, 128 - d * NBP, 1), 0.0) for d in range(3)]
    turned.append(jnp.zeros((8, 128), F32))
    kv[...] = stacked_left(jnp.concatenate(turned, axis=0), 32).astype(BF16)
    lift = jnp.transpose(lsc[...])[0:32]
    lift_high = lift.astype(BF16).astype(F32)
    ls[:, 0:128] = (lift_high + pltpu.roll(lift_high, 64, 1)).astype(BF16)
    ls[:, 128:256] = (lift - lift_high).astype(BF16)
    shift = lax.rem(iota((256, 128), 0), 128) - iota((256, 128), 1)
    taps = jnp.zeros((256, 128), F32)
    for m, tap in enumerate(TAPS, 1):
        taps = jnp.where(shift == m, tap, jnp.where(shift == -m, -tap, taps))
    wy[...] = taps.astype(BF16)

    slot_row = iota((1, 128), 1) // CAP

    def combine(block, mine, buffer, row):
        total = jnp.zeros((1, 128), F32)
        for r in range(REACH):
            gap = block - (r - 2)
            if gap == 0:
                total = jnp.where(slot_row == r, mine, total)
            else:
                ok = (a + gap >= 0) & (a + gap < strips)
                total = jnp.where(slot_row == jnp.where(ok, r, -1), buffer[gap + 3, row : row + 1, :], total)
        return total

    pieces = (((8, 8), (8, 32), (4, 8), (0, 32)), ((4, 4), (16, 16), (0, 4), (8, 16)), ((16, 4), (16, 16), (12, 4), (8, 16)))
    middle = ((8, 8), (16, 16), (4, 8), (8, 16))

    def view(ref, f, box, dx=0, dz=0):
        (x, nx), (z, nz) = box[:2]
        return ref[f, x + dx : x + dx + nx, z + dz : z + dz + nz, :]

    def tap_sum(pick):
        total = None
        for m, tap in enumerate(TAPS, 1):
            term = tap * (pick(m) - pick(-m))
            total = term if total is None else total + term
        return total

    def along_x(ref, f, box):
        return tap_sum(lambda m: view(ref, f, box, dx=m))

    def along_z(ref, f, box):
        return tap_sum(lambda m: view(ref, f, box, dz=m))

    def along_y(ref, f, box):
        x = view(ref, f, box)
        shape = x.shape
        x = x.reshape(shape[0] * shape[1], 128)
        return dot(jnp.concatenate(halves(x), axis=1), wy[...]).reshape(shape)

    def coefs(f, box):
        (x, nx), (z, nz) = box[2:]
        return coef[f, x : x + nx, z : z + nz, :]

    def gradient(ref, f, box):
        return along_x(ref, f, box), along_z(ref, f, box), along_y(ref, f, box)

    def blown(slopes, box):
        return coefs(0, box) * slopes[0] + coefs(1, box) * slopes[1] + coefs(2, box) * slopes[2]

    def put(ref, box, value):
        (x, nx), (z, nz) = box[2:]
        ref[x : x + nx, z : z + nz, :] = value

    def get(ref, box):
        (x, nx), (z, nz) = box[2:]
        return ref[x : x + nx, z : z + nz, :]

    def squeeze(ref, box):
        return coefs(3, box) * (along_x(ref, 1, box) + along_z(ref, 2, box) + along_y(ref, 3, box))

    def names_block(i, carry):
        start = pl.multiple_of(64 * i, 64)
        for f, block in enumerate(names(start, 64)):
            nmat[pl.ds(start, 64), f * NT : (f + 1) * NT] = block
        return carry

    lax.fori_loop(0, 24, names_block, 0)
    given = dot_nt(ohl[...], nmat[1024:1664, :])
    given = given[0:144] + given[144:288]
    for d in range(4):
        for q in range(NQ):
            tout[d, q * NJ : (q + 1) * NJ, :] = given[q * NJP : q * NJP + NJ, d * RIM : (d + 1) * RIM]
    traces_arrive = exchange([(d, tout.at[d], trecv.at[mirror_of[d]]) for d in range(4)])
    own_at = given[:, 512:640]

    speeds_arrive()
    start_pressure[...] = e0[0, own_x, own_z, :].reshape(128, 128)
    for block in (-1, 0, 1):
        arrived = combine(block, own_speed, srecv, 0)
        cells = combine(block, own_cells, srecv, 1).astype(jnp.int32)
        cell_rows = lax.shift_right_logical(cells, 7)
        cell_lanes = lax.bitwise_and(cells, 127)
        at_row = jnp.where(iota((128, 128), 0) == cell_rows, arrived, 0.0)
        at_lane = jnp.where(iota((128, 128), 0) == cell_lanes, 1.0, 0.0).astype(BF16)
        if block == 0:
            own_rows = cell_rows
            bt[...] = at_lane
        gained[block + 1] = dot_nt(
            jnp.concatenate(halves(at_row), axis=1), jnp.concatenate([at_lane, at_lane], axis=1)
        ).reshape(8, 16, 128)
    e0[0, own_x, own_z, :] = e0[0, own_x, own_z, :] + gained[1]
    pressure_first()
    for block in (-1, 1):
        where = pl.ds(8 + 8 * block, 8)
        e0[0, where, own_z, :] = e0[0, where, own_z, :] + gained[block + 1]
    pressure_arrive = exchange(send_pressure_z(e0))

    picked = dot(jnp.concatenate(thirds(start_pressure[...]), axis=0), bt[...])
    picked = picked[0:128] + picked[128:256] + picked[256:384]
    looked = jnp.sum(jnp.where(iota((128, 128), 0) == own_rows, picked, 0.0), axis=0, keepdims=True)
    ptile[...] = jnp.broadcast_to(looked, (8, 128))
    replies_arrive = surface(ptile, lambda off: precv.at[off + 2], -1, 2)

    first_arrive()
    local["lift"].wait()
    for box in pieces:
        (x, nx), (z, nz) = box[2:]
        coef[:, x : x + nx, z : z + nz, :] = coef[:, x : x + nx, z : z + nz, :] * TAP_UNIT
    lift_of[...] = lift_of[...] * TAP_UNIT
    for box, d in zip(pieces, (None, LEFT, RIGHT)):
        value = squeeze(e0, box)
        put(base, box, value if d is None else value - added[0, d])

    def shadow_first():
        for f in range(4):
            cols = slice(f * NT, (f + 1) * NT)
            gathered = dot(ohl[...], nmat[0:SLOTS, cols])
            gathered = gathered[0:144] + gathered[144:288]
            for q in range(NQ):
                rows = slice(f * NJP, (f + 1) * NJP)
                diff[q, rows, :] = gathered[q * NJP : (q + 1) * NJP] - own[q, rows, :]

    def shadow_second():
        rotate(kv)

        for cols in lane_halves:
            vol[:, :, cols] = contract(cols)

    def shadow_third():
        replies_arrive()
        traces_arrive()
        replies = jnp.where(slot_row == 2, looked, 0.0)
        for r in (0, 1, 3, 4):
            ok = (a + r - 2 >= 0) & (a + r - 2 < strips)
            replies = jnp.where(slot_row == jnp.where(ok, r, -1), precv[r, 0:1, :], replies)
        replies = coupled * replies
        row_q = iota((NQ * NJP, 128), 0) // NJP
        mirrored = jnp.where(row_q < 3, -2.0 * replies - own_at, own_at)
        for half, values in enumerate(halves(mirrored)):
            rl[half * 144 : half * 144 + 144, 512:640] = values
        for d in range(4):
            for q in range(NQ):
                x = jnp.concatenate([trecv[d, q * NJ : (q + 1) * NJ, :], jnp.zeros((NJP - NJ, RIM), F32)], axis=0)
                for half, values in enumerate(halves(x)):
                    start = half * 144 + q * NJP
                    rl[start : start + NJP, d * RIM : (d + 1) * RIM] = values
        for f in range(4):
            cols = slice(f * NT, (f + 1) * NT)
            gathered = dot(rl[...], nmat[SLOTS:1664, cols])
            gathered = gathered[0:144] + gathered[144:288]
            for q in range(NQ):
                rows = slice(f * NJP, (f + 1) * NJP)
                diff[q, rows, :] = diff[q, rows, :] + gathered[q * NJP : (q + 1) * NJP]

    def shadow_fourth():
        local["flx"].wait()

        def step(i, carry):
            faces = []
            for f in range(4):
                total = None
                for q in range(NQ):
                    term = flx[pl.ds(3 * i, 3), q, f : f + 1, :] * diff[q, f * NJP : (f + 1) * NJP, :][None]
                    total = term if total is None else total + term
                faces.append(total)
            fluxed = jnp.concatenate(faces, axis=1)
            for k in range(3):
                high, low = halves(fluxed[k])
                lifted = dot(ls[:, 0:192], jnp.concatenate([high, low, high], axis=0))
                p = 3 * i + k
                sout[p] = sol[p] + (vol[p] + lifted[0:NBP])[0:NB]
            return carry

        lax.fori_loop(0, 3, step, 0)

    for f in range(3):
        adv[f] = view(e0, 1 + f, middle) - blown(gradient(e0, 1 + f, middle), middle)
    shadow_first()
    for substep in range(SUBSTEPS):
        here = ext[substep]
        final = substep == SUBSTEPS - 1
        pressure_arrive()
        if substep == 0:
            for box in pieces:
                put(pe, box, view(here, 0, box) - get(base, box) - blown(gradient(here, 0, box), box))
        else:
            for box in pieces:
                put(base, box, view(here, 0, box) - blown(gradient(here, 0, box), box))
            beyond_arrive()
            rest_arrive()
            for box, d in zip(pieces, (None, LEFT, RIGHT)):
                value = get(base, box) - squeeze(here, box)
                put(pe, box, value if d is None else value + added[substep, d])
            for f in range(3):
                adv[f] = view(here, 1 + f, middle) - blown(gradient(here, 1 + f, middle), middle)
        if not final:
            there = ext[substep + 1]
            there[0, 4:20, own_z, :] = pe[:, 8:24, :]
            pressure_arrive = send_pressure(there)
        def take(f, slope):
            value = adv[f] - lift_of[...] * slope
            if final:
                uout[1 + f] = value
            else:
                there[1 + f, own_x, own_z, :] = value

        take(0, tap_sum(lambda m: pe[4 + m : 12 + m, 8:24, :]))
        if not final:
            beyond_arrive = send_beyond(there, substep + 1)
        take(1, tap_sum(lambda m: pe[4:12, 8 + m : 24 + m, :]))
        x = pe[4:12, 8:24, :].reshape(128, 128)
        take(2, dot(jnp.concatenate(halves(x), axis=1), wy[...]).reshape(8, 16, 128))
        if final:
            uout[0] = pe[4:12, 8:24, :]
        else:
            rest_arrive = send_speeds(there, substep + 1)
            if substep == 0:
                shadow_second()
            else:
                shadow_third()
                shadow_fourth()
                settle()

    fetch("sol_out", sout, sol_out)
    fetch("air_out", uout, air_out)
    local["sol_out"].wait()
    local["air_out"].wait()
    settle()


def vmem(*shape, dtype=F32):
    return pltpu.VMEM(shape, dtype)


def solution(mesh):
    strips, bands = mesh.shape["gx"], mesh.shape["gz"]

    def shards(
        solid_state, jacobians, flux_solvers, stiffness, trace_matrix, lift_matrix,
        neighbours, send_faces, surface_map, surface_normals, air_state, wind_field, air_medium,
    ):
        def body(*refs):
            kernel(strips, bands, *refs)

        hbm = pl.BlockSpec(memory_space=pl.ANY)
        out = pl.pallas_call(
            body,
            out_shape=(
                jax.ShapeDtypeStruct(solid_state.shape, F32),
                jax.ShapeDtypeStruct(air_state.shape, F32),
            ),
            in_specs=[hbm] * 12,
            out_specs=(hbm, hbm),
            scratch_shapes=[
                vmem(3, NB, NB), vmem(NJ, 4, NB), vmem(NJ, 4, NB), vmem(4, NT, dtype=jnp.int32),
                vmem(REACH, 3, CAP, dtype=jnp.int32), vmem(REACH, 3, CAP),
                vmem(NQ, NB, NT), vmem(NQ, NQ, 3, NT), vmem(NQ, NQ, 4, NT),
                vmem(4, 24, 48, 128), vmem(4, 24, 48, 128), vmem(4, 24, 48, 128),
                vmem(4, 16, 32, 128), vmem(16, 32, 128), vmem(8, 16, 128),
                vmem(NQ, 128, NT, dtype=BF16), vmem(NQ, 80, NT), vmem(NQ, NBP, NT), vmem(NQ, 64, NT),
                vmem(288, SLOTS, dtype=BF16), vmem(1664, SLOTS, dtype=BF16), vmem(NQ, 64, NT),
                vmem(NQ, NBP, NT), vmem(NQ, NB, NT), vmem(4, 8, 16, 128),
                vmem(128, 128), vmem(128, 128), vmem(64, 128),
                vmem(80, 128, dtype=BF16), vmem(80, 128, dtype=BF16), vmem(64, 128, dtype=BF16),
                vmem(32, 256, dtype=BF16), vmem(256, 128, dtype=BF16),
                vmem(3, 8, 128), vmem(3, 8, 128),
                vmem(16, 32, 128), vmem(3, 8, 16, 128), vmem(128, 128), vmem(3, 8, 16, 128), vmem(128, 128, dtype=BF16),
                vmem(3, 4, 2, 2, 8, 128), vmem(3, 4, 2, 2, 8, 128),
                vmem(3, 2, 4, 16, 128), vmem(3, 2, 4, 16, 128),
                vmem(8, 128), vmem(8, 128),
                vmem(7, 8, 128), vmem(REACH, 8, 128),
                vmem(4, 96, RIM), vmem(4, 96, RIM), vmem(288, 640, dtype=BF16),
                pltpu.SemaphoreType.DMA((16,)),
                pltpu.SemaphoreType.DMA((96,)),
                pltpu.SemaphoreType.DMA((96,)),
            ],
            compiler_params=pltpu.CompilerParams(
                collective_id=0, has_side_effects=True, vmem_limit_bytes=56 * 1024 * 1024
            ),
            name="coupled_step",
        )(
            solid_state,
            jnp.transpose(jacobians, (1, 2, 0, 3)),
            jnp.transpose(flux_solvers, (1, 2, 0, 3)),
            stiffness,
            jnp.transpose(trace_matrix, (1, 0, 2)),
            jnp.transpose(lift_matrix, (2, 0, 1)),
            neighbours,
            jnp.transpose(surface_map, (1, 0, 2)),
            jnp.transpose(surface_normals, (1, 0, 2)),
            air_state, wind_field, air_medium,
        )
        def hand(x, y, xo, yo, xv, yv, sem):
            pairs = [(x, xv, xo)] + [(y.at[k], yv.at[k], yo.at[k]) for k in range(4)]
            reads = [pltpu.make_async_copy(p[0], p[1], sem.at[0, i]) for i, p in enumerate(pairs)]
            writes = [pltpu.make_async_copy(p[1], p[2], sem.at[1, i]) for i, p in enumerate(pairs)]
            for r in reads:
                r.start()
            for r, w in zip(reads, writes):
                r.wait()
                w.start()
            for w in writes:
                w.wait()

        return pl.pallas_call(
            hand,
            out_shape=(jax.ShapeDtypeStruct(solid_state.shape, F32), jax.ShapeDtypeStruct(air_state.shape, F32)),
            in_specs=[hbm, hbm],
            out_specs=(hbm, hbm),
            scratch_shapes=[vmem(*solid_state.shape), vmem(*air_state.shape), pltpu.SemaphoreType.DMA((2, 5))],
            compiler_params=pltpu.CompilerParams(vmem_limit_bytes=60 * 1024 * 1024),
            name="hand_over",
        )(*out)

    in_specs = (
        P(None, None, ("gx", "gz")),
        P(None, None, None, ("gx", "gz")),
        P(None, None, None, ("gx", "gz")),
        P(),
        P(),
        P(),
        P(None, ("gx", "gz")),
        P(None, ("gx", "gz")),
        P(None, None, ("gx", "gz")),
        P(None, None, ("gx", "gz")),
        P(None, "gx", "gz", None),
        P(None, "gx", "gz", None),
        P(None, "gx", "gz", None),
    )
    out_specs = (P(None, None, ("gx", "gz")), P(None, "gx", "gz", None))
    return jax.shard_map(shards, mesh=mesh, in_specs=in_specs, out_specs=out_specs, check_vma=False)
```

```python
import jax
import jax.numpy as jnp
from jax import lax
from jax.experimental import pallas as pl
from jax.experimental.pallas import tpu as pltpu
from jax.sharding import PartitionSpec as P

F32, BF16 = jnp.float32, jnp.bfloat16
MESH = pl.DeviceIdType.MESH

ORDERS = 4
TIME_STEP = 0.5
SUBSTEPS = 3
TAPS = (672.0, -168.0, 32.0, -3.0)
TAP_UNIT = 1.0 / 840.0

NQ, NB, NBP = 9, 20, 24
NJ, NJP = 10, 16
NT = 256
SLOTS = 4 * NT
RIM = 128
CAP, REACH = 8, 5
LEFT, RIGHT, BELOW, ABOVE = range(4)


def halves(x):
    high = x.astype(BF16)
    return high, (x - high.astype(F32)).astype(BF16)


def thirds(x):
    high = x.astype(BF16)
    rest = x - high.astype(F32)
    mid = rest.astype(BF16)
    return high, mid, (rest - mid.astype(F32)).astype(BF16)


def dot(a, b):
    return jnp.dot(a, b, preferred_element_type=F32)


def dot_nt(a, b):
    return lax.dot_general(a, b, (((1,), (1,)), ((), ())), preferred_element_type=F32)


def iota(shape, dim):
    return lax.broadcasted_iota(jnp.int32, shape, dim)


def stacked_left(padded, gap):
    high = padded.astype(BF16).astype(F32)
    low = padded - high
    return high + pltpu.roll(high, gap, 1) + pltpu.roll(low, 2 * gap, 1)


def lane_row(tile):
    total = tile[0:1]
    for r in range(1, REACH):
        total = total + pltpu.roll(tile, CAP * r, 1)[r : r + 1]
    return total


def kernel(strips, bands, *refs):
    (
        sol_h, jac_h, flx_h, stiff_h, trace_h, lift_h, nbr_h, surf_h, normal_h,
        air_h, wind_h, med_h,
        sol_out, air_out,
        stiff_ref, trace_ref, lift_ref, nbr_ref, surf_ref, normal_ref,
        sol, jac, flx, e0, e1, e2, coef, pe, lift_of,
        ds, rot, integ, own, ohl, nmat, diff, vol, sout, uout,
        ksc, lsc, tsc, kp, kv, ts, ls, wy, smt, nmt,
        base, adv, start_pressure, gained, bt, packed, corners, beyond, added,
        stile, ptile, srecv, precv, tout, trecv, rl,
        local_sem, send_sem, recv_sem,
    ) = refs
    ext = (e0, e1, e2)
    a = lax.axis_index("gx")
    b = lax.axis_index("gz")

    own_x, own_z = pl.ds(8, 8), pl.ds(16, 16)
    coef_x_own, coef_z_own = pl.ds(4, 8), pl.ds(8, 16)
    local = {}

    def fetch(name, src, dst):
        local[name] = pltpu.make_async_copy(src, dst, local_sem.at[len(local)])
        local[name].start()

    fetch("stiff", stiff_h, stiff_ref)
    fetch("sol", sol_h, sol)
    fetch("jac", jac_h, jac)
    fetch("trace", trace_h, trace_ref)
    fetch("nbr", nbr_h, nbr_ref)
    fetch("surf", surf_h, surf_ref)
    fetch("normal", normal_h, normal_ref)
    fetch("air", air_h, e0.at[:, own_x, own_z, :])
    fetch("wind", wind_h, coef.at[pl.ds(0, 3), coef_x_own, coef_z_own])
    fetch("bulk", med_h.at[0], coef.at[3, coef_x_own, coef_z_own])
    fetch("lift", med_h.at[1], lift_of)
    fetch("flx", flx_h, flx)
    fetch("lifting", lift_h, lift_ref)

    can = {LEFT: a > 0, RIGHT: a < strips - 1, BELOW: b > 0, ABOVE: b < bands - 1}
    peer = {
        LEFT: (jnp.maximum(a - 1, 0), b),
        RIGHT: (jnp.minimum(a + 1, strips - 1), b),
        BELOW: (a, jnp.maximum(b - 1, 0)),
        ABOVE: (a, jnp.minimum(b + 1, bands - 1)),
    }
    mirror_of = {LEFT: RIGHT, RIGHT: LEFT, BELOW: ABOVE, ABOVE: BELOW}
    sem_count = [0]
    pending = []

    def remote(src, dst, device, sem):
        return pltpu.make_async_remote_copy(
            src_ref=src, dst_ref=dst, send_sem=send_sem.at[sem], recv_sem=recv_sem.at[sem],
            device_id=device, device_id_type=MESH,
        )

    def exchange(parts):
        groups = {}
        for d, src, dst in parts:
            groups.setdefault(d, []).append(remote(src, dst, side(d)[1], sem_count[0]))
            sem_count[0] += 1
        for d, copies in groups.items():
            pl.when(side(d)[0])(every(copies, "start"))
            pending.append((side(d)[0], copies))

        def arrive():
            for d, copies in groups.items():
                pl.when(side(opposite(d))[0])(every(copies, "wait_recv"))

        return arrive

    def every(copies, name):
        def act():
            for copy in copies:
                getattr(copy, name)()

        return act

    def settle():
        for ok, copies in pending:
            pl.when(ok)(every(copies, "wait_send"))
        pending.clear()

    def opposite(d):
        return tuple(mirror_of[k] for k in d) if isinstance(d, tuple) else mirror_of[d]

    def side(d):
        if isinstance(d, tuple):
            return can[d[0]] & can[d[1]], (peer[d[0]][0], peer[d[1]][1])
        return can[d], peer[d]

    def surface(src, place, sign, reach):
        waits = []
        for off in (3, -3, 2, -2, 1, -1):
            if abs(off) > reach:
                continue
            to = a + sign * off
            source = a - sign * off
            to_ok = (to >= 0) & (to < strips)
            from_ok = (source >= 0) & (source < strips)
            copy = remote(src, place(off), (jnp.clip(to, 0, strips - 1), b), sem_count[0])
            sem_count[0] += 1
            pl.when(to_ok)(copy.start)
            pending.append((to_ok, [copy]))
            waits.append((from_ok, copy))

        def arrive():
            for from_ok, copy in waits:
                pl.when(from_ok)(copy.wait_recv)

        return arrive

    diagonals = ((LEFT, BELOW), (LEFT, ABOVE), (RIGHT, BELOW), (RIGHT, ABOVE))
    x_near = {LEFT: pl.ds(8, 4), RIGHT: pl.ds(12, 4)}
    near_land = {LEFT: pl.ds(16, 4), RIGHT: pl.ds(4, 4)}
    z_near = {BELOW: pl.ds(16, 8), ABOVE: pl.ds(24, 8)}
    z_land = {BELOW: pl.ds(32, 8), ABOVE: pl.ds(8, 8)}
    raw_x = {LEFT: pl.ds(0, 4), RIGHT: pl.ds(4, 4)}
    raw_z = {BELOW: pl.ds(0, 8), ABOVE: pl.ds(8, 8)}
    coef_x = {LEFT: pl.ds(12, 4), RIGHT: pl.ds(0, 4)}
    coef_z = {BELOW: pl.ds(24, 8), ABOVE: pl.ds(0, 8)}
    with_arms = pl.ds(4, 16)

    corner_x = {LEFT: (8, 16), RIGHT: (12, 4)}
    corner_z = {BELOW: (16, 32), ABOVE: (28, 12)}

    def send_corners(buffer, turn):
        parts = []
        for i, d in enumerate(diagonals):
            x, z = corner_x[d[0]][0], corner_z[d[1]][0]
            for plane in range(4):
                half = 4 * (plane % 2)
                packed[turn, i, :, plane // 2, half : half + 4, :] = buffer[1:3, x + plane, z : z + 4, :]
            parts.append((d, packed.at[turn, i], corners.at[turn, i]))
        arrive = exchange(parts)

        def unpack():
            arrive()
            for i, d in enumerate(diagonals):
                x, z = corner_x[d[0]][1], corner_z[d[1]][1]
                for plane in range(4):
                    half = 4 * (plane % 2)
                    buffer[1:3, x + plane, z : z + 4, :] = corners[turn, i, :, plane // 2, half : half + 4, :]

        return unpack

    def send_speeds(buffer, turn):
        some = pl.ds(1, 3)
        parts = [(d, buffer.at[some, x_near[d], own_z], buffer.at[some, near_land[d], own_z]) for d in (LEFT, RIGHT)]
        strips_arrive = exchange(parts)
        bands_arrive = exchange(
            [(d, buffer.at[some, own_x, z_near[d]], buffer.at[some, own_x, z_land[d]]) for d in (BELOW, ABOVE)]
        )
        unpack = send_corners(buffer, turn)

        def arrive():
            strips_arrive()
            unpack()

        return bands_arrive, arrive

    def send_beyond(buffer, turn, unit=1.0):
        for d in (LEFT, RIGHT):
            for plane in range(4):
                x = 8 + plane if d == LEFT else 12 + plane
                parts = []
                for f in (0, 1):
                    total = None
                    for m, tap in enumerate(TAPS, 1):
                        other = x + m if d == LEFT else x - m
                        if (d == LEFT) == (other >= 12):
                            term = tap * buffer[f, other, 16:32, :]
                            total = term if total is None else total + term
                    parts.append(total)
                value = unit * (coef[0, x - 4, 8:24, :] * parts[0] + coef[3, x - 4, 8:24, :] * parts[1])
                beyond[turn, d, plane] = -value if d == LEFT else value
        return exchange([(d, beyond.at[turn, d], added.at[turn, mirror_of[d]]) for d in (LEFT, RIGHT)])

    def send_pressure_z(buffer):
        return [(d, buffer.at[0, with_arms, z_near[d]], buffer.at[0, with_arms, z_land[d]]) for d in (BELOW, ABOVE)]

    def send_pressure(buffer):
        return exchange(send_pressure_z(buffer))

    def send_first():
        local["air"].wait()
        local["wind"].wait()
        local["bulk"].wait()
        first = exchange([(d, air_h.at[0, raw_x[d]], e0.at[0, near_land[d], own_z]) for d in (LEFT, RIGHT)])
        second = send_beyond(e0, 0, TAP_UNIT)
        fourth, fifth = send_speeds(e0, 0)
        parts = []
        for d in (LEFT, RIGHT):
            parts.append((d, wind_h.at[:, raw_x[d]], coef.at[pl.ds(0, 3), coef_x[d], coef_z_own]))
            parts.append((d, med_h.at[0, raw_x[d]], coef.at[3, coef_x[d], coef_z_own]))
        for d in (BELOW, ABOVE):
            parts.append((d, wind_h.at[:, :, raw_z[d]], coef.at[pl.ds(0, 3), coef_x_own, coef_z[d]]))
            parts.append((d, med_h.at[0, :, raw_z[d]], coef.at[3, coef_x_own, coef_z[d]]))
        third_parts = parts

        def arrive():
            second()
            fourth()
            fifth()
            third[0]()

        third = []
        return first, arrive, lambda: third.append(exchange(third_parts))

    for d, where, narrow in ((LEFT, pl.ds(0, 8), pl.ds(0, 4)), (RIGHT, pl.ds(16, 8), pl.ds(12, 4))):
        @pl.when(jnp.logical_not(can[d]))
        def _(where=where, narrow=narrow):
            for buffer in ext:
                buffer[:, where, 8:40, :] = jnp.zeros((4, 8, 32, 128), F32)
            coef[:, narrow, 8:24, :] = jnp.zeros((4, 4, 16, 128), F32)
    for d, where, narrow in ((BELOW, pl.ds(8, 8), pl.ds(0, 8)), (ABOVE, pl.ds(32, 8), pl.ds(24, 8))):
        @pl.when(jnp.logical_not(can[d]))
        def _(where=where, narrow=narrow):
            for buffer in ext:
                buffer[:, 4:20, where, :] = jnp.zeros((4, 16, 8, 128), F32)
            coef[:, 4:12, narrow, :] = jnp.zeros((4, 8, 8, 128), F32)
    srecv[...] = jnp.zeros_like(srecv)
    precv[...] = jnp.zeros_like(precv)
    trecv[...] = jnp.zeros_like(trecv)
    corners[...] = jnp.zeros_like(corners)
    added[...] = jnp.zeros_like(added)
    for buffer in ext:
        for x in (0, 20):
            buffer[0:2, x : x + 4, 16:32, :] = jnp.zeros((2, 4, 16, 128), F32)

    barrier = pltpu.get_barrier_semaphore()
    greet = [(off, 0) for off in (-3, -2, -1, 1, 2, 3)] + [(x, z) for x in (-1, 0, 1) for z in (-1, 1)]
    for x, z in greet:
        pl.semaphore_signal(
            barrier, inc=1, device_id=(lax.rem(a + x + strips, strips), lax.rem(b + z + bands, bands)),
            device_id_type=MESH,
        )

    lane_halves = (slice(0, 128), slice(128, 256))

    def put_stack(cols, x):
        high, low = halves(jnp.concatenate([x, jnp.zeros((NQ, 8, 128), F32)], axis=1))
        ds[:, 0:32, cols] = high
        ds[:, 32:64, cols] = low
        ds[:, 64:96, cols] = high

    def rotate(left):
        for q in range(NQ):
            rot[q] = dot(left[...], ds[q])

    def contract(cols):
        total = None
        for q in range(NQ):
            for d in range(3):
                term = jac[:, q, d : d + 1, cols] * rot[q, d * NBP : (d + 1) * NBP, cols][None]
                total = term if total is None else total + term
        return total

    ksc[...] = jnp.zeros_like(ksc)
    tsc[...] = jnp.zeros_like(tsc)
    lsc[...] = jnp.zeros_like(lsc)
    smt[...] = jnp.zeros_like(smt)
    nmt[...] = jnp.zeros_like(nmt)
    integ[...] = jnp.zeros_like(integ)
    ds[:, 96:128, :] = jnp.zeros((NQ, 32, NT), BF16)
    local["stiff"].wait()
    for d in range(3):
        ksc[d * NBP : d * NBP + NB, 0:NB] = stiff_ref[d]
    kp[...] = (-stacked_left(ksc[0:80], 32)).astype(BF16)
    local["trace"].wait()
    for f in range(4):
        rows = trace_ref[:, f, :]
        tsc[f * NJP : f * NJP + NJ, 0:NB] = rows
        tsc[f * NJP + NJ : f * NJP + NJ + 1, 0:NB] = jnp.sum(rows, axis=0, keepdims=True) * (1.0 / NJ)
    ts[...] = stacked_left(tsc[...], 32).astype(BF16)

    def names(start, count):
        these = iota((count, NT), 0) + start
        return [jnp.where(these == nbr_ref[f : f + 1, :], 1.0, 0.0).astype(BF16) for f in range(4)]

    local["nbr"].wait()
    for f, block in enumerate(names(1536, 128)):
        nmat[1536:1664, f * NT : (f + 1) * NT] = block
    local["surf"].wait()
    local["normal"].wait()
    for i in range(3):
        smt[i, 0:REACH, 0:CAP] = surf_ref[:, i, :].astype(F32)
        nmt[i, 0:REACH, 0:CAP] = normal_ref[:, i, :]
    own_cells = lane_row(smt[1])
    coupled = lane_row(smt[2])
    normals = [lane_row(nmt[c]) for c in range(3)]

    local["sol"].wait()
    for q in range(NQ):
        integ[q, 0:NB, :] = TIME_STEP * sol[q]
    for cols in lane_halves:
        put_stack(cols, integ[:, :, cols] * (1.0 / TIME_STEP))
    local["jac"].wait()
    weight = TIME_STEP
    for degree in range(1, ORDERS):
        weight = weight * TIME_STEP / (degree + 1)
        rotate(kp)
        if degree == 1:
            pl.semaphore_wait(barrier, len(greet))
            pressure_first, first_arrive, send_coefs = send_first()

        for cols in lane_halves:
            now = contract(cols)
            total = integ[:, :, cols] + weight * now
            integ[:, :, cols] = total
            put_stack(cols, total if degree == ORDERS - 1 else now)

    def put_traces(q):
        traces = dot(ts[...], ds[q])
        own[q] = traces
        high, low = halves(traces)
        for f in range(4):
            rows, cols = slice(f * NJP, (f + 1) * NJP), slice(f * NT, (f + 1) * NT)
            ohl[q * NJP : (q + 1) * NJP, cols] = high[rows]
            ohl[(NQ + q) * NJP : (NQ + q + 1) * NJP, cols] = low[rows]

    for q in (6, 7, 8):
        put_traces(q)
    surf_names = nmat[1536:1664, :]
    at_faces = dot_nt(ohl[96:144, :], surf_names) + dot_nt(ohl[240:288, :], surf_names)
    speed = jnp.zeros((1, 128), F32)
    for c in range(3):
        speed = speed + normals[c] * at_faces[c * NJP + NJ : c * NJP + NJ + 1, :]
    own_speed = coupled * speed
    stile[...] = jnp.where(iota((8, 128), 0) == 0, own_speed, own_cells)

    speeds_arrive = surface(stile, lambda off: srecv.at[3 - off], 1, 3)

    send_coefs()
    for q in range(6):
        put_traces(q)

    local["lifting"].wait()
    for f in range(4):
        lsc[f * NJP : f * NJP + NJ, 0:NB] = lift_ref[:, f, :]
    flipped = jnp.transpose(ksc[...])[0:NBP]
    lanes = iota((NBP, 128), 1)
    turned = [jnp.where(lanes < NBP, flipped if d == 0 else pltpu.roll(flipped, 128 - d * NBP, 1), 0.0) for d in range(3)]
    turned.append(jnp.zeros((8, 128), F32))
    kv[...] = stacked_left(jnp.concatenate(turned, axis=0), 32).astype(BF16)
    lift = jnp.transpose(lsc[...])[0:32]
    lift_high = lift.astype(BF16).astype(F32)
    ls[:, 0:128] = (lift_high + pltpu.roll(lift_high, 64, 1)).astype(BF16)
    ls[:, 128:256] = (lift - lift_high).astype(BF16)
    shift = lax.rem(iota((256, 128), 0), 128) - iota((256, 128), 1)
    taps = jnp.zeros((256, 128), F32)
    for m, tap in enumerate(TAPS, 1):
        taps = jnp.where(shift == m, tap, jnp.where(shift == -m, -tap, taps))
    wy[...] = taps.astype(BF16)

    slot_row = iota((1, 128), 1) // CAP

    def combine(block, mine, buffer, row):
        total = jnp.zeros((1, 128), F32)
        for r in range(REACH):
            gap = block - (r - 2)
            if gap == 0:
                total = jnp.where(slot_row == r, mine, total)
            else:
                ok = (a + gap >= 0) & (a + gap < strips)
                total = jnp.where(slot_row == jnp.where(ok, r, -1), buffer[gap + 3, row : row + 1, :], total)
        return total

    pieces = (((8, 8), (8, 32), (4, 8), (0, 32)), ((4, 4), (16, 16), (0, 4), (8, 16)), ((16, 4), (16, 16), (12, 4), (8, 16)))
    middle = ((8, 8), (16, 16), (4, 8), (8, 16))

    def view(ref, f, box, dx=0, dz=0):
        (x, nx), (z, nz) = box[:2]
        return ref[f, x + dx : x + dx + nx, z + dz : z + dz + nz, :]

    def tap_sum(pick):
        total = None
        for m, tap in enumerate(TAPS, 1):
            term = tap * (pick(m) - pick(-m))
            total = term if total is None else total + term
        return total

    def along_x(ref, f, box):
        return tap_sum(lambda m: view(ref, f, box, dx=m))

    def along_z(ref, f, box):
        return tap_sum(lambda m: view(ref, f, box, dz=m))

    def along_y(ref, f, box):
        x = view(ref, f, box)
        shape = x.shape
        x = x.reshape(shape[0] * shape[1], 128)
        return dot(jnp.concatenate(halves(x), axis=1), wy[...]).reshape(shape)

    def coefs(f, box):
        (x, nx), (z, nz) = box[2:]
        return coef[f, x : x + nx, z : z + nz, :]

    def gradient(ref, f, box):
        return along_x(ref, f, box), along_z(ref, f, box), along_y(ref, f, box)

    def blown(slopes, box):
        return coefs(0, box) * slopes[0] + coefs(1, box) * slopes[1] + coefs(2, box) * slopes[2]

    def put(ref, box, value):
        (x, nx), (z, nz) = box[2:]
        ref[x : x + nx, z : z + nz, :] = value

    def get(ref, box):
        (x, nx), (z, nz) = box[2:]
        return ref[x : x + nx, z : z + nz, :]

    def squeeze(ref, box):
        return coefs(3, box) * (along_x(ref, 1, box) + along_z(ref, 2, box) + along_y(ref, 3, box))

    def names_block(i, carry):
        start = pl.multiple_of(64 * i, 64)
        for f, block in enumerate(names(start, 64)):
            nmat[pl.ds(start, 64), f * NT : (f + 1) * NT] = block
        return carry

    lax.fori_loop(0, 24, names_block, 0)
    given = dot_nt(ohl[...], nmat[1024:1664, :])
    given = given[0:144] + given[144:288]
    for d in range(4):
        for q in range(NQ):
            tout[d, q * NJ : (q + 1) * NJ, :] = given[q * NJP : q * NJP + NJ, d * RIM : (d + 1) * RIM]
    traces_arrive = exchange([(d, tout.at[d], trecv.at[mirror_of[d]]) for d in range(4)])
    own_at = given[:, 512:640]

    speeds_arrive()
    start_pressure[...] = e0[0, own_x, own_z, :].reshape(128, 128)
    for block in (-1, 0, 1):
        arrived = combine(block, own_speed, srecv, 0)
        cells = combine(block, own_cells, srecv, 1).astype(jnp.int32)
        cell_rows = lax.shift_right_logical(cells, 7)
        cell_lanes = lax.bitwise_and(cells, 127)
        at_row = jnp.where(iota((128, 128), 0) == cell_rows, arrived, 0.0)
        at_lane = jnp.where(iota((128, 128), 0) == cell_lanes, 1.0, 0.0).astype(BF16)
        if block == 0:
            own_rows = cell_rows
            bt[...] = at_lane
        gained[block + 1] = dot_nt(
            jnp.concatenate(halves(at_row), axis=1), jnp.concatenate([at_lane, at_lane], axis=1)
        ).reshape(8, 16, 128)
    e0[0, own_x, own_z, :] = e0[0, own_x, own_z, :] + gained[1]
    pressure_first()
    for block in (-1, 1):
        where = pl.ds(8 + 8 * block, 8)
        e0[0, where, own_z, :] = e0[0, where, own_z, :] + gained[block + 1]
    pressure_arrive = exchange(send_pressure_z(e0))

    picked = dot(jnp.concatenate(thirds(start_pressure[...]), axis=0), bt[...])
    picked = picked[0:128] + picked[128:256] + picked[256:384]
    looked = jnp.sum(jnp.where(iota((128, 128), 0) == own_rows, picked, 0.0), axis=0, keepdims=True)
    ptile[...] = jnp.broadcast_to(looked, (8, 128))
    replies_arrive = surface(ptile, lambda off: precv.at[off + 2], -1, 2)

    first_arrive()
    local["lift"].wait()
    for box in pieces:
        (x, nx), (z, nz) = box[2:]
        coef[:, x : x + nx, z : z + nz, :] = coef[:, x : x + nx, z : z + nz, :] * TAP_UNIT
    lift_of[...] = lift_of[...] * TAP_UNIT
    for box, d in zip(pieces, (None, LEFT, RIGHT)):
        value = squeeze(e0, box)
        put(base, box, value if d is None else value - added[0, d])

    def shadow_first():
        for f in range(4):
            cols = slice(f * NT, (f + 1) * NT)
            gathered = dot(ohl[...], nmat[0:SLOTS, cols])
            gathered = gathered[0:144] + gathered[144:288]
            for q in range(NQ):
                rows = slice(f * NJP, (f + 1) * NJP)
                diff[q, rows, :] = gathered[q * NJP : (q + 1) * NJP] - own[q, rows, :]

    def shadow_second():
        rotate(kv)

        for cols in lane_halves:
            vol[:, :, cols] = contract(cols)

    def shadow_third():
        replies_arrive()
        traces_arrive()
        replies = jnp.where(slot_row == 2, looked, 0.0)
        for r in (0, 1, 3, 4):
            ok = (a + r - 2 >= 0) & (a + r - 2 < strips)
            replies = jnp.where(slot_row == jnp.where(ok, r, -1), precv[r, 0:1, :], replies)
        replies = coupled * replies
        row_q = iota((NQ * NJP, 128), 0) // NJP
        mirrored = jnp.where(row_q < 3, -2.0 * replies - own_at, own_at)
        for half, values in enumerate(halves(mirrored)):
            rl[half * 144 : half * 144 + 144, 512:640] = values
        for d in range(4):
            for q in range(NQ):
                x = jnp.concatenate([trecv[d, q * NJ : (q + 1) * NJ, :], jnp.zeros((NJP - NJ, RIM), F32)], axis=0)
                for half, values in enumerate(halves(x)):
                    start = half * 144 + q * NJP
                    rl[start : start + NJP, d * RIM : (d + 1) * RIM] = values
        for f in range(4):
            cols = slice(f * NT, (f + 1) * NT)
            gathered = dot(rl[...], nmat[SLOTS:1664, cols])
            gathered = gathered[0:144] + gathered[144:288]
            for q in range(NQ):
                rows = slice(f * NJP, (f + 1) * NJP)
                diff[q, rows, :] = diff[q, rows, :] + gathered[q * NJP : (q + 1) * NJP]

    def shadow_fourth():
        local["flx"].wait()

        def step(i, carry):
            faces = []
            for f in range(4):
                total = None
                for q in range(NQ):
                    term = flx[pl.ds(3 * i, 3), q, f : f + 1, :] * diff[q, f * NJP : (f + 1) * NJP, :][None]
                    total = term if total is None else total + term
                faces.append(total)
            fluxed = jnp.concatenate(faces, axis=1)
            for k in range(3):
                high, low = halves(fluxed[k])
                lifted = dot(ls[:, 0:192], jnp.concatenate([high, low, high], axis=0))
                p = 3 * i + k
                sout[p] = sol[p] + (vol[p] + lifted[0:NBP])[0:NB]
            return carry

        lax.fori_loop(0, 3, step, 0)

    for f in range(3):
        adv[f] = view(e0, 1 + f, middle) - blown(gradient(e0, 1 + f, middle), middle)
    shadow_first()
    for substep in range(SUBSTEPS):
        here = ext[substep]
        final = substep == SUBSTEPS - 1
        pressure_arrive()
        if substep == 0:
            for box in pieces:
                put(pe, box, view(here, 0, box) - get(base, box) - blown(gradient(here, 0, box), box))
        else:
            for box in pieces:
                put(base, box, view(here, 0, box) - blown(gradient(here, 0, box), box))
            bands_arrive()
            center, left, right = pieces
            put(base, center, get(base, center) - coefs(3, center) * (along_z(here, 2, center) + along_y(here, 3, center)))
            for f in range(3):
                adv[f] = view(here, 1 + f, middle) - (
                    coefs(1, middle) * along_z(here, 1 + f, middle) + coefs(2, middle) * along_y(here, 1 + f, middle)
                )
            beyond_arrive()
            strips_arrive()
            put(pe, center, get(base, center) - coefs(3, center) * along_x(here, 1, center))
            for box, d in ((left, LEFT), (right, RIGHT)):
                put(pe, box, get(base, box) - squeeze(here, box) + added[substep, d])
            for f in range(3):
                adv[f] = adv[f] - coefs(0, middle) * along_x(here, 1 + f, middle)
        if not final:
            there = ext[substep + 1]
            there[0, 4:20, own_z, :] = pe[:, 8:24, :]
            pressure_arrive = send_pressure(there)
        else:
            uout[0] = pe[4:12, 8:24, :]
            fetch("air_out0", uout.at[0], air_out.at[0])
        def take(f, slope):
            value = adv[f] - lift_of[...] * slope
            if final:
                uout[1 + f] = value
                fetch(f"air_out{1 + f}", uout.at[1 + f], air_out.at[1 + f])
            else:
                there[1 + f, own_x, own_z, :] = value

        take(0, tap_sum(lambda m: pe[4 + m : 12 + m, 8:24, :]))
        if not final:
            beyond_arrive = send_beyond(there, substep + 1)
        take(1, tap_sum(lambda m: pe[4:12, 8 + m : 24 + m, :]))
        x = pe[4:12, 8:24, :].reshape(128, 128)
        take(2, dot(jnp.concatenate(halves(x), axis=1), wy[...]).reshape(8, 16, 128))
        if not final:
            bands_arrive, strips_arrive = send_speeds(there, substep + 1)
            if substep == 0:
                shadow_second()
            else:
                shadow_third()
                shadow_fourth()
                fetch("sol_out", sout, sol_out)
                settle()

    local["sol_out"].wait()
    for f in range(4):
        local[f"air_out{f}"].wait()
    settle()


def vmem(*shape, dtype=F32):
    return pltpu.VMEM(shape, dtype)


def solution(mesh):
    strips, bands = mesh.shape["gx"], mesh.shape["gz"]

    def shards(
        solid_state, jacobians, flux_solvers, stiffness, trace_matrix, lift_matrix,
        neighbours, send_faces, surface_map, surface_normals, air_state, wind_field, air_medium,
    ):
        def body(*refs):
            kernel(strips, bands, *refs)

        hbm = pl.BlockSpec(memory_space=pl.ANY)
        out = pl.pallas_call(
            body,
            out_shape=(
                jax.ShapeDtypeStruct(solid_state.shape, F32),
                jax.ShapeDtypeStruct(air_state.shape, F32),
            ),
            in_specs=[hbm] * 12,
            out_specs=(hbm, hbm),
            scratch_shapes=[
                vmem(3, NB, NB), vmem(NJ, 4, NB), vmem(NJ, 4, NB), vmem(4, NT, dtype=jnp.int32),
                vmem(REACH, 3, CAP, dtype=jnp.int32), vmem(REACH, 3, CAP),
                vmem(NQ, NB, NT), vmem(NQ, NQ, 3, NT), vmem(NQ, NQ, 4, NT),
                vmem(4, 24, 48, 128), vmem(4, 24, 48, 128), vmem(4, 24, 48, 128),
                vmem(4, 16, 32, 128), vmem(16, 32, 128), vmem(8, 16, 128),
                vmem(NQ, 128, NT, dtype=BF16), vmem(NQ, 80, NT), vmem(NQ, NBP, NT), vmem(NQ, 64, NT),
                vmem(288, SLOTS, dtype=BF16), vmem(1664, SLOTS, dtype=BF16), vmem(NQ, 64, NT),
                vmem(NQ, NBP, NT), vmem(NQ, NB, NT), vmem(4, 8, 16, 128),
                vmem(128, 128), vmem(128, 128), vmem(64, 128),
                vmem(80, 128, dtype=BF16), vmem(80, 128, dtype=BF16), vmem(64, 128, dtype=BF16),
                vmem(32, 256, dtype=BF16), vmem(256, 128, dtype=BF16),
                vmem(3, 8, 128), vmem(3, 8, 128),
                vmem(16, 32, 128), vmem(3, 8, 16, 128), vmem(128, 128), vmem(3, 8, 16, 128), vmem(128, 128, dtype=BF16),
                vmem(3, 4, 2, 2, 8, 128), vmem(3, 4, 2, 2, 8, 128),
                vmem(3, 2, 4, 16, 128), vmem(3, 2, 4, 16, 128),
                vmem(8, 128), vmem(8, 128),
                vmem(7, 8, 128), vmem(REACH, 8, 128),
                vmem(4, 96, RIM), vmem(4, 96, RIM), vmem(288, 640, dtype=BF16),
                pltpu.SemaphoreType.DMA((20,)),
                pltpu.SemaphoreType.DMA((96,)),
                pltpu.SemaphoreType.DMA((96,)),
            ],
            compiler_params=pltpu.CompilerParams(
                collective_id=0, has_side_effects=True, vmem_limit_bytes=56 * 1024 * 1024
            ),
            name="coupled_step",
        )(
            solid_state,
            jnp.transpose(jacobians, (1, 2, 0, 3)),
            jnp.transpose(flux_solvers, (1, 2, 0, 3)),
            stiffness,
            jnp.transpose(trace_matrix, (1, 0, 2)),
            jnp.transpose(lift_matrix, (2, 0, 1)),
            neighbours,
            jnp.transpose(surface_map, (1, 0, 2)),
            jnp.transpose(surface_normals, (1, 0, 2)),
            air_state, wind_field, air_medium,
        )
        def hand(x, y, xo, yo, xv, yv, sem):
            thirds_of = [pl.ds(3 * k, 3) for k in range(3)]
            pairs = [(x.at[k], xv.at[k], xo.at[k]) for k in thirds_of] + [(y.at[k], yv.at[k], yo.at[k]) for k in range(4)]
            reads = [pltpu.make_async_copy(p[0], p[1], sem.at[0, i]) for i, p in enumerate(pairs)]
            writes = [pltpu.make_async_copy(p[1], p[2], sem.at[1, i]) for i, p in enumerate(pairs)]
            for r in reads:
                r.start()
            for r, w in zip(reads, writes):
                r.wait()
                w.start()
            for w in writes:
                w.wait()

        return pl.pallas_call(
            hand,
            out_shape=(jax.ShapeDtypeStruct(solid_state.shape, F32), jax.ShapeDtypeStruct(air_state.shape, F32)),
            in_specs=[hbm, hbm],
            out_specs=(hbm, hbm),
            scratch_shapes=[vmem(*solid_state.shape), vmem(*air_state.shape), pltpu.SemaphoreType.DMA((2, 7))],
            compiler_params=pltpu.CompilerParams(vmem_limit_bytes=60 * 1024 * 1024),
            name="hand_over",
        )(*out)

    in_specs = (
        P(None, None, ("gx", "gz")),
        P(None, None, None, ("gx", "gz")),
        P(None, None, None, ("gx", "gz")),
        P(),
        P(),
        P(),
        P(None, ("gx", "gz")),
        P(None, ("gx", "gz")),
        P(None, None, ("gx", "gz")),
        P(None, None, ("gx", "gz")),
        P(None, "gx", "gz", None),
        P(None, "gx", "gz", None),
        P(None, "gx", "gz", None),
    )
    out_specs = (P(None, None, ("gx", "gz")), P(None, "gx", "gz", None))
    return jax.shard_map(shards, mesh=mesh, in_specs=in_specs, out_specs=out_specs, check_vma=False)
```

```python
import jax
import jax.numpy as jnp
from jax import lax
from jax.experimental import pallas as pl
from jax.experimental.pallas import tpu as pltpu
from jax.sharding import PartitionSpec as P

F32, BF16 = jnp.float32, jnp.bfloat16
MESH = pl.DeviceIdType.MESH

ORDERS = 4
TIME_STEP = 0.5
SUBSTEPS = 3
TAPS = (672.0, -168.0, 32.0, -3.0)
TAP_UNIT = 1.0 / 840.0

NQ, NB, NBP = 9, 20, 24
NJ, NJP = 10, 16
NT = 256
SLOTS = 4 * NT
RIM = 128
CAP, REACH = 8, 5
LEFT, RIGHT, BELOW, ABOVE = range(4)


def halves(x):
    high = x.astype(BF16)
    return high, (x - high.astype(F32)).astype(BF16)


def thirds(x):
    high = x.astype(BF16)
    rest = x - high.astype(F32)
    mid = rest.astype(BF16)
    return high, mid, (rest - mid.astype(F32)).astype(BF16)


def dot(a, b):
    return jnp.dot(a, b, preferred_element_type=F32)


def dot_nt(a, b):
    return lax.dot_general(a, b, (((1,), (1,)), ((), ())), preferred_element_type=F32)


def iota(shape, dim):
    return lax.broadcasted_iota(jnp.int32, shape, dim)


def stacked_left(padded, gap):
    high = padded.astype(BF16).astype(F32)
    low = padded - high
    return high + pltpu.roll(high, gap, 1) + pltpu.roll(low, 2 * gap, 1)


def lane_row(tile):
    total = tile[0:1]
    for r in range(1, REACH):
        total = total + pltpu.roll(tile, CAP * r, 1)[r : r + 1]
    return total


def kernel(strips, bands, *refs):
    (
        sol_h, jac_h, flx_h, stiff_h, trace_h, lift_h, nbr_h, surf_h, normal_h,
        air_h, wind_h, med_h,
        sol_out, air_out,
        stiff_ref, trace_ref, lift_ref, nbr_ref, surf_ref, normal_ref,
        sol, jac, flx, e0, e1, e2, coef, pe, lift_of,
        ds, rot, integ, own, ohl, nmat, diff, vol, sout, uout,
        ksc, lsc, tsc, kp, kv, ts, ls, wy, smt, nmt,
        base, adv, start_pressure, gained, bt, packed, corners, beyond, added,
        stile, ptile, srecv, precv, tout, trecv, rl,
        local_sem, send_sem, recv_sem,
    ) = refs
    ext = (e0, e1, e2)
    a = lax.axis_index("gx")
    b = lax.axis_index("gz")

    own_x, own_z = pl.ds(8, 8), pl.ds(16, 16)
    coef_x_own, coef_z_own = pl.ds(4, 8), pl.ds(8, 16)
    local = {}

    def fetch(name, src, dst):
        local[name] = pltpu.make_async_copy(src, dst, local_sem.at[len(local)])
        local[name].start()

    fetch("stiff", stiff_h, stiff_ref)
    fetch("sol", sol_h, sol)
    fetch("jac", jac_h, jac)
    fetch("trace", trace_h, trace_ref)
    fetch("nbr", nbr_h, nbr_ref)
    fetch("surf", surf_h, surf_ref)
    fetch("normal", normal_h, normal_ref)
    fetch("air", air_h, e0.at[:, own_x, own_z, :])
    fetch("wind", wind_h, coef.at[pl.ds(0, 3), coef_x_own, coef_z_own])
    fetch("bulk", med_h.at[0], coef.at[3, coef_x_own, coef_z_own])
    fetch("lift", med_h.at[1], lift_of)
    fetch("flx", flx_h, flx)
    fetch("lifting", lift_h, lift_ref)

    can = {LEFT: a > 0, RIGHT: a < strips - 1, BELOW: b > 0, ABOVE: b < bands - 1}
    peer = {
        LEFT: (jnp.maximum(a - 1, 0), b),
        RIGHT: (jnp.minimum(a + 1, strips - 1), b),
        BELOW: (a, jnp.maximum(b - 1, 0)),
        ABOVE: (a, jnp.minimum(b + 1, bands - 1)),
    }
    mirror_of = {LEFT: RIGHT, RIGHT: LEFT, BELOW: ABOVE, ABOVE: BELOW}
    sem_count = [0]
    pending = []

    def remote(src, dst, device, sem):
        return pltpu.make_async_remote_copy(
            src_ref=src, dst_ref=dst, send_sem=send_sem.at[sem], recv_sem=recv_sem.at[sem],
            device_id=device, device_id_type=MESH,
        )

    def exchange(parts):
        groups = {}
        for d, src, dst in parts:
            groups.setdefault(d, []).append(remote(src, dst, side(d)[1], sem_count[0]))
            sem_count[0] += 1
        for d, copies in groups.items():
            pl.when(side(d)[0])(every(copies, "start"))
            pending.append((side(d)[0], copies))

        def arrive():
            for d, copies in groups.items():
                pl.when(side(opposite(d))[0])(every(copies, "wait_recv"))

        return arrive

    def every(copies, name):
        def act():
            for copy in copies:
                getattr(copy, name)()

        return act

    def settle():
        for ok, copies in pending:
            pl.when(ok)(every(copies, "wait_send"))
        pending.clear()

    def opposite(d):
        return tuple(mirror_of[k] for k in d) if isinstance(d, tuple) else mirror_of[d]

    def side(d):
        if isinstance(d, tuple):
            return can[d[0]] & can[d[1]], (peer[d[0]][0], peer[d[1]][1])
        return can[d], peer[d]

    def surface(src, place, sign, reach):
        waits = []
        for off in (3, -3, 2, -2, 1, -1):
            if abs(off) > reach:
                continue
            to = a + sign * off
            source = a - sign * off
            to_ok = (to >= 0) & (to < strips)
            from_ok = (source >= 0) & (source < strips)
            copy = remote(src, place(off), (jnp.clip(to, 0, strips - 1), b), sem_count[0])
            sem_count[0] += 1
            pl.when(to_ok)(copy.start)
            pending.append((to_ok, [copy]))
            waits.append((from_ok, copy))

        def arrive():
            for from_ok, copy in waits:
                pl.when(from_ok)(copy.wait_recv)

        return arrive

    diagonals = ((LEFT, BELOW), (LEFT, ABOVE), (RIGHT, BELOW), (RIGHT, ABOVE))
    x_near = {LEFT: pl.ds(8, 4), RIGHT: pl.ds(12, 4)}
    near_land = {LEFT: pl.ds(16, 4), RIGHT: pl.ds(4, 4)}
    z_near = {BELOW: pl.ds(16, 8), ABOVE: pl.ds(24, 8)}
    z_land = {BELOW: pl.ds(32, 8), ABOVE: pl.ds(8, 8)}
    raw_x = {LEFT: pl.ds(0, 4), RIGHT: pl.ds(4, 4)}
    raw_z = {BELOW: pl.ds(0, 8), ABOVE: pl.ds(8, 8)}
    coef_x = {LEFT: pl.ds(12, 4), RIGHT: pl.ds(0, 4)}
    coef_z = {BELOW: pl.ds(24, 8), ABOVE: pl.ds(0, 8)}
    with_arms = pl.ds(4, 16)

    corner_x = {LEFT: (8, 16), RIGHT: (12, 4)}
    corner_z = {BELOW: (16, 32), ABOVE: (28, 12)}

    def send_corners(buffer, turn):
        parts = []
        for i, d in enumerate(diagonals):
            x, z = corner_x[d[0]][0], corner_z[d[1]][0]
            for plane in range(4):
                half = 4 * (plane % 2)
                packed[turn, i, :, plane // 2, half : half + 4, :] = buffer[1:3, x + plane, z : z + 4, :]
            parts.append((d, packed.at[turn, i], corners.at[turn, i]))
        arrive = exchange(parts)

        def unpack():
            arrive()
            for i, d in enumerate(diagonals):
                x, z = corner_x[d[0]][1], corner_z[d[1]][1]
                for plane in range(4):
                    half = 4 * (plane % 2)
                    buffer[1:3, x + plane, z : z + 4, :] = corners[turn, i, :, plane // 2, half : half + 4, :]

        return unpack

    def send_speeds(buffer, turn):
        some = pl.ds(1, 3)
        parts = [(d, buffer.at[some, x_near[d], own_z], buffer.at[some, near_land[d], own_z]) for d in (LEFT, RIGHT)]
        strips_arrive = exchange(parts)
        bands_arrive = exchange(
            [(d, buffer.at[some, own_x, z_near[d]], buffer.at[some, own_x, z_land[d]]) for d in (BELOW, ABOVE)]
        )
        unpack = send_corners(buffer, turn)

        def arrive():
            strips_arrive()
            unpack()

        return bands_arrive, arrive

    def send_beyond(buffer, turn, unit=1.0):
        for d in (LEFT, RIGHT):
            for plane in range(4):
                x = 8 + plane if d == LEFT else 12 + plane
                parts = []
                for f in (0, 1):
                    total = None
                    for m, tap in enumerate(TAPS, 1):
                        other = x + m if d == LEFT else x - m
                        if (d == LEFT) == (other >= 12):
                            term = tap * buffer[f, other, 16:32, :]
                            total = term if total is None else total + term
                    parts.append(total)
                value = unit * (coef[0, x - 4, 8:24, :] * parts[0] + coef[3, x - 4, 8:24, :] * parts[1])
                beyond[turn, d, plane] = -value if d == LEFT else value
        return exchange([(d, beyond.at[turn, d], added.at[turn, mirror_of[d]]) for d in (LEFT, RIGHT)])

    def send_pressure_z(buffer):
        return [(d, buffer.at[0, with_arms, z_near[d]], buffer.at[0, with_arms, z_land[d]]) for d in (BELOW, ABOVE)]

    def send_pressure(buffer):
        return exchange(send_pressure_z(buffer))

    def send_first():
        local["air"].wait()
        local["wind"].wait()
        local["bulk"].wait()
        first = exchange([(d, air_h.at[0, raw_x[d]], e0.at[0, near_land[d], own_z]) for d in (LEFT, RIGHT)])
        second = send_beyond(e0, 0, TAP_UNIT)
        fourth, fifth = send_speeds(e0, 0)
        parts = []
        for d in (LEFT, RIGHT):
            parts.append((d, wind_h.at[:, raw_x[d]], coef.at[pl.ds(0, 3), coef_x[d], coef_z_own]))
            parts.append((d, med_h.at[0, raw_x[d]], coef.at[3, coef_x[d], coef_z_own]))
        for d in (BELOW, ABOVE):
            parts.append((d, wind_h.at[:, :, raw_z[d]], coef.at[pl.ds(0, 3), coef_x_own, coef_z[d]]))
            parts.append((d, med_h.at[0, :, raw_z[d]], coef.at[3, coef_x_own, coef_z[d]]))
        third_parts = parts

        def arrive():
            second()
            fourth()
            fifth()
            third[0]()

        third = []
        return first, arrive, lambda: third.append(exchange(third_parts))

    for d, where, narrow in ((LEFT, pl.ds(0, 8), pl.ds(0, 4)), (RIGHT, pl.ds(16, 8), pl.ds(12, 4))):
        @pl.when(jnp.logical_not(can[d]))
        def _(where=where, narrow=narrow):
            for buffer in ext:
                buffer[:, where, 8:40, :] = jnp.zeros((4, 8, 32, 128), F32)
            coef[:, narrow, 8:24, :] = jnp.zeros((4, 4, 16, 128), F32)
    for d, where, narrow in ((BELOW, pl.ds(8, 8), pl.ds(0, 8)), (ABOVE, pl.ds(32, 8), pl.ds(24, 8))):
        @pl.when(jnp.logical_not(can[d]))
        def _(where=where, narrow=narrow):
            for buffer in ext:
                buffer[:, 4:20, where, :] = jnp.zeros((4, 16, 8, 128), F32)
            coef[:, 4:12, narrow, :] = jnp.zeros((4, 8, 8, 128), F32)
    srecv[...] = jnp.zeros_like(srecv)
    precv[...] = jnp.zeros_like(precv)
    trecv[...] = jnp.zeros_like(trecv)
    corners[...] = jnp.zeros_like(corners)
    added[...] = jnp.zeros_like(added)
    for buffer in ext:
        for x in (0, 20):
            buffer[0:2, x : x + 4, 16:32, :] = jnp.zeros((2, 4, 16, 128), F32)

    barrier = pltpu.get_barrier_semaphore()
    greet = [(off, 0) for off in (-3, -2, -1, 1, 2, 3)] + [(x, z) for x in (-1, 0, 1) for z in (-1, 1)]
    for x, z in greet:
        pl.semaphore_signal(
            barrier, inc=1, device_id=(lax.rem(a + x + strips, strips), lax.rem(b + z + bands, bands)),
            device_id_type=MESH,
        )

    lane_halves = (slice(0, 128), slice(128, 256))

    def put_stack(cols, x):
        high, low = halves(jnp.concatenate([x, jnp.zeros((NQ, 8, 128), F32)], axis=1))
        ds[:, 0:32, cols] = high
        ds[:, 32:64, cols] = low
        ds[:, 64:96, cols] = high

    def rotate(left):
        for q in range(NQ):
            rot[q] = dot(left[...], ds[q])

    def contract(cols):
        total = None
        for q in range(NQ):
            for d in range(3):
                term = jac[:, q, d : d + 1, cols] * rot[q, d * NBP : (d + 1) * NBP, cols][None]
                total = term if total is None else total + term
        return total

    ksc[...] = jnp.zeros_like(ksc)
    tsc[...] = jnp.zeros_like(tsc)
    lsc[...] = jnp.zeros_like(lsc)
    smt[...] = jnp.zeros_like(smt)
    nmt[...] = jnp.zeros_like(nmt)
    integ[...] = jnp.zeros_like(integ)
    ds[:, 96:128, :] = jnp.zeros((NQ, 32, NT), BF16)
    local["stiff"].wait()
    for d in range(3):
        ksc[d * NBP : d * NBP + NB, 0:NB] = stiff_ref[d]
    kp[...] = (-stacked_left(ksc[0:80], 32)).astype(BF16)
    local["trace"].wait()
    for f in range(4):
        rows = trace_ref[:, f, :]
        tsc[f * NJP : f * NJP + NJ, 0:NB] = rows
        tsc[f * NJP + NJ : f * NJP + NJ + 1, 0:NB] = jnp.sum(rows, axis=0, keepdims=True) * (1.0 / NJ)
    ts[...] = stacked_left(tsc[...], 32).astype(BF16)

    def names(start, count):
        these = iota((count, NT), 0) + start
        return [jnp.where(these == nbr_ref[f : f + 1, :], 1.0, 0.0).astype(BF16) for f in range(4)]

    local["nbr"].wait()
    for f, block in enumerate(names(1536, 128)):
        nmat[1536:1664, f * NT : (f + 1) * NT] = block
    local["surf"].wait()
    local["normal"].wait()
    for i in range(3):
        smt[i, 0:REACH, 0:CAP] = surf_ref[:, i, :].astype(F32)
        nmt[i, 0:REACH, 0:CAP] = normal_ref[:, i, :]
    own_cells = lane_row(smt[1])
    coupled = lane_row(smt[2])
    normals = [lane_row(nmt[c]) for c in range(3)]

    local["sol"].wait()
    for q in range(NQ):
        integ[q, 0:NB, :] = TIME_STEP * sol[q]
    for cols in lane_halves:
        put_stack(cols, integ[:, :, cols] * (1.0 / TIME_STEP))
    local["jac"].wait()
    weight = TIME_STEP
    for degree in range(1, ORDERS):
        weight = weight * TIME_STEP / (degree + 1)
        if degree == 1:
            pl.semaphore_wait(barrier, len(greet))
            pressure_first, first_arrive, send_coefs = send_first()
        rotate(kp)

        for cols in lane_halves:
            now = contract(cols)
            total = integ[:, :, cols] + weight * now
            integ[:, :, cols] = total
            put_stack(cols, total if degree == ORDERS - 1 else now)

    def put_traces(q):
        traces = dot(ts[...], ds[q])
        own[q] = traces
        high, low = halves(traces)
        for f in range(4):
            rows, cols = slice(f * NJP, (f + 1) * NJP), slice(f * NT, (f + 1) * NT)
            ohl[q * NJP : (q + 1) * NJP, cols] = high[rows]
            ohl[(NQ + q) * NJP : (NQ + q + 1) * NJP, cols] = low[rows]

    for q in (6, 7, 8):
        put_traces(q)
    surf_names = nmat[1536:1664, :]
    at_faces = dot_nt(ohl[96:144, :], surf_names) + dot_nt(ohl[240:288, :], surf_names)
    speed = jnp.zeros((1, 128), F32)
    for c in range(3):
        speed = speed + normals[c] * at_faces[c * NJP + NJ : c * NJP + NJ + 1, :]
    own_speed = coupled * speed
    stile[...] = jnp.where(iota((8, 128), 0) == 0, own_speed, own_cells)

    speeds_arrive = surface(stile, lambda off: srecv.at[3 - off], 1, 3)

    send_coefs()
    for q in range(6):
        put_traces(q)

    local["lifting"].wait()
    for f in range(4):
        lsc[f * NJP : f * NJP + NJ, 0:NB] = lift_ref[:, f, :]
    flipped = jnp.transpose(ksc[...])[0:NBP]
    lanes = iota((NBP, 128), 1)
    turned = [jnp.where(lanes < NBP, flipped if d == 0 else pltpu.roll(flipped, 128 - d * NBP, 1), 0.0) for d in range(3)]
    turned.append(jnp.zeros((8, 128), F32))
    kv[...] = stacked_left(jnp.concatenate(turned, axis=0), 32).astype(BF16)
    lift = jnp.transpose(lsc[...])[0:32]
    lift_high = lift.astype(BF16).astype(F32)
    ls[:, 0:128] = (lift_high + pltpu.roll(lift_high, 64, 1)).astype(BF16)
    ls[:, 128:256] = (lift - lift_high).astype(BF16)
    shift = lax.rem(iota((256, 128), 0), 128) - iota((256, 128), 1)
    taps = jnp.zeros((256, 128), F32)
    for m, tap in enumerate(TAPS, 1):
        taps = jnp.where(shift == m, tap, jnp.where(shift == -m, -tap, taps))
    wy[...] = taps.astype(BF16)

    slot_row = iota((1, 128), 1) // CAP

    def combine(block, mine, buffer, row):
        total = jnp.zeros((1, 128), F32)
        for r in range(REACH):
            gap = block - (r - 2)
            if gap == 0:
                total = jnp.where(slot_row == r, mine, total)
            else:
                ok = (a + gap >= 0) & (a + gap < strips)
                total = jnp.where(slot_row == jnp.where(ok, r, -1), buffer[gap + 3, row : row + 1, :], total)
        return total

    pieces = (((8, 8), (8, 32), (4, 8), (0, 32)), ((4, 4), (16, 16), (0, 4), (8, 16)), ((16, 4), (16, 16), (12, 4), (8, 16)))
    middle = ((8, 8), (16, 16), (4, 8), (8, 16))

    def view(ref, f, box, dx=0, dz=0):
        (x, nx), (z, nz) = box[:2]
        return ref[f, x + dx : x + dx + nx, z + dz : z + dz + nz, :]

    def tap_sum(pick):
        total = None
        for m, tap in enumerate(TAPS, 1):
            term = tap * (pick(m) - pick(-m))
            total = term if total is None else total + term
        return total

    def along_x(ref, f, box):
        return tap_sum(lambda m: view(ref, f, box, dx=m))

    def along_z(ref, f, box):
        return tap_sum(lambda m: view(ref, f, box, dz=m))

    def along_y(ref, f, box):
        x = view(ref, f, box)
        shape = x.shape
        x = x.reshape(shape[0] * shape[1], 128)
        return dot(jnp.concatenate(halves(x), axis=1), wy[...]).reshape(shape)

    def coefs(f, box):
        (x, nx), (z, nz) = box[2:]
        return coef[f, x : x + nx, z : z + nz, :]

    def gradient(ref, f, box):
        return along_x(ref, f, box), along_z(ref, f, box), along_y(ref, f, box)

    def blown(slopes, box):
        return coefs(0, box) * slopes[0] + coefs(1, box) * slopes[1] + coefs(2, box) * slopes[2]

    def put(ref, box, value):
        (x, nx), (z, nz) = box[2:]
        ref[x : x + nx, z : z + nz, :] = value

    def get(ref, box):
        (x, nx), (z, nz) = box[2:]
        return ref[x : x + nx, z : z + nz, :]

    def squeeze(ref, box):
        return coefs(3, box) * (along_x(ref, 1, box) + along_z(ref, 2, box) + along_y(ref, 3, box))

    def names_block(i, carry):
        start = pl.multiple_of(64 * i, 64)
        for f, block in enumerate(names(start, 64)):
            nmat[pl.ds(start, 64), f * NT : (f + 1) * NT] = block
        return carry

    lax.fori_loop(0, 24, names_block, 0)
    given = dot_nt(ohl[...], nmat[1024:1664, :])
    given = given[0:144] + given[144:288]
    for d in range(4):
        for q in range(NQ):
            tout[d, q * NJ : (q + 1) * NJ, :] = given[q * NJP : q * NJP + NJ, d * RIM : (d + 1) * RIM]
    traces_arrive = exchange([(d, tout.at[d], trecv.at[mirror_of[d]]) for d in range(4)])
    own_at = given[:, 512:640]

    speeds_arrive()
    start_pressure[...] = e0[0, own_x, own_z, :].reshape(128, 128)
    for block in (-1, 0, 1):
        arrived = combine(block, own_speed, srecv, 0)
        cells = combine(block, own_cells, srecv, 1).astype(jnp.int32)
        cell_rows = lax.shift_right_logical(cells, 7)
        cell_lanes = lax.bitwise_and(cells, 127)
        at_row = jnp.where(iota((128, 128), 0) == cell_rows, arrived, 0.0)
        at_lane = jnp.where(iota((128, 128), 0) == cell_lanes, 1.0, 0.0).astype(BF16)
        if block == 0:
            own_rows = cell_rows
            bt[...] = at_lane
        gained[block + 1] = dot_nt(
            jnp.concatenate(halves(at_row), axis=1), jnp.concatenate([at_lane, at_lane], axis=1)
        ).reshape(8, 16, 128)
    e0[0, own_x, own_z, :] = e0[0, own_x, own_z, :] + gained[1]
    pressure_first()
    for block in (-1, 1):
        where = pl.ds(8 + 8 * block, 8)
        e0[0, where, own_z, :] = e0[0, where, own_z, :] + gained[block + 1]
    pressure_arrive = exchange(send_pressure_z(e0))

    picked = dot(jnp.concatenate(thirds(start_pressure[...]), axis=0), bt[...])
    picked = picked[0:128] + picked[128:256] + picked[256:384]
    looked = jnp.sum(jnp.where(iota((128, 128), 0) == own_rows, picked, 0.0), axis=0, keepdims=True)
    ptile[...] = jnp.broadcast_to(looked, (8, 128))
    replies_arrive = surface(ptile, lambda off: precv.at[off + 2], -1, 2)

    first_arrive()
    local["lift"].wait()
    for box in pieces:
        (x, nx), (z, nz) = box[2:]
        coef[:, x : x + nx, z : z + nz, :] = coef[:, x : x + nx, z : z + nz, :] * TAP_UNIT
    lift_of[...] = lift_of[...] * TAP_UNIT
    for box, d in zip(pieces, (None, LEFT, RIGHT)):
        value = squeeze(e0, box)
        put(base, box, value if d is None else value - added[0, d])

    def shadow_first():
        for f in range(4):
            cols = slice(f * NT, (f + 1) * NT)
            gathered = dot(ohl[...], nmat[0:SLOTS, cols])
            gathered = gathered[0:144] + gathered[144:288]
            for q in range(NQ):
                rows = slice(f * NJP, (f + 1) * NJP)
                diff[q, rows, :] = gathered[q * NJP : (q + 1) * NJP] - own[q, rows, :]

    def shadow_second():
        rotate(kv)

        for cols in lane_halves:
            vol[:, :, cols] = contract(cols)

    def shadow_third():
        replies_arrive()
        traces_arrive()
        replies = jnp.where(slot_row == 2, looked, 0.0)
        for r in (0, 1, 3, 4):
            ok = (a + r - 2 >= 0) & (a + r - 2 < strips)
            replies = jnp.where(slot_row == jnp.where(ok, r, -1), precv[r, 0:1, :], replies)
        replies = coupled * replies
        row_q = iota((NQ * NJP, 128), 0) // NJP
        mirrored = jnp.where(row_q < 3, -2.0 * replies - own_at, own_at)
        for half, values in enumerate(halves(mirrored)):
            rl[half * 144 : half * 144 + 144, 512:640] = values
        for d in range(4):
            for q in range(NQ):
                x = jnp.concatenate([trecv[d, q * NJ : (q + 1) * NJ, :], jnp.zeros((NJP - NJ, RIM), F32)], axis=0)
                for half, values in enumerate(halves(x)):
                    start = half * 144 + q * NJP
                    rl[start : start + NJP, d * RIM : (d + 1) * RIM] = values
        for f in range(4):
            cols = slice(f * NT, (f + 1) * NT)
            gathered = dot(rl[...], nmat[SLOTS:1664, cols])
            gathered = gathered[0:144] + gathered[144:288]
            for q in range(NQ):
                rows = slice(f * NJP, (f + 1) * NJP)
                diff[q, rows, :] = diff[q, rows, :] + gathered[q * NJP : (q + 1) * NJP]

    def shadow_fourth():
        local["flx"].wait()

        def step(i, carry):
            faces = []
            for f in range(4):
                total = None
                for q in range(NQ):
                    term = flx[pl.ds(3 * i, 3), q, f : f + 1, :] * diff[q, f * NJP : (f + 1) * NJP, :][None]
                    total = term if total is None else total + term
                faces.append(total)
            fluxed = jnp.concatenate(faces, axis=1)
            for k in range(3):
                high, low = halves(fluxed[k])
                lifted = dot(ls[:, 0:192], jnp.concatenate([high, low, high], axis=0))
                p = 3 * i + k
                sout[p] = sol[p] + (vol[p] + lifted[0:NBP])[0:NB]
            return carry

        lax.fori_loop(0, 3, step, 0)

    for f in range(3):
        adv[f] = view(e0, 1 + f, middle) - blown(gradient(e0, 1 + f, middle), middle)
    shadow_first()
    for substep in range(SUBSTEPS):
        here = ext[substep]
        final = substep == SUBSTEPS - 1
        pressure_arrive()
        if substep == 0:
            for box in pieces:
                put(pe, box, view(here, 0, box) - get(base, box) - blown(gradient(here, 0, box), box))
        else:
            for box in pieces:
                put(base, box, view(here, 0, box) - blown(gradient(here, 0, box), box))
            bands_arrive()
            center, left, right = pieces
            put(base, center, get(base, center) - coefs(3, center) * (along_z(here, 2, center) + along_y(here, 3, center)))
            for f in range(3):
                adv[f] = view(here, 1 + f, middle) - (
                    coefs(1, middle) * along_z(here, 1 + f, middle) + coefs(2, middle) * along_y(here, 1 + f, middle)
                )
            beyond_arrive()
            strips_arrive()
            put(pe, center, get(base, center) - coefs(3, center) * along_x(here, 1, center))
            for box, d in ((left, LEFT), (right, RIGHT)):
                put(pe, box, get(base, box) - squeeze(here, box) + added[substep, d])
            for f in range(3):
                adv[f] = adv[f] - coefs(0, middle) * along_x(here, 1 + f, middle)
        if not final:
            there = ext[substep + 1]
            there[0, 4:20, own_z, :] = pe[:, 8:24, :]
            pressure_arrive = send_pressure(there)
        else:
            uout[0] = pe[4:12, 8:24, :]
            fetch("air_out0", uout.at[0], air_out.at[0])
        def take(f, slope):
            value = adv[f] - lift_of[...] * slope
            if final:
                uout[1 + f] = value
                fetch(f"air_out{1 + f}", uout.at[1 + f], air_out.at[1 + f])
            else:
                there[1 + f, own_x, own_z, :] = value

        take(0, tap_sum(lambda m: pe[4 + m : 12 + m, 8:24, :]))
        if not final:
            beyond_arrive = send_beyond(there, substep + 1)
        take(1, tap_sum(lambda m: pe[4:12, 8 + m : 24 + m, :]))
        x = pe[4:12, 8:24, :].reshape(128, 128)
        take(2, dot(jnp.concatenate(halves(x), axis=1), wy[...]).reshape(8, 16, 128))
        if not final:
            bands_arrive, strips_arrive = send_speeds(there, substep + 1)
            if substep == 0:
                shadow_second()
            else:
                shadow_third()
                shadow_fourth()
                fetch("sol_out", sout, sol_out)
                settle()

    local["sol_out"].wait()
    for f in range(4):
        local[f"air_out{f}"].wait()
    settle()


def vmem(*shape, dtype=F32):
    return pltpu.VMEM(shape, dtype)


def solution(mesh):
    strips, bands = mesh.shape["gx"], mesh.shape["gz"]

    def shards(
        solid_state, jacobians, flux_solvers, stiffness, trace_matrix, lift_matrix,
        neighbours, send_faces, surface_map, surface_normals, air_state, wind_field, air_medium,
    ):
        def body(*refs):
            kernel(strips, bands, *refs)

        hbm = pl.BlockSpec(memory_space=pl.ANY)
        out = pl.pallas_call(
            body,
            out_shape=(
                jax.ShapeDtypeStruct(solid_state.shape, F32),
                jax.ShapeDtypeStruct(air_state.shape, F32),
            ),
            in_specs=[hbm] * 12,
            out_specs=(hbm, hbm),
            scratch_shapes=[
                vmem(3, NB, NB), vmem(NJ, 4, NB), vmem(NJ, 4, NB), vmem(4, NT, dtype=jnp.int32),
                vmem(REACH, 3, CAP, dtype=jnp.int32), vmem(REACH, 3, CAP),
                vmem(NQ, NB, NT), vmem(NQ, NQ, 3, NT), vmem(NQ, NQ, 4, NT),
                vmem(4, 24, 48, 128), vmem(4, 24, 48, 128), vmem(4, 24, 48, 128),
                vmem(4, 16, 32, 128), vmem(16, 32, 128), vmem(8, 16, 128),
                vmem(NQ, 128, NT, dtype=BF16), vmem(NQ, 80, NT), vmem(NQ, NBP, NT), vmem(NQ, 64, NT),
                vmem(288, SLOTS, dtype=BF16), vmem(1664, SLOTS, dtype=BF16), vmem(NQ, 64, NT),
                vmem(NQ, NBP, NT), vmem(NQ, NB, NT), vmem(4, 8, 16, 128),
                vmem(128, 128), vmem(128, 128), vmem(64, 128),
                vmem(80, 128, dtype=BF16), vmem(80, 128, dtype=BF16), vmem(64, 128, dtype=BF16),
                vmem(32, 256, dtype=BF16), vmem(256, 128, dtype=BF16),
                vmem(3, 8, 128), vmem(3, 8, 128),
                vmem(16, 32, 128), vmem(3, 8, 16, 128), vmem(128, 128), vmem(3, 8, 16, 128), vmem(128, 128, dtype=BF16),
                vmem(3, 4, 2, 2, 8, 128), vmem(3, 4, 2, 2, 8, 128),
                vmem(3, 2, 4, 16, 128), vmem(3, 2, 4, 16, 128),
                vmem(8, 128), vmem(8, 128),
                vmem(7, 8, 128), vmem(REACH, 8, 128),
                vmem(4, 96, RIM), vmem(4, 96, RIM), vmem(288, 640, dtype=BF16),
                pltpu.SemaphoreType.DMA((20,)),
                pltpu.SemaphoreType.DMA((96,)),
                pltpu.SemaphoreType.DMA((96,)),
            ],
            compiler_params=pltpu.CompilerParams(
                collective_id=0, has_side_effects=True, vmem_limit_bytes=56 * 1024 * 1024
            ),
            name="coupled_step",
        )(
            solid_state,
            jnp.transpose(jacobians, (1, 2, 0, 3)),
            jnp.transpose(flux_solvers, (1, 2, 0, 3)),
            stiffness,
            jnp.transpose(trace_matrix, (1, 0, 2)),
            jnp.transpose(lift_matrix, (2, 0, 1)),
            neighbours,
            jnp.transpose(surface_map, (1, 0, 2)),
            jnp.transpose(surface_normals, (1, 0, 2)),
            air_state, wind_field, air_medium,
        )
        def hand(x, y, xo, yo, xv, yv, sem):
            thirds_of = [pl.ds(3 * k, 3) for k in range(3)]
            pairs = [(x.at[k], xv.at[k], xo.at[k]) for k in thirds_of] + [(y.at[k], yv.at[k], yo.at[k]) for k in range(4)]
            reads = [pltpu.make_async_copy(p[0], p[1], sem.at[0, i]) for i, p in enumerate(pairs)]
            writes = [pltpu.make_async_copy(p[1], p[2], sem.at[1, i]) for i, p in enumerate(pairs)]
            for r in reads:
                r.start()
            for r, w in zip(reads, writes):
                r.wait()
                w.start()
            for w in writes:
                w.wait()

        return pl.pallas_call(
            hand,
            out_shape=(jax.ShapeDtypeStruct(solid_state.shape, F32), jax.ShapeDtypeStruct(air_state.shape, F32)),
            in_specs=[hbm, hbm],
            out_specs=(hbm, hbm),
            scratch_shapes=[vmem(*solid_state.shape), vmem(*air_state.shape), pltpu.SemaphoreType.DMA((2, 7))],
            compiler_params=pltpu.CompilerParams(vmem_limit_bytes=60 * 1024 * 1024),
            name="hand_over",
        )(*out)

    in_specs = (
        P(None, None, ("gx", "gz")),
        P(None, None, None, ("gx", "gz")),
        P(None, None, None, ("gx", "gz")),
        P(),
        P(),
        P(),
        P(None, ("gx", "gz")),
        P(None, ("gx", "gz")),
        P(None, None, ("gx", "gz")),
        P(None, None, ("gx", "gz")),
        P(None, "gx", "gz", None),
        P(None, "gx", "gz", None),
        P(None, "gx", "gz", None),
    )
    out_specs = (P(None, None, ("gx", "gz")), P(None, "gx", "gz", None))
    return jax.shard_map(shards, mesh=mesh, in_specs=in_specs, out_specs=out_specs, check_vma=False)
```
